32 devices in a mesh: row: 4 (over z), col: 8 (over y, x, core).
Axes of the slice: x: 2, y: 2, z: 4, core: 2. Of those that a mesh axis runs over, the one named last changes fastest.
Arguments:
- counts: int32 [8192, 16384], P('row', 'col'), may hold values from 0 to 512
- block_mask: int32 [32, 64], P('row', 'col'), may hold values from 0 to 1
- row_perm: int32 [8192], P('row'), may hold values from 0 to 8191, as said below
- col_perm: int32 [16384], P('col'), may hold values from 0 to 16383, as said below
- row_logm: float32 [8192], P('row'), may hold values from 0 to 3
- col_logm: float32 [16384], P('col'), may hold values from 0 to 3
- row_emb: bfloat16 [8192, 512], P(('row', 'col')), may hold values from -1.1953125 to 1.1953125
- col_emb: bfloat16 [16384, 512], P(('col', 'row')), may hold values from -1.1953125 to 1.1953125
Outputs:
- row_grad: float32 [8192, 512], P(('row', 'col'))
- col_grad: float32 [16384, 512], P(('col', 'row'))
The draws below stay inside these ranges and needn't reach their ends.
Inputs may be any that keep to these rules, and one draw needn't show every extreme that they name: `row_perm`: each aligned block of 2048 entries is a permutation of that block's own index range. `col_perm`: each aligned block of 2048 entries is a permutation of that block's own index range.
All inputs are finite; a program needn't handle non-finite values.
Results may differ from the reference program's by a relative error of at most 0.0022.
Values may be sent and summed in bfloat16 or wider, within the bound.
No kernel may reach another device: no remote copies, remote signals or barrier semaphores. Data moves between devices by JAX's collectives and lax.ppermute only.
A program may use at most 128 MiB of HBM per device.

```python
import jax
import jax.numpy as jnp
from jax import lax

D = 512
SR = 2048
SC = 2048
BLK = 256
ROWS = 8192
COLS = 16384
N_ROW = 4


def draw_counts(key, part):
    key = jax.random.fold_in(key, 11)
    first, second, third = jax.random.split(key, 3)
    present = jax.random.randint(first, (ROWS, COLS), 0, 2)
    expo = jax.random.randint(second, (ROWS, COLS), 0, 10)
    upper = jnp.left_shift(jnp.ones((ROWS, COLS), jnp.int32), expo) + 1
    value = jax.random.randint(third, (ROWS, COLS), 1, upper)
    return (present * value).astype(jnp.int32)


def draw_block_mask(key, part):
    key = jax.random.fold_in(key, 12)
    first, second = jax.random.split(key)
    groups_r = ROWS // SR
    groups_c = COLS // SC
    level = jax.random.randint(first, (groups_r, 1, groups_c, 1), 1, 5)
    pick = jax.random.randint(second, (groups_r, SR // BLK, groups_c, SC // BLK), 0, 4)
    return (pick < level).astype(jnp.int32).reshape(ROWS // BLK, COLS // BLK)


def block_perms(key, total, block):
    groups = total // block
    keys = jax.random.split(key, groups)
    perms = jax.vmap(lambda single: jax.random.permutation(single, block))(keys)
    perms = perms + (jnp.arange(groups, dtype=jnp.int32) * block)[:, None]
    return perms.reshape(total).astype(jnp.int32)


def draw_row_perm(key, part):
    key = jax.random.fold_in(key, 13)
    return block_perms(key, ROWS, SR)


def draw_col_perm(key, part):
    key = jax.random.fold_in(key, 14)
    return block_perms(key, COLS, SC)


def steps_of(key, extent, cuts, smallest, high):
    def one(axis_at, parts):
        draws = jax.random.uniform(jax.random.fold_in(jax.random.fold_in(key, 6), axis_at), (parts,), jnp.float32, smallest / len(cuts), high / len(cuts))
        return jnp.repeat(jnp.exp(draws), extent[axis_at] // parts).reshape((-1,) + (1,) * (len(extent) - axis_at - 1))

    factor_of = one(*cuts[0])
    for cut in cuts[1:]:
        factor_of = factor_of * one(*cut)
    return factor_of


def noise(key, shape, spread, reach, cuts=(), kind=jnp.bfloat16):
    values = spread * jax.random.normal(key, shape, jnp.float32)
    if cuts:
        values = values * steps_of(key, shape, cuts, -0.22, 0.18)
    return jnp.clip(values, -reach, reach).astype(kind)


def setup_inputs(seed: int = 0) -> dict:
    seeds = jax.random.split(jax.random.key(seed), 9)
    return {
        "counts": draw_counts(jax.random.fold_in(seeds[8], 71), 0),
        "block_mask": draw_block_mask(jax.random.fold_in(seeds[8], 71), 0),
        "row_perm": draw_row_perm(jax.random.fold_in(seeds[8], 71), 0),
        "col_perm": draw_col_perm(jax.random.fold_in(seeds[8], 71), 0),
        "row_logm": jnp.clip(3.0 * jax.random.uniform(seeds[4], (ROWS,), jnp.float32) ** steps_of(seeds[4], (ROWS,), ((0, 4),), -0.2, 0.2), 0.0, 3.0),
        "col_logm": jnp.clip(3.0 * jax.random.uniform(seeds[5], (COLS,), jnp.float32) ** steps_of(seeds[5], (COLS,), ((0, 8),), -0.2, 0.2), 0.0, 3.0),
        "row_emb": noise(seeds[6], (ROWS, D), 0.2, 1.1953125, ((0, 32),)),
        "col_emb": noise(seeds[7], (COLS, D), 0.2, 1.1953125, ((0, 32),)),
    }


def cell_delta(score, count, active, row_part, col_part):
    real_count = count.astype(jnp.float32)
    safe = jnp.maximum(real_count, 1.0)
    pmi = jnp.log(safe) - row_part[:, None] - col_part[None, :]
    confid = 0.1 + 0.25 * jnp.sqrt(safe)
    positive = confid * (score - pmi)
    zeroed = jax.nn.sigmoid(score - pmi)
    deriv = jnp.where(count > 0, positive, zeroed)
    return (active.astype(jnp.float32) * deriv).astype(jnp.bfloat16)

def reference(counts, block_mask, row_perm, col_perm, row_logm, col_logm, row_emb, col_emb):
    cvec = col_emb[col_perm]
    col_active = jnp.repeat(block_mask, BLK, axis=1)

    def group_step(accum, inputs):
        count_rows, mask_rows, perm_rows, logm_rows = inputs
        wvec = row_emb[perm_rows]
        score = lax.dot_general(wvec, cvec, (((1,), (1,)), ((), ())), preferred_element_type=jnp.float32)
        active = jnp.repeat(mask_rows, BLK, axis=0)
        delta = cell_delta(score, count_rows, active, logm_rows, col_logm)
        gshard = jnp.dot(delta, cvec, preferred_element_type=jnp.float32) / jnp.sqrt(jnp.float32(COLS))
        hpart = lax.dot_general(delta, wvec, (((0,), (0,)), ((), ())), preferred_element_type=jnp.float32)
        return (accum + hpart, gshard)
    inputs = (counts.reshape(N_ROW, SR, COLS), col_active.reshape(N_ROW, SR // BLK, COLS), row_perm.reshape(N_ROW, SR), row_logm.reshape(N_ROW, SR))
    start = jnp.zeros((COLS, D), jnp.float32)
    hsum, gparts = lax.scan(group_step, start, inputs)
    gshard = gparts.reshape(ROWS, D)
    hshard = hsum / jnp.sqrt(jnp.float32(ROWS))
    row_grad = jnp.zeros((ROWS, D), jnp.float32).at[row_perm].set(gshard)
    col_grad = jnp.zeros((COLS, D), jnp.float32).at[col_perm].set(hshard)
    return (row_grad, col_grad)
```

```python
import functools

import jax
import jax.numpy as jnp
import numpy as np
from jax import lax
from jax.experimental import pallas as pl
from jax.experimental.pallas import tpu as pltpu
from jax.sharding import PartitionSpec as P

F32 = jnp.float32
BF16 = jnp.bfloat16
LANES = 128
MIB = 1 << 20


def cell_delta(score, count, active, row_part, col_part):
    real_count = count.astype(F32)
    safe = jnp.maximum(real_count, 1.0)
    pmi = jnp.log(safe) - row_part[:, None] - col_part[None, :]
    confid = 0.1 + 0.25 * jnp.sqrt(safe)
    positive = confid * (score - pmi)
    zeroed = jax.nn.sigmoid(score - pmi)
    deriv = jnp.where(count > 0, positive, zeroed)
    return (active.astype(F32) * deriv).astype(BF16)


def plain_shards(counts, block_mask, row_perm, col_perm, row_logm, col_logm, row_emb, col_emb):
    shard_rows, shard_cols = counts.shape
    all_cols = shard_cols * lax.axis_size("col")
    all_rows = shard_rows * lax.axis_size("row")
    block_side = shard_rows // block_mask.shape[0]
    row_group = lax.all_gather(row_emb, "col", axis=0, tiled=True)
    col_group = lax.all_gather(col_emb, "row", axis=0, tiled=True)
    row_local = row_perm - lax.axis_index("row") * shard_rows
    col_local = col_perm - lax.axis_index("col") * shard_cols
    wvec = jnp.take(row_group, row_local, axis=0)
    cvec = jnp.take(col_group, col_local, axis=0)
    score = lax.dot_general(wvec, cvec, (((1,), (1,)), ((), ())), preferred_element_type=F32)
    active = jnp.repeat(jnp.repeat(block_mask, block_side, axis=0), block_side, axis=1)
    delta = cell_delta(score, counts, active, row_logm, col_logm)
    gshard = jnp.dot(delta, cvec, preferred_element_type=F32) / jnp.sqrt(F32(all_cols))
    ordered = jnp.zeros(gshard.shape, F32).at[row_local].set(gshard)
    row_grad = lax.psum_scatter(ordered, "col", scatter_dimension=0, tiled=True)
    hshard = lax.dot_general(
        delta, wvec, (((0,), (0,)), ((), ())), preferred_element_type=F32
    ) / jnp.sqrt(F32(all_rows))
    col_ordered = jnp.zeros(hshard.shape, F32).at[col_local].set(hshard)
    col_grad = lax.psum_scatter(col_ordered, "row", scatter_dimension=0, tiled=True)
    return (row_grad, col_grad)


def params(mib):
    return pltpu.CompilerParams(vmem_limit_bytes=mib * MIB)


def cost(flops, moved, trans=0):
    return pl.CostEstimate(flops=flops, bytes_accessed=moved, transcendentals=trans)


def onehot(flag):
    return jnp.where(flag, 1.0, 0.0).astype(BF16)


def pieces_of(value):
    high = value.astype(BF16)
    rest = value - high.astype(F32)
    middle = rest.astype(BF16)
    low = (rest - middle.astype(F32)).astype(BF16)
    return high, middle, low


def order_kernel(width, parts, base_ref, index_ref, aux_ref, count_ref, out_ref, aux_out_ref, pick):
    @pl.when(pl.program_id(0) == 0)
    def _():
        index = index_ref[...].T
        depth = pick.shape[0]
        lane = lax.broadcasted_iota(jnp.int32, (LANES, width), 1)
        for part in range(parts):
            vocab = (lane + base_ref[part] * width).astype(F32)
            for group in range(depth // LANES):
                pick[pl.ds(group * LANES, LANES), pl.ds(part * width, width)] = onehot(
                    index[:, group : group + 1] == vocab
                )
        aux = jnp.concatenate(pieces_of(aux_ref[...]), axis=0)
        moved = jnp.dot(aux, pick[...], preferred_element_type=F32)
        rows = aux_ref.shape[0]
        aux_out_ref[...] = moved[:rows] + moved[rows : 2 * rows] + moved[2 * rows :]

    shifted = (count_ref[...].astype(F32) - 256.0).astype(BF16)
    out_ref[...] = jnp.dot(shifted, pick[...], preferred_element_type=F32).astype(BF16)


def order_counts(counts, index, aux, bases, width):
    rows, cols = counts.shape
    parts = bases.shape[0]
    step = 512
    grid_spec = pltpu.PrefetchScalarGridSpec(
        num_scalar_prefetch=1,
        grid=(rows // step,),
        in_specs=[
            pl.BlockSpec((LANES, LANES), lambda i, s: (0, 0)),
            pl.BlockSpec(aux.shape, lambda i, s: (0, 0)),
            pl.BlockSpec((step, cols), lambda i, s: (i, 0)),
        ],
        out_specs=[
            pl.BlockSpec((step, parts * width), lambda i, s: (i, 0)),
            pl.BlockSpec((aux.shape[0], parts * width), lambda i, s: (0, 0)),
        ],
        scratch_shapes=[pltpu.VMEM((cols, parts * width), BF16)],
    )
    return pl.pallas_call(
        functools.partial(order_kernel, width, parts),
        grid_spec=grid_spec,
        out_shape=[
            jax.ShapeDtypeStruct((rows, parts * width), BF16),
            jax.ShapeDtypeStruct((aux.shape[0], parts * width), F32),
        ],
        compiler_params=params(48),
        cost_estimate=cost(2 * rows * cols * parts * width, 4 * rows * cols),
        name="order_counts",
    )(bases, index, aux, counts)


def rows_kernel(index_ref, *refs):
    blocks, (out_ref, logm_ref, group, pick) = refs[:-4], refs[-4:]
    side = blocks[0].shape[0]
    for at, block in enumerate(blocks):
        group[pl.ds(at * side, side), :] = block[...]
    index = index_ref[...].T
    rows = out_ref.shape[0]
    depth = group.shape[0]
    step = pick.shape[0]
    vocab = lax.broadcasted_iota(jnp.int32, (LANES, depth), 1).astype(F32)
    for first in range(0, rows, step):
        for inner in range(0, step, LANES):
            at = (first + inner) // LANES
            column = rows // LANES + at
            pick[pl.ds(inner, LANES), :] = onehot(index[:, column : column + 1] == vocab)
            column = 2 * (rows // LANES) + at
            logm_ref[pl.ds(first + inner, LANES), :] = jnp.broadcast_to(
                index[:, column : column + 1], (LANES, LANES)
            )
        out_ref[pl.ds(first, step), :] = jnp.dot(
            pick[...], group[...], preferred_element_type=F32
        ).astype(BF16)


def take_rows(index, blocks, rows):
    side, width = blocks[0].shape
    depth = side * len(blocks)
    return pl.pallas_call(
        rows_kernel,
        out_shape=[
            jax.ShapeDtypeStruct((rows, width), BF16),
            jax.ShapeDtypeStruct((rows, LANES), F32),
        ],
        scratch_shapes=[pltpu.VMEM((depth, width), BF16), pltpu.VMEM((512, depth), BF16)],
        compiler_params=params(32),
        cost_estimate=cost(2 * rows * depth * width, 4 * rows * width),
        name="take_rows",
    )(index, *blocks)


def cells_kernel(has_sum, pick_ref, first_ref, second_ref, wvec_ref, count_ref, aux_ref, logm_ref, *refs):
    if has_sum:
        before_ref, refs = refs[0], refs[1:]
    grad_ref, term_ref, sent_ref, chunk = refs
    step_at = pl.program_id(0)

    @pl.when(step_at == 0)
    def _():
        @pl.when(pick_ref[0] == 1)
        def _():
            chunk[...] = first_ref[...]

        @pl.when(pick_ref[0] == 0)
        def _():
            chunk[...] = second_ref[...]

    cvec = chunk[...]
    width = cvec.shape[0]
    side = 256
    halves = wvec_ref.shape[0] // side
    col_logm = aux_ref[8:9, :]
    total = None
    for half in range(halves):
        here = pl.ds(half * side, side)
        wvec = wvec_ref[here, :]
        score = lax.dot_general(wvec, cvec, (((1,), (1,)), ((), ())), preferred_element_type=F32)
        count = count_ref[here, :].astype(F32) + 256.0
        safe = jnp.maximum(count, 1.0)
        row_logm = jnp.concatenate([logm_ref[here, :]] * (width // LANES), axis=1)
        gap = score + ((row_logm + col_logm) - jnp.log(safe))
        confid = 0.1 + 0.25 * (safe * lax.rsqrt(safe))
        zeroed = 0.5 * jnp.tanh(0.5 * gap) + 0.5
        deriv = jnp.where(count > 0.0, confid * gap, zeroed)
        active = aux_ref[pl.ds(step_at * halves + half, 1), :]
        delta = (deriv * active).astype(BF16)
        grad = jnp.dot(delta, cvec, preferred_element_type=F32)
        if has_sum:
            grad = grad + before_ref[here, :]
        grad_ref[here, :] = grad
        term = lax.dot_general(delta, wvec, (((0,), (0,)), ((), ())), preferred_element_type=F32)
        total = term if total is None else total + term

    @pl.when(step_at == 0)
    def _():
        term_ref[...] = total

    @pl.when(step_at > 0)
    def _():
        term_ref[...] += total

    @pl.when(step_at == pl.num_programs(0) - 1)
    def _():
        sent_ref[...] = term_ref[...].astype(BF16)


def cells(pick, first, second, wvec, ordered, aux, at, logm, before):
    rows, depth = wvec.shape
    width = first.shape[0]
    step = 512
    whole = lambda i, s: (0, 0)
    block = lambda i, s: (i, 0)
    in_specs = [
        pl.BlockSpec((width, depth), whole),
        pl.BlockSpec((width, depth), whole),
        pl.BlockSpec((step, depth), block),
        pl.BlockSpec((step, width), lambda i, s: (i, at)),
        pl.BlockSpec((aux.shape[0], width), lambda i, s: (0, at)),
        pl.BlockSpec((step, LANES), block),
    ]
    args = [pick, first, second, wvec, ordered, aux, logm]
    aliases = {}
    if before is not None:
        in_specs.append(pl.BlockSpec((step, depth), block))
        aliases = {len(args): 0}
        args.append(before)
    grid_spec = pltpu.PrefetchScalarGridSpec(
        num_scalar_prefetch=1,
        grid=(rows // step,),
        in_specs=in_specs,
        out_specs=[
            pl.BlockSpec((step, depth), block),
            pl.BlockSpec((width, depth), whole),
            pl.BlockSpec((width, depth), whole),
        ],
        scratch_shapes=[pltpu.VMEM((width, depth), BF16)],
    )
    return pl.pallas_call(
        functools.partial(cells_kernel, before is not None),
        grid_spec=grid_spec,
        out_shape=[
            jax.ShapeDtypeStruct((rows, depth), F32),
            jax.ShapeDtypeStruct((width, depth), F32),
            jax.ShapeDtypeStruct((width, depth), BF16),
        ],
        input_output_aliases=aliases,
        compiler_params=params(32),
        cost_estimate=cost(6 * rows * width * depth, 12 * MIB, 3 * rows * width),
        name="cells",
    )(*args)


def put_kernel(first, index_ref, grad_ref, out_ref):
    grad = grad_ref[...]
    high = grad.astype(BF16)
    low = (grad - high.astype(F32)).astype(BF16)
    both = jnp.concatenate([high, low], axis=1)
    width = grad.shape[1]
    blocks, side = out_ref.shape[0], out_ref.shape[1]
    vocab = lax.broadcasted_iota(jnp.int32, (side, grad.shape[0]), 0)
    for at in range(blocks):
        pick = onehot(index_ref[...] == (vocab + (first + at) * side).astype(F32))
        moved = jnp.dot(pick, both, preferred_element_type=F32)
        out_ref[at] = moved[:, :width] + moved[:, width:]


def put_rows(index, grad, first, blocks, side):
    rows, width = grad.shape
    return pl.pallas_call(
        functools.partial(put_kernel, first),
        out_shape=jax.ShapeDtypeStruct((blocks, side, width), F32),
        compiler_params=params(32),
        cost_estimate=cost(4 * rows * blocks * side * width, 6 * rows * width),
        name="put_rows",
    )(index, grad)


def swap(value, axis, pairs):
    return lax.ppermute(value, axis, pairs)


def line_shards(counts, block_mask, row_perm, col_perm, row_logm, col_logm, row_emb, col_emb):
    shard_rows, shard_cols = counts.shape
    row_at = lax.axis_index("row")
    col_at = lax.axis_index("col")
    side = row_emb.shape[0]
    width = col_emb.shape[0]
    block_side = shard_rows // block_mask.shape[0]

    outward = [(1, 0), (2, 3)]
    inward = [(0, 1), (3, 2)]
    across = [(1, 2), (2, 1)]
    flip = lambda bit: [(i, i ^ bit) for i in range(8)]

    near = swap(col_emb, "row", outward + inward)
    over = swap(col_emb, "row", across)
    row_x = swap(row_emb, "col", flip(2))
    row_y = swap(row_emb, "col", flip(4))
    row_xy = swap(row_emb, "col", flip(6))
    mine = [row_emb, row_x, row_y, row_xy]
    other = [swap(block, "col", flip(1)) for block in mine]
    two_out = swap(over, "row", outward)
    far_over = swap(near, "row", across)
    three_out = swap(far_over, "row", outward)

    row_local = row_perm - row_at * shard_rows
    col_local = col_perm - col_at * shard_cols
    gap = (row_local // side) ^ col_at
    row_slot = ((gap >> 1) + 4 * (gap & 1)) * side + row_local % side
    row_index = row_slot.astype(F32)
    index = jnp.concatenate(
        [col_local.astype(F32), row_index, row_logm, jnp.zeros((LANES * LANES - 3 * shard_rows,), F32)]
    ).reshape(LANES, LANES)
    active = jnp.repeat(block_mask.astype(F32), block_side, axis=1)
    aux = jnp.concatenate([active, col_logm[None, :], jnp.zeros((7, shard_cols), F32)], axis=0)

    end = (row_at == 0) | (row_at == 3)
    real = lambda m: jnp.where(row_at >= 2, 3 - m, m)
    order = [real(jnp.where(end, e, m)) for e, m in ((1, 2), (2, 0), (3, 3), (0, 1))]
    order = [o.astype(jnp.int32) for o in order]
    at_end = end.astype(jnp.int32).reshape(1)

    early, aux_early = order_counts(counts, index, aux, jnp.stack(order[:2]), width)
    late, aux_late = order_counts(counts, index, aux, jnp.stack(order[2:]), width)
    wvec, logm = take_rows(index, mine + other, shard_rows)

    work = functools.partial(cells, at_end)
    grad, term_a, sent_a = work(near, over, wvec, early, aux_early, 0, logm, None)
    got_1 = swap(sent_a, "row", inward)
    grad, term_b, sent_b = work(two_out, near, wvec, early, aux_early, 1, logm, grad)
    got_2 = swap(sent_b, "row", inward)
    grad, term_c, sent_c = work(three_out, far_over, wvec, late, aux_late, 0, logm, grad)
    got_3 = swap(sent_c, "row", inward)
    grad, term_d, _ = work(col_emb, col_emb, wvec, late, aux_late, 1, logm, grad)

    sum_2 = (term_a + got_2.astype(F32)).astype(BF16)
    got_4 = swap(sum_2, "row", across)
    sum_3 = (term_c + got_3.astype(F32)).astype(BF16)
    got_5 = swap(sum_3, "row", across)
    sum_0 = (term_b + got_5.astype(F32)).astype(BF16)
    got_6 = swap(sum_0, "row", outward)
    col_sum = term_d + got_1.astype(F32) + got_4.astype(F32) + got_6.astype(F32)
    col_scale = np.float32(1.0 / np.sqrt(shard_rows * 4))
    col_grad = col_sum * col_scale

    row_line = row_index[None, :]
    away = put_rows(row_line, grad, 4, 4, side)
    home = put_rows(row_line, grad, 0, 4, side)
    core = swap(away, "col", flip(1))
    both = home + core
    sent = both[1:].astype(BF16)
    got_x = swap(sent[0], "col", flip(2))
    got_y = swap(sent[1], "col", flip(4))
    got_xy = swap(sent[2], "col", flip(6))
    row_scale = np.float32(1.0 / np.sqrt(shard_cols * 8))
    row_sum = both[0] + got_x.astype(F32) + got_y.astype(F32) + got_xy.astype(F32)
    return (row_sum * row_scale, col_grad)


def solution(mesh):
    in_specs = (
        P("row", "col"),
        P("row", "col"),
        P("row"),
        P("col"),
        P("row"),
        P("col"),
        P(("row", "col"), None),
        P(("col", "row"), None),
    )
    out_specs = (P(("row", "col"), None), P(("col", "row"), None))
    line = mesh.shape["row"] == 4 and mesh.shape["col"] == 8
    body = line_shards if line else plain_shards
    return jax.shard_map(body, mesh=mesh, in_specs=in_specs, out_specs=out_specs, check_vma=False)
```

```python
import functools

import jax
import jax.numpy as jnp
import numpy as np
from jax import lax
from jax.experimental import pallas as pl
from jax.experimental.pallas import tpu as pltpu
from jax.sharding import PartitionSpec as P

F32 = jnp.float32
BF16 = jnp.bfloat16
LANES = 128
MIB = 1 << 20


def cell_delta(score, count, active, row_part, col_part):
    real_count = count.astype(F32)
    safe = jnp.maximum(real_count, 1.0)
    pmi = jnp.log(safe) - row_part[:, None] - col_part[None, :]
    confid = 0.1 + 0.25 * jnp.sqrt(safe)
    positive = confid * (score - pmi)
    zeroed = jax.nn.sigmoid(score - pmi)
    deriv = jnp.where(count > 0, positive, zeroed)
    return (active.astype(F32) * deriv).astype(BF16)


def plain_shards(counts, block_mask, row_perm, col_perm, row_logm, col_logm, row_emb, col_emb):
    shard_rows, shard_cols = counts.shape
    all_cols = shard_cols * lax.axis_size("col")
    all_rows = shard_rows * lax.axis_size("row")
    block_side = shard_rows // block_mask.shape[0]
    row_group = lax.all_gather(row_emb, "col", axis=0, tiled=True)
    col_group = lax.all_gather(col_emb, "row", axis=0, tiled=True)
    row_local = row_perm - lax.axis_index("row") * shard_rows
    col_local = col_perm - lax.axis_index("col") * shard_cols
    wvec = jnp.take(row_group, row_local, axis=0)
    cvec = jnp.take(col_group, col_local, axis=0)
    score = lax.dot_general(wvec, cvec, (((1,), (1,)), ((), ())), preferred_element_type=F32)
    active = jnp.repeat(jnp.repeat(block_mask, block_side, axis=0), block_side, axis=1)
    delta = cell_delta(score, counts, active, row_logm, col_logm)
    gshard = jnp.dot(delta, cvec, preferred_element_type=F32) / jnp.sqrt(F32(all_cols))
    ordered = jnp.zeros(gshard.shape, F32).at[row_local].set(gshard)
    row_grad = lax.psum_scatter(ordered, "col", scatter_dimension=0, tiled=True)
    hshard = lax.dot_general(
        delta, wvec, (((0,), (0,)), ((), ())), preferred_element_type=F32
    ) / jnp.sqrt(F32(all_rows))
    col_ordered = jnp.zeros(hshard.shape, F32).at[col_local].set(hshard)
    col_grad = lax.psum_scatter(col_ordered, "row", scatter_dimension=0, tiled=True)
    return (row_grad, col_grad)


ROW_AT, COL_AT, AT_END, ORDER = 0, 1, 2, 3

WHOLE = pl.BlockSpec(memory_space=pltpu.VMEM)
SCALARS = pl.BlockSpec(memory_space=pltpu.SMEM)


def params(mib):
    return pltpu.CompilerParams(vmem_limit_bytes=mib * MIB)


def cost(flops, moved):
    return pl.CostEstimate(flops=flops, bytes_accessed=moved, transcendentals=0)


def onehot(flag):
    return jnp.where(flag, 1.0, 0.0).astype(BF16)


def pieces_of(value):
    high = value.astype(BF16)
    rest = value - high.astype(F32)
    middle = rest.astype(BF16)
    low = (rest - middle.astype(F32)).astype(BF16)
    return high, middle, low


def along_sublanes(value):
    fill = jnp.zeros((LANES - value.shape[0], LANES), F32)
    return jnp.concatenate([value, fill], axis=0).T


def order_kernel(slots, width, scalars, perm_ref, mask_ref, logm_ref, count_ref, *refs):
    parts = len(slots)
    outs, aux_outs, pick = refs[:parts], refs[parts : 2 * parts], refs[-1]
    depth = pick.shape[0]

    @pl.when(pl.program_id(0) == 0)
    def _():
        index = along_sublanes((perm_ref[...] - scalars[COL_AT] * depth).astype(F32))
        lane = lax.broadcasted_iota(jnp.int32, (LANES, width), 1)
        for part, slot in enumerate(slots):
            vocab = (lane + scalars[ORDER + slot] * width).astype(F32)
            for group in range(depth // LANES):
                pick[pl.ds(group * LANES, LANES), pl.ds(part * width, width)] = onehot(
                    index[:, group : group + 1] == vocab
                )
        blocks_r, blocks_c = mask_ref.shape
        mask = mask_ref[...].astype(F32)
        side = (blocks_r, depth // blocks_c)
        active = jnp.concatenate(
            [jnp.broadcast_to(mask[:, at : at + 1], side) for at in range(blocks_c)], axis=1
        )
        logm = jnp.broadcast_to(logm_ref[...], (8, depth))
        values = jnp.concatenate([active.astype(BF16), *pieces_of(logm)], axis=0)
        moved = jnp.dot(values, pick[...], preferred_element_type=F32)
        logm_out = moved[blocks_r : blocks_r + 8]
        logm_out = logm_out + moved[blocks_r + 8 : blocks_r + 16]
        logm_out = logm_out + moved[blocks_r + 16 :]
        for part in range(parts):
            here = slice(part * width, (part + 1) * width)
            aux_outs[part][pl.ds(0, blocks_r), :] = moved[:blocks_r, here]
            aux_outs[part][pl.ds(blocks_r, 8), :] = logm_out[:, here]

    tile = 256
    for first in range(0, count_ref.shape[0], tile):
        here = pl.ds(first, tile)
        shifted = (count_ref[here, :] - 256).astype(F32).astype(BF16)
        for part in range(parts):
            chosen = pick[:, pl.ds(part * width, width)]
            moved = jnp.dot(shifted, chosen, preferred_element_type=F32)
            outs[part][here, :] = moved.astype(BF16)


def order_counts(scalars, col_perm, block_mask, col_logm, counts, slots, width):
    rows, cols = counts.shape
    parts = len(slots)
    step = 512
    aux_rows = block_mask.shape[0] + 8
    fixed = lambda i: (0, 0)
    return pl.pallas_call(
        functools.partial(order_kernel, slots, width),
        grid=(rows // step,),
        in_specs=[
            SCALARS,
            pl.BlockSpec((cols // LANES, LANES), fixed),
            pl.BlockSpec(block_mask.shape, fixed),
            pl.BlockSpec((1, cols), fixed),
            pl.BlockSpec((step, cols), lambda i: (i, 0)),
        ],
        out_specs=[pl.BlockSpec((step, width), lambda i: (i, 0))] * parts
        + [pl.BlockSpec((aux_rows, width), fixed)] * parts,
        scratch_shapes=[pltpu.VMEM((cols, parts * width), BF16)],
        out_shape=[jax.ShapeDtypeStruct((rows, width), BF16)] * parts
        + [jax.ShapeDtypeStruct((aux_rows, width), F32)] * parts,
        compiler_params=params(46),
        cost_estimate=cost(2 * rows * cols * parts * width, 4 * rows * cols),
        name="order_counts",
    )(scalars, col_perm.reshape(-1, LANES), block_mask, col_logm[None, :], counts)


def take_kernel(scalars, perm_ref, logm_ref, group_ref, out_ref, logm_out, pick):
    rows = out_ref.shape[0]
    depth = group_ref.shape[0]
    groups = rows // LANES
    index = (perm_ref[...] - scalars[ROW_AT] * rows).astype(F32)
    columns = along_sublanes(jnp.concatenate([index, logm_ref[...]], axis=0))
    step = pick.shape[1]
    vocab = lax.broadcasted_iota(jnp.int32, (LANES, depth), 1).astype(F32)
    for first in range(0, rows, step):
        slot = (first // step) % pick.shape[0]
        for inner in range(0, step, LANES):
            at = (first + inner) // LANES
            pick[slot, pl.ds(inner, LANES), :] = onehot(columns[:, at : at + 1] == vocab)
            logm_out[pl.ds(first + inner, LANES), :] = jnp.broadcast_to(
                columns[:, groups + at : groups + at + 1], (LANES, LANES)
            )
        out_ref[pl.ds(first, step), :] = jnp.dot(
            pick[slot], group_ref[...], preferred_element_type=F32
        ).astype(BF16)


def take_rows(scalars, row_perm, row_logm, group):
    rows = row_perm.shape[0]
    width = group.shape[1]
    return pl.pallas_call(
        take_kernel,
        in_specs=[SCALARS, WHOLE, WHOLE, WHOLE],
        out_specs=[WHOLE, WHOLE],
        out_shape=[
            jax.ShapeDtypeStruct((rows, width), BF16),
            jax.ShapeDtypeStruct((rows, LANES), F32),
        ],
        scratch_shapes=[pltpu.VMEM((2, 512, group.shape[0]), BF16)],
        compiler_params=params(16),
        cost_estimate=cost(2 * rows * rows * width, 4 * rows * width),
        name="take_rows",
    )(scalars, row_perm.reshape(-1, LANES), row_logm.reshape(-1, LANES), group)


def cells_kernel(has_sum, scalars, first_ref, second_ref, wvec_ref, count_ref, aux_ref, logm_ref, *refs):
    if has_sum:
        before_ref, refs = refs[0], refs[1:]
    grad_ref, term_ref, sent_ref, chunk, delta_ref = refs

    @pl.when(scalars[AT_END] == 1)
    def _():
        chunk[...] = first_ref[...]

    @pl.when(scalars[AT_END] == 0)
    def _():
        chunk[...] = second_ref[...]

    cvec = chunk[...]
    rows = wvec_ref.shape[0]
    width = cvec.shape[0]
    blocks = aux_ref.shape[0] - 8
    tile = rows // blocks
    col_logm = aux_ref[blocks : blocks + 1, :]

    def score_of(at):
        wvec = wvec_ref[pl.ds(at * tile, tile), :]
        return lax.dot_general(wvec, cvec, (((1,), (1,)), ((), ())), preferred_element_type=F32)

    def delta_of(at, score):
        here = pl.ds(at * tile, tile)
        count = count_ref[here, :].astype(F32) + 256.0
        safe = jnp.maximum(count, 1.0)
        row_logm = jnp.concatenate([logm_ref[here, :]] * (width // LANES), axis=1)
        gap = score + ((row_logm + col_logm) - jnp.log(safe))
        confid = 0.1 + 0.25 * (safe * lax.rsqrt(safe))
        zeroed = 0.5 * jnp.tanh(0.5 * gap) + 0.5
        deriv = jnp.where(count > 0.0, confid * gap, zeroed)
        delta_ref[here, :] = (deriv * aux_ref[at : at + 1, :]).astype(BF16)

    def terms_of(first, count):
        here = pl.ds(first * tile, count * tile)
        delta = delta_ref[here, :]
        grad = jnp.dot(delta, cvec, preferred_element_type=F32)
        if has_sum:
            grad = grad + before_ref[here, :]
        grad_ref[here, :] = grad
        term = lax.dot_general(
            delta, wvec_ref[here, :], (((0,), (0,)), ((), ())), preferred_element_type=F32
        )
        if first:
            term = term_ref[...] + term
        term_ref[...] = term

    joined = 2
    ahead = score_of(0)
    for at in range(blocks):
        score = ahead
        if at + 1 < blocks:
            ahead = score_of(at + 1)
        delta_of(at, score)
        if at and at % joined == 0:
            terms_of(at - joined, joined)
    terms_of(blocks - joined, joined)
    sent_ref[...] = term_ref[...].astype(BF16)


def cells(scalars, first, second, wvec, ordered, aux, logm, before):
    rows, depth = wvec.shape
    width = first.shape[0]
    args = [scalars, first, second, wvec, ordered, aux, logm]
    aliases = {}
    if before is not None:
        aliases = {len(args): 0}
        args.append(before)
    return pl.pallas_call(
        functools.partial(cells_kernel, before is not None),
        in_specs=[SCALARS] + [WHOLE] * (len(args) - 1),
        out_specs=[WHOLE] * 3,
        out_shape=[
            jax.ShapeDtypeStruct((rows, depth), F32),
            jax.ShapeDtypeStruct((width, depth), F32),
            jax.ShapeDtypeStruct((width, depth), BF16),
        ],
        scratch_shapes=[pltpu.VMEM((width, depth), BF16), pltpu.VMEM((rows, width), BF16)],
        input_output_aliases=aliases,
        compiler_params=params(32),
        cost_estimate=cost(rows * width * depth, rows * depth),
        name="cells",
    )(*args)


def put_kernel(offsets, exact, scalars, perm_ref, grad_ref, out_ref):
    grad = grad_ref[...]
    rows, width = grad.shape
    high = grad.astype(BF16)
    moving = high
    if exact:
        moving = jnp.concatenate([high, (grad - high.astype(F32)).astype(BF16)], axis=1)
    side = out_ref.shape[1]
    index = jnp.broadcast_to((perm_ref[...] - scalars[ROW_AT] * rows).astype(F32), (8, rows))[:1]
    vocab = lax.broadcasted_iota(jnp.int32, (side, rows), 0)
    for at, offset in enumerate(offsets):
        base = jnp.bitwise_xor(scalars[COL_AT], offset) * side
        pick = onehot(index == (vocab + base).astype(F32))
        moved = jnp.dot(pick, moving, preferred_element_type=F32)
        if exact:
            moved = moved[:, :width] + moved[:, width:]
        out_ref[at] = moved.astype(out_ref.dtype)


def put_rows(scalars, row_perm, grad, offsets, side, exact):
    width = grad.shape[1]
    return pl.pallas_call(
        functools.partial(put_kernel, offsets, exact),
        in_specs=[SCALARS, WHOLE, WHOLE],
        out_specs=WHOLE,
        out_shape=jax.ShapeDtypeStruct((len(offsets), side, width), F32 if exact else BF16),
        compiler_params=params(24),
        cost_estimate=cost(grad.size, grad.size),
        name="put_rows",
    )(scalars, row_perm[None, :], grad)


def swap(value, axis, pairs):
    return lax.ppermute(value, axis, pairs)


def together(values):
    return lax.optimization_barrier(values)


def line_shards(counts, block_mask, row_perm, col_perm, row_logm, col_logm, row_emb, col_emb):
    shard_rows, shard_cols = counts.shape
    row_at = lax.axis_index("row")
    col_at = lax.axis_index("col")
    side = row_emb.shape[0]
    width = col_emb.shape[0]

    outward = [(1, 0), (2, 3)]
    inward = [(0, 1), (3, 2)]
    across = [(1, 2), (2, 1)]
    flip = lambda bit: [(i, i ^ bit) for i in range(8)]

    near = swap(col_emb, "row", outward + inward)
    over = swap(col_emb, "row", across)
    group = lax.all_gather(row_emb, "col", axis=0, tiled=True)

    end = (row_at == 0) | (row_at == 3)
    real = lambda m: jnp.where(row_at >= 2, 3 - m, m)
    order = [real(jnp.where(end, e, m)) for e, m in ((3, 3), (2, 0), (1, 2), (0, 1))]
    scalars = jnp.stack([row_at, col_at, end, *order]).astype(jnp.int32)

    ordered = functools.partial(order_counts, scalars, col_perm, block_mask, col_logm)
    count_a, count_b, aux_a, aux_b = ordered(counts, (0, 1), width)
    near, over, count_a, counts = together((near, over, count_a, counts))
    two_out = swap(over, "row", outward)
    far_over = swap(near, "row", across)
    count_c, count_d, aux_c, aux_d = ordered(counts, (2, 3), width)
    two_out, far_over, count_c, group = together((two_out, far_over, count_c, group))
    three_out = swap(far_over, "row", outward)
    wvec, logm = take_rows(scalars, row_perm, row_logm, group)

    work = functools.partial(cells, scalars)
    grad, term_a, sent_a = work(three_out, far_over, wvec, count_a, aux_a, logm, None)
    got_a = swap(sent_a, "row", inward)
    grad, term_b, sent_b = work(two_out, near, wvec, count_b, aux_b, logm, grad)
    got_b = swap(sent_b, "row", inward)
    grad, term_c, sent_c = work(near, over, wvec, count_c, aux_c, logm, grad)
    got_c = swap(sent_c, "row", inward)
    grad, got_a = together((grad, got_a))

    sum_3 = (term_a + got_a.astype(F32)).astype(BF16)
    got_3 = swap(sum_3, "row", across)
    grad, sum_3 = together((grad, sum_3))
    grad, term_d, _ = work(col_emb, col_emb, wvec, count_d, aux_d, logm, grad)
    away = put_rows(scalars, row_perm, grad, (1, 3, 5, 7), side, False)
    core = swap(away, "col", flip(1))
    grad, away, got_b, got_3 = together((grad, away, got_b, got_3))
    sum_2 = (term_c + got_b.astype(F32)).astype(BF16)
    got_2 = swap(sum_2, "row", across)
    home = put_rows(scalars, row_perm, grad, (0, 2, 4, 6), side, True)
    sum_0 = (term_b + got_3.astype(F32)).astype(BF16)
    got_0 = swap(sum_0, "row", outward)
    both = home + core.astype(F32)
    got_x = swap(both[1].astype(BF16), "col", flip(2))
    got_y = swap(both[2].astype(BF16), "col", flip(4))
    got_xy = swap(both[3].astype(BF16), "col", flip(6))
    row_sum = both[0] + got_x.astype(F32) + got_y.astype(F32) + got_xy.astype(F32)
    col_sum = term_d + got_c.astype(F32) + got_2.astype(F32) + got_0.astype(F32)
    row_scale = np.float32(1.0 / np.sqrt(shard_cols * 8))
    col_scale = np.float32(1.0 / np.sqrt(shard_rows * 4))
    return (row_sum * row_scale, col_sum * col_scale)


def solution(mesh):
    in_specs = (
        P("row", "col"),
        P("row", "col"),
        P("row"),
        P("col"),
        P("row"),
        P("col"),
        P(("row", "col"), None),
        P(("col", "row"), None),
    )
    out_specs = (P(("row", "col"), None), P(("col", "row"), None))
    line = mesh.shape["row"] == 4 and mesh.shape["col"] == 8
    body = line_shards if line else plain_shards
    return jax.shard_map(body, mesh=mesh, in_specs=in_specs, out_specs=out_specs, check_vma=False)
```

```python
import functools

import jax
import jax.numpy as jnp
import numpy as np
from jax import lax
from jax.experimental import pallas as pl
from jax.experimental.pallas import tpu as pltpu
from jax.sharding import PartitionSpec as P

F32 = jnp.float32
BF16 = jnp.bfloat16
LANES = 128
MIB = 1 << 20


def cell_delta(score, count, active, row_part, col_part):
    real_count = count.astype(F32)
    safe = jnp.maximum(real_count, 1.0)
    pmi = jnp.log(safe) - row_part[:, None] - col_part[None, :]
    confid = 0.1 + 0.25 * jnp.sqrt(safe)
    positive = confid * (score - pmi)
    zeroed = jax.nn.sigmoid(score - pmi)
    deriv = jnp.where(count > 0, positive, zeroed)
    return (active.astype(F32) * deriv).astype(BF16)


def plain_shards(counts, block_mask, row_perm, col_perm, row_logm, col_logm, row_emb, col_emb):
    shard_rows, shard_cols = counts.shape
    all_cols = shard_cols * lax.axis_size("col")
    all_rows = shard_rows * lax.axis_size("row")
    block_side = shard_rows // block_mask.shape[0]
    row_group = lax.all_gather(row_emb, "col", axis=0, tiled=True)
    col_group = lax.all_gather(col_emb, "row", axis=0, tiled=True)
    row_local = row_perm - lax.axis_index("row") * shard_rows
    col_local = col_perm - lax.axis_index("col") * shard_cols
    wvec = jnp.take(row_group, row_local, axis=0)
    cvec = jnp.take(col_group, col_local, axis=0)
    score = lax.dot_general(wvec, cvec, (((1,), (1,)), ((), ())), preferred_element_type=F32)
    active = jnp.repeat(jnp.repeat(block_mask, block_side, axis=0), block_side, axis=1)
    delta = cell_delta(score, counts, active, row_logm, col_logm)
    gshard = jnp.dot(delta, cvec, preferred_element_type=F32) / jnp.sqrt(F32(all_cols))
    ordered = jnp.zeros(gshard.shape, F32).at[row_local].set(gshard)
    row_grad = lax.psum_scatter(ordered, "col", scatter_dimension=0, tiled=True)
    hshard = lax.dot_general(
        delta, wvec, (((0,), (0,)), ((), ())), preferred_element_type=F32
    ) / jnp.sqrt(F32(all_rows))
    col_ordered = jnp.zeros(hshard.shape, F32).at[col_local].set(hshard)
    col_grad = lax.psum_scatter(col_ordered, "row", scatter_dimension=0, tiled=True)
    return (row_grad, col_grad)


ROW_AT, COL_AT, AT_END, ORDER = 0, 1, 2, 3

WHOLE = pl.BlockSpec(memory_space=pltpu.VMEM)
SCALARS = pl.BlockSpec(memory_space=pltpu.SMEM)


def params(mib):
    return pltpu.CompilerParams(vmem_limit_bytes=mib * MIB)


def cost(flops, moved):
    return pl.CostEstimate(flops=flops, bytes_accessed=moved, transcendentals=0)


def onehot(flag):
    return jnp.where(flag, 1.0, 0.0).astype(BF16)


def pieces_of(value):
    high = value.astype(BF16)
    rest = value - high.astype(F32)
    middle = rest.astype(BF16)
    low = (rest - middle.astype(F32)).astype(BF16)
    return high, middle, low


def along_sublanes(value):
    fill = jnp.zeros((LANES - value.shape[0], LANES), F32)
    return jnp.concatenate([value, fill], axis=0).T


def copies(pairs, sems):
    made = [pltpu.make_async_copy(src, dst, sems.at[at]) for at, (src, dst) in enumerate(pairs)]
    for copy in made:
        copy.start()
    return made


def fill_pick(pick, columns, base):
    depth, width = pick.shape
    vocab = (lax.broadcasted_iota(jnp.int32, (LANES, width), 1) + base).astype(F32)
    for group in range(depth // LANES):
        pick[pl.ds(group * LANES, LANES), :] = onehot(columns[:, group : group + 1] == vocab)


def move_values(values, pick, aux_ref):
    moved = jnp.dot(values, pick[...], preferred_element_type=F32)
    rows = values.shape[0] - 24
    aux_ref[pl.ds(0, rows), :] = moved[:rows]
    aux_ref[pl.ds(rows, 8), :] = moved[rows : rows + 8] + moved[rows + 8 : rows + 16] + moved[rows + 16 :]


def order_first_kernel(
    slot, scalars, perm_hbm, mask_hbm, logm_hbm, count_hbm,
    out_ref, aux_ref, shifted_ref, columns_ref, values_ref,
    perm, mask_ref, logm_ref, tiles, pick, sems, tile_sems,
):
    depth, width = pick.shape
    rows = out_ref.shape[0]
    step = tiles.shape[1]
    steps = rows // step

    def tile_copy(at):
        slot_at = at % tiles.shape[0]
        return pltpu.make_async_copy(
            count_hbm.at[pl.ds(at * step, step)], tiles.at[slot_at], tile_sems.at[slot_at]
        )

    small = copies([(perm_hbm, perm), (mask_hbm, mask_ref), (logm_hbm, logm_ref)], sems)
    for at in range(tiles.shape[0]):
        tile_copy(at).start()
    for copy in small:
        copy.wait()
    columns = along_sublanes((perm[...] - scalars[COL_AT] * depth).astype(F32))
    columns_ref[...] = columns
    fill_pick(pick, columns, scalars[ORDER + slot] * width)
    blocks_r, blocks_c = mask_ref.shape
    mask = mask_ref[...].astype(F32)
    side = (blocks_r, depth // blocks_c)
    active = jnp.concatenate(
        [jnp.broadcast_to(mask[:, at : at + 1], side) for at in range(blocks_c)], axis=1
    )
    logm = jnp.broadcast_to(logm_ref[...], (8, depth))
    values = jnp.concatenate([active, *[piece.astype(F32) for piece in pieces_of(logm)]], axis=0)
    values_ref[...] = values
    move_values(values.astype(BF16), pick, aux_ref)
    for at in range(steps):
        here = pl.ds(at * step, step)
        tile_copy(at).wait()
        shifted = (tiles[at % tiles.shape[0]] - 256).astype(F32).astype(BF16)
        shifted_ref[here, :] = shifted
        out_ref[here, :] = jnp.dot(shifted, pick[...], preferred_element_type=F32).astype(BF16)
        if at + tiles.shape[0] < steps:
            tile_copy(at + tiles.shape[0]).start()


def order_first(scalars, col_perm, block_mask, col_logm, counts, slot, width):
    rows, cols = counts.shape
    blocks = block_mask.shape[0]
    outside = pl.BlockSpec(memory_space=pltpu.HBM)
    step = 512
    return pl.pallas_call(
        functools.partial(order_first_kernel, slot),
        in_specs=[SCALARS] + [outside] * 4,
        out_specs=[WHOLE] * 5,
        out_shape=[
            jax.ShapeDtypeStruct((rows, width), BF16),
            jax.ShapeDtypeStruct((blocks + 8, width), F32),
            jax.ShapeDtypeStruct((rows, cols), BF16),
            jax.ShapeDtypeStruct((LANES, LANES), F32),
            jax.ShapeDtypeStruct((blocks + 24, cols), F32),
        ],
        scratch_shapes=[
            pltpu.VMEM((cols // LANES, LANES), jnp.int32),
            pltpu.VMEM(block_mask.shape, jnp.int32),
            pltpu.VMEM((1, cols), F32),
            pltpu.VMEM((2, step, cols), jnp.int32),
            pltpu.VMEM((cols, width), BF16),
            pltpu.SemaphoreType.DMA((3,)),
            pltpu.SemaphoreType.DMA((2,)),
        ],
        compiler_params=params(24),
        cost_estimate=cost(2 * rows * cols * width, 4 * rows * cols),
        name="order_first",
    )(scalars, col_perm.reshape(-1, LANES), block_mask, col_logm[None, :], counts)


def order_next_kernel(slot, scalars, shifted_ref, columns_ref, values_ref, out_ref, aux_ref, pick):
    fill_pick(pick, columns_ref[...], scalars[ORDER + slot] * pick.shape[1])
    move_values(values_ref[...].astype(BF16), pick, aux_ref)
    step = 512
    for first in range(0, out_ref.shape[0], step):
        here = pl.ds(first, step)
        moved = jnp.dot(shifted_ref[here, :], pick[...], preferred_element_type=F32)
        out_ref[here, :] = moved.astype(BF16)


def order_next(scalars, shifted, columns, values, slot, width):
    rows, cols = shifted.shape
    return pl.pallas_call(
        functools.partial(order_next_kernel, slot),
        in_specs=[SCALARS] + [WHOLE] * 3,
        out_specs=[WHOLE] * 2,
        out_shape=[
            jax.ShapeDtypeStruct((rows, width), BF16),
            jax.ShapeDtypeStruct((values.shape[0] - 16, width), F32),
        ],
        scratch_shapes=[pltpu.VMEM((cols, width), BF16)],
        compiler_params=params(24),
        cost_estimate=cost(2 * rows * cols * width, 2 * rows * width),
        name="order_next",
    )(scalars, shifted, columns, values)


def take_kernel(scalars, perm_ref, logm_ref, *refs):
    own, from_x, from_y, from_xy, from_core, out_ref, turned_ref, logm_out, group, pick = refs
    side = own.shape[0]
    mine = [own, from_x, from_y, from_xy]
    blocks = [(2 * at, mine[at]) for at in range(4)] + [(2 * at + 1, from_core.at[at]) for at in range(4)]
    for offset, block in blocks:
        first = pl.multiple_of(jnp.bitwise_xor(scalars[COL_AT], offset) * side, side)
        group[pl.ds(first, side), :] = block[...]
    rows = out_ref.shape[0]
    depth = group.shape[0]
    groups = rows // LANES
    index = (perm_ref[...] - scalars[ROW_AT] * rows).astype(F32)
    columns = along_sublanes(jnp.concatenate([index, logm_ref[...]], axis=0))
    step = pick.shape[1]
    vocab = lax.broadcasted_iota(jnp.int32, (LANES, depth), 1).astype(F32)
    for first in range(0, rows, step):
        slot = (first // step) % pick.shape[0]
        for inner in range(0, step, LANES):
            at = (first + inner) // LANES
            pick[slot, pl.ds(inner, LANES), :] = onehot(columns[:, at : at + 1] == vocab)
            logm_out[pl.ds(first + inner, LANES), :] = jnp.broadcast_to(
                columns[:, groups + at : groups + at + 1], (LANES, LANES)
            )
        taken = jnp.dot(pick[slot], group[...], preferred_element_type=F32).astype(BF16)
        out_ref[pl.ds(first, step), :] = taken
        turned_ref[:, pl.ds(first, step)] = taken.T


def take_rows(scalars, row_perm, row_logm, blocks):
    rows = row_perm.shape[0]
    side, width = blocks[0].shape
    return pl.pallas_call(
        take_kernel,
        in_specs=[SCALARS] + [WHOLE] * 7,
        out_specs=[WHOLE] * 3,
        out_shape=[
            jax.ShapeDtypeStruct((rows, width), BF16),
            jax.ShapeDtypeStruct((width, rows), BF16),
            jax.ShapeDtypeStruct((rows, LANES), F32),
        ],
        scratch_shapes=[pltpu.VMEM((8 * side, width), BF16), pltpu.VMEM((2, 512, 8 * side), BF16)],
        compiler_params=params(24),
        cost_estimate=cost(2 * rows * rows * width, 4 * rows * width),
        name="take_rows",
    )(scalars, row_perm.reshape(-1, LANES), row_logm.reshape(-1, LANES), *blocks)


def cells_kernel(
    has_sum, scalars, first_ref, second_ref, wvec_ref, turned_ref, count_ref, aux_ref, logm_ref, *refs
):
    if has_sum:
        before_ref, refs = refs[0], refs[1:]
    grad_ref, term_ref, sent_ref, chunk, chunk_turned, delta_ref, sum_ref = refs

    @pl.when(scalars[AT_END] == 1)
    def _():
        chunk[...] = first_ref[...]

    @pl.when(scalars[AT_END] == 0)
    def _():
        chunk[...] = second_ref[...]

    chunk_turned[...] = chunk[...].T
    rows = wvec_ref.shape[0]
    width = chunk.shape[0]
    blocks = aux_ref.shape[0] - 8
    tile = rows // blocks
    col_logm = aux_ref[blocks : blocks + 1, :]

    def score_of(at):
        wvec = wvec_ref[pl.ds(at * tile, tile), :]
        return jnp.dot(wvec, chunk_turned[...], preferred_element_type=F32)

    def delta_of(at, score):
        here = pl.ds(at * tile, tile)
        count = count_ref[here, :].astype(F32) + 256.0
        safe = jnp.maximum(count, 1.0)
        row_logm = jnp.concatenate([logm_ref[here, :]] * (width // LANES), axis=1)
        gap = score + ((row_logm + col_logm) - jnp.log(safe))
        confid = 0.1 + 0.25 * (safe * lax.rsqrt(safe))
        zeroed = 0.5 * jnp.tanh(0.5 * gap) + 0.5
        deriv = jnp.where(count > 0.0, confid * gap, zeroed)
        delta_ref[here, :] = (deriv * aux_ref[at : at + 1, :]).astype(BF16)

    def terms_of(first, count):
        here = pl.ds(first * tile, count * tile)
        delta = delta_ref[here, :]
        grad = jnp.dot(delta, chunk[...], preferred_element_type=F32)
        if has_sum:
            grad = grad + before_ref[here, :]
        grad_ref[here, :] = grad
        term = jnp.dot(turned_ref[:, here], delta, preferred_element_type=F32)
        if first:
            term = sum_ref[...] + term
        sum_ref[...] = term

    joined = 2
    ahead = score_of(0)
    for at in range(blocks):
        score = ahead
        if at + 1 < blocks:
            ahead = score_of(at + 1)
        delta_of(at, score)
        if at and at % joined == 0:
            terms_of(at - joined, joined)
    terms_of(blocks - joined, joined)
    total = sum_ref[...].T
    term_ref[...] = total
    sent_ref[...] = total.astype(BF16)


def cells(scalars, first, second, wvec, turned, ordered, aux, logm, before):
    rows, depth = wvec.shape
    width = first.shape[0]
    args = [scalars, first, second, wvec, turned, ordered, aux, logm]
    aliases = {}
    if before is not None:
        aliases = {len(args): 0}
        args.append(before)
    return pl.pallas_call(
        functools.partial(cells_kernel, before is not None),
        in_specs=[SCALARS] + [WHOLE] * (len(args) - 1),
        out_specs=[WHOLE] * 3,
        out_shape=[
            jax.ShapeDtypeStruct((rows, depth), F32),
            jax.ShapeDtypeStruct((width, depth), F32),
            jax.ShapeDtypeStruct((width, depth), BF16),
        ],
        scratch_shapes=[
            pltpu.VMEM((width, depth), BF16),
            pltpu.VMEM((depth, width), BF16),
            pltpu.VMEM((rows, width), BF16),
            pltpu.VMEM((depth, width), F32),
        ],
        input_output_aliases=aliases,
        compiler_params=params(24),
        cost_estimate=cost(rows * width * depth, rows * depth),
        name="cells",
    )(*args)


def put_kernel(offsets, exact, scalars, perm_ref, grad_ref, out_ref):
    grad = grad_ref[...]
    rows, width = grad.shape
    high = grad.astype(BF16)
    moving = high
    if exact:
        moving = jnp.concatenate([high, (grad - high.astype(F32)).astype(BF16)], axis=1)
    side = out_ref.shape[1]
    index = jnp.broadcast_to((perm_ref[...] - scalars[ROW_AT] * rows).astype(F32), (8, rows))[:1]
    vocab = lax.broadcasted_iota(jnp.int32, (side, rows), 0)
    for at, offset in enumerate(offsets):
        base = jnp.bitwise_xor(scalars[COL_AT], offset) * side
        pick = onehot(index == (vocab + base).astype(F32))
        moved = jnp.dot(pick, moving, preferred_element_type=F32)
        if exact:
            moved = moved[:, :width] + moved[:, width:]
        out_ref[at] = moved.astype(out_ref.dtype)


def put_rows(scalars, row_perm, grad, offsets, side, exact):
    width = grad.shape[1]
    return pl.pallas_call(
        functools.partial(put_kernel, offsets, exact),
        in_specs=[SCALARS, WHOLE, WHOLE],
        out_specs=WHOLE,
        out_shape=jax.ShapeDtypeStruct((len(offsets), side, width), F32 if exact else BF16),
        compiler_params=params(24),
        cost_estimate=cost(grad.size, grad.size),
        name="put_rows",
    )(scalars, row_perm[None, :], grad)


def swap(value, axis, pairs):
    return lax.ppermute(value, axis, pairs)


def together(values):
    return lax.optimization_barrier(values)


def line_shards(counts, block_mask, row_perm, col_perm, row_logm, col_logm, row_emb, col_emb):
    shard_rows, shard_cols = counts.shape
    row_at = lax.axis_index("row")
    col_at = lax.axis_index("col")
    side = row_emb.shape[0]
    width = col_emb.shape[0]

    outward = [(1, 0), (2, 3)]
    inward = [(0, 1), (3, 2)]
    across = [(1, 2), (2, 1)]
    flip = lambda bit: [(i, i ^ bit) for i in range(8)]

    near = swap(col_emb, "row", outward + inward)
    over = swap(col_emb, "row", across)
    from_x = swap(row_emb, "col", flip(2))
    from_y = swap(row_emb, "col", flip(4))
    from_xy = swap(row_emb, "col", flip(6))

    end = (row_at == 0) | (row_at == 3)
    real = lambda m: jnp.where(row_at >= 2, 3 - m, m)
    order = [real(jnp.where(end, e, m)) for e, m in ((3, 3), (2, 0), (1, 2), (0, 1))]
    scalars = jnp.stack([row_at, col_at, end, *order]).astype(jnp.int32)

    counts = pltpu.with_memory_space_constraint(counts, pltpu.HBM)
    count_a, aux_a, shifted, columns, values = order_first(
        scalars, col_perm, block_mask, col_logm, counts, 0, width
    )
    near, over, from_x, from_y, from_xy, shifted = together((near, over, from_x, from_y, from_xy, shifted))
    far_over = swap(near, "row", across)
    two_out = swap(over, "row", outward)
    from_core = swap(jnp.stack([row_emb, from_x, from_y, from_xy]), "col", flip(1))
    ordered = functools.partial(order_next, scalars)
    count_b, aux_b = ordered(shifted, columns, values, 1, width)
    blocks = [row_emb, from_x, from_y, from_xy, from_core]
    count_b, blocks = together((count_b, blocks))
    wvec, turned, logm = take_rows(scalars, row_perm, row_logm, blocks)
    far_over, two_out, shifted, wvec = together((far_over, two_out, shifted, wvec))
    three_out = swap(far_over, "row", outward)
    count_c, aux_c = ordered(shifted, columns, values, 2, width)
    count_d, aux_d = ordered(shifted, columns, values, 3, width)
    three_out, count_c, count_d = together((three_out, count_c, count_d))

    work = functools.partial(cells, scalars)
    grad, term_a, sent_a = work(three_out, far_over, wvec, turned, count_a, aux_a, logm, None)
    got_a = swap(sent_a, "row", inward)
    grad, term_b, sent_b = work(two_out, near, wvec, turned, count_b, aux_b, logm, grad)
    got_b = swap(sent_b, "row", inward)
    grad, term_c, sent_c = work(near, over, wvec, turned, count_c, aux_c, logm, grad)
    got_c = swap(sent_c, "row", inward)
    grad, got_a = together((grad, got_a))

    sum_3 = (term_a + got_a.astype(F32)).astype(BF16)
    got_3 = swap(sum_3, "row", across)
    grad, sum_3 = together((grad, sum_3))
    grad, term_d, _ = work(col_emb, col_emb, wvec, turned, count_d, aux_d, logm, grad)
    away = put_rows(scalars, row_perm, grad, (1, 3, 5, 7), side, False)
    core = swap(away, "col", flip(1))
    grad, away, got_b, got_3 = together((grad, away, got_b, got_3))
    sum_2 = (term_c + got_b.astype(F32)).astype(BF16)
    got_2 = swap(sum_2, "row", across)
    home = put_rows(scalars, row_perm, grad, (0, 2, 4, 6), side, True)
    sum_0 = (term_b + got_3.astype(F32)).astype(BF16)
    got_0 = swap(sum_0, "row", outward)
    both = home + core.astype(F32)
    got_x = swap(both[1].astype(BF16), "col", flip(2))
    got_y = swap(both[2].astype(BF16), "col", flip(4))
    got_xy = swap(both[3].astype(BF16), "col", flip(6))
    row_sum = both[0] + got_x.astype(F32) + got_y.astype(F32) + got_xy.astype(F32)
    col_sum = term_d + got_c.astype(F32) + got_2.astype(F32) + got_0.astype(F32)
    row_scale = np.float32(1.0 / np.sqrt(shard_cols * 8))
    col_scale = np.float32(1.0 / np.sqrt(shard_rows * 4))
    return (row_sum * row_scale, col_sum * col_scale)


def solution(mesh):
    in_specs = (
        P("row", "col"),
        P("row", "col"),
        P("row"),
        P("col"),
        P("row"),
        P("col"),
        P(("row", "col"), None),
        P(("col", "row"), None),
    )
    out_specs = (P(("row", "col"), None), P(("col", "row"), None))
    line = mesh.shape["row"] == 4 and mesh.shape["col"] == 8
    body = line_shards if line else plain_shards
    return jax.shard_map(body, mesh=mesh, in_specs=in_specs, out_specs=out_specs, check_vma=False)
```

```python
import functools

import jax
import jax.numpy as jnp
import numpy as np
from jax import lax
from jax.experimental import pallas as pl
from jax.experimental.pallas import tpu as pltpu
from jax.sharding import PartitionSpec as P

F32 = jnp.float32
BF16 = jnp.bfloat16
LANES = 128
MIB = 1 << 20


def cell_delta(score, count, active, row_part, col_part):
    real_count = count.astype(F32)
    safe = jnp.maximum(real_count, 1.0)
    pmi = jnp.log(safe) - row_part[:, None] - col_part[None, :]
    confid = 0.1 + 0.25 * jnp.sqrt(safe)
    positive = confid * (score - pmi)
    zeroed = jax.nn.sigmoid(score - pmi)
    deriv = jnp.where(count > 0, positive, zeroed)
    return (active.astype(F32) * deriv).astype(BF16)


def plain_shards(counts, block_mask, row_perm, col_perm, row_logm, col_logm, row_emb, col_emb):
    shard_rows, shard_cols = counts.shape
    all_cols = shard_cols * lax.axis_size("col")
    all_rows = shard_rows * lax.axis_size("row")
    block_side = shard_rows // block_mask.shape[0]
    row_group = lax.all_gather(row_emb, "col", axis=0, tiled=True)
    col_group = lax.all_gather(col_emb, "row", axis=0, tiled=True)
    row_local = row_perm - lax.axis_index("row") * shard_rows
    col_local = col_perm - lax.axis_index("col") * shard_cols
    wvec = jnp.take(row_group, row_local, axis=0)
    cvec = jnp.take(col_group, col_local, axis=0)
    score = lax.dot_general(wvec, cvec, (((1,), (1,)), ((), ())), preferred_element_type=F32)
    active = jnp.repeat(jnp.repeat(block_mask, block_side, axis=0), block_side, axis=1)
    delta = cell_delta(score, counts, active, row_logm, col_logm)
    gshard = jnp.dot(delta, cvec, preferred_element_type=F32) / jnp.sqrt(F32(all_cols))
    ordered = jnp.zeros(gshard.shape, F32).at[row_local].set(gshard)
    row_grad = lax.psum_scatter(ordered, "col", scatter_dimension=0, tiled=True)
    hshard = lax.dot_general(
        delta, wvec, (((0,), (0,)), ((), ())), preferred_element_type=F32
    ) / jnp.sqrt(F32(all_rows))
    col_ordered = jnp.zeros(hshard.shape, F32).at[col_local].set(hshard)
    col_grad = lax.psum_scatter(col_ordered, "row", scatter_dimension=0, tiled=True)
    return (row_grad, col_grad)


ROW_AT, COL_AT = 0, 1

WHOLE = pl.BlockSpec(memory_space=pltpu.VMEM)
SCALARS = pl.BlockSpec(memory_space=pltpu.SMEM)


def params(mib):
    return pltpu.CompilerParams(vmem_limit_bytes=mib * MIB)


def cost(flops, moved):
    return pl.CostEstimate(flops=flops, bytes_accessed=moved, transcendentals=0)


def onehot(flag):
    return jnp.where(flag, 1.0, 0.0).astype(BF16)


def pieces_of(value):
    high = value.astype(BF16)
    rest = value - high.astype(F32)
    middle = rest.astype(BF16)
    low = (rest - middle.astype(F32)).astype(BF16)
    return high, middle, low


def along_sublanes(value):
    fill = jnp.zeros((LANES - value.shape[0], LANES), F32)
    return jnp.concatenate([value, fill], axis=0).T


def copies(pairs, sems):
    made = [pltpu.make_async_copy(src, dst, sems.at[at]) for at, (src, dst) in enumerate(pairs)]
    for copy in made:
        copy.start()
    return made


def fill_pick(pick, columns, base, groups):
    vocab = (lax.broadcasted_iota(jnp.int32, (LANES, pick.shape[1]), 1) + base).astype(F32)
    for group in groups:
        pick[pl.ds(group * LANES, LANES), :] = onehot(columns[:, group : group + 1] == vocab)


def chunk_base(scalars, offset, width):
    return jnp.bitwise_xor(scalars[ROW_AT], offset) * width


def move_values(values, pick, aux_ref):
    moved = jnp.dot(values, pick[...], preferred_element_type=F32)
    rows = values.shape[0] - 24
    aux_ref[pl.ds(0, rows), :] = moved[:rows]
    aux_ref[pl.ds(rows, 8), :] = moved[rows : rows + 8] + moved[rows + 8 : rows + 16] + moved[rows + 16 :]


def order_first_kernel(offsets, scalars, perm_hbm, mask_hbm, logm_hbm, count_hbm, *refs):
    parts = len(offsets)
    outs, auxes, refs = refs[:parts], refs[parts : 2 * parts], refs[2 * parts :]
    shifted_ref, columns_ref, values_ref, perm, mask_ref, logm_ref, tiles, pick, sems, tile_sems = refs
    depth = pick.shape[1]
    width = pick.shape[2]
    rows = outs[0].shape[0]
    step = tiles.shape[1]
    steps = rows // step

    def tile_copy(at):
        slot_at = at % tiles.shape[0]
        return pltpu.make_async_copy(
            count_hbm.at[pl.ds(at * step, step)], tiles.at[slot_at], tile_sems.at[slot_at]
        )

    small = copies([(perm_hbm, perm), (mask_hbm, mask_ref), (logm_hbm, logm_ref)], sems)
    for at in range(tiles.shape[0]):
        tile_copy(at).start()
    for copy in small:
        copy.wait()
    columns = along_sublanes((perm[...] - scalars[COL_AT] * depth).astype(F32))
    columns_ref[...] = columns
    blocks_r, blocks_c = mask_ref.shape
    mask = mask_ref[...].astype(F32)
    side = (blocks_r, depth // blocks_c)
    active = jnp.concatenate(
        [jnp.broadcast_to(mask[:, at : at + 1], side) for at in range(blocks_c)], axis=1
    )
    logm = jnp.broadcast_to(logm_ref[...], (8, depth))
    values = jnp.concatenate([active, *[piece.astype(F32) for piece in pieces_of(logm)]], axis=0)
    values_ref[...] = values
    values = values.astype(BF16)
    for part, offset in enumerate(offsets):
        fill_pick(pick.at[part], columns, chunk_base(scalars, offset, width), range(depth // LANES))
        move_values(values, pick.at[part], auxes[part])
    for at in range(steps):
        here = pl.ds(at * step, step)
        tile_copy(at).wait()
        shifted = (tiles[at % tiles.shape[0]] - 256).astype(F32).astype(BF16)
        shifted_ref[here, :] = shifted
        if at + tiles.shape[0] < steps:
            tile_copy(at + tiles.shape[0]).start()
        for part in range(parts):
            moved = jnp.dot(shifted, pick[part], preferred_element_type=F32)
            outs[part][here, :] = moved.astype(BF16)


def order_first(scalars, col_perm, block_mask, col_logm, counts, offsets, width):
    rows, cols = counts.shape
    parts = len(offsets)
    blocks = block_mask.shape[0]
    outside = pl.BlockSpec(memory_space=pltpu.HBM)
    step = 256
    return pl.pallas_call(
        functools.partial(order_first_kernel, offsets),
        in_specs=[SCALARS] + [outside] * 4,
        out_specs=[WHOLE] * (2 * parts + 3),
        out_shape=[jax.ShapeDtypeStruct((rows, width), BF16)] * parts
        + [jax.ShapeDtypeStruct((blocks + 8, width), F32)] * parts
        + [
            jax.ShapeDtypeStruct((rows, cols), BF16),
            jax.ShapeDtypeStruct((LANES, LANES), F32),
            jax.ShapeDtypeStruct((blocks + 24, cols), F32),
        ],
        scratch_shapes=[
            pltpu.VMEM((cols // LANES, LANES), jnp.int32),
            pltpu.VMEM(block_mask.shape, jnp.int32),
            pltpu.VMEM((1, cols), F32),
            pltpu.VMEM((3, step, cols), jnp.int32),
            pltpu.VMEM((parts, cols, width), BF16),
            pltpu.SemaphoreType.DMA((3,)),
            pltpu.SemaphoreType.DMA((3,)),
        ],
        compiler_params=params(28),
        cost_estimate=cost(2 * parts * rows * cols * width, 4 * rows * cols),
        name="order_first",
    )(scalars, col_perm.reshape(-1, LANES), block_mask, col_logm[None, :], counts)


def order_next_kernel(offset, scalars, shifted_ref, columns_ref, values_ref, out_ref, aux_ref, pick):
    depth, width = pick.shape
    base = chunk_base(scalars, offset, width)
    fill_pick(pick, columns_ref[...], base, range(depth // LANES))
    move_values(values_ref[...].astype(BF16), pick, aux_ref)
    step = 256
    for first in range(0, out_ref.shape[0], step):
        here = pl.ds(first, step)
        moved = jnp.dot(shifted_ref[here, :], pick[...], preferred_element_type=F32)
        out_ref[here, :] = moved.astype(BF16)


def order_next(scalars, shifted, columns, values, offset, width):
    rows, cols = shifted.shape
    return pl.pallas_call(
        functools.partial(order_next_kernel, offset),
        in_specs=[SCALARS] + [WHOLE] * 3,
        out_specs=[WHOLE] * 2,
        out_shape=[
            jax.ShapeDtypeStruct((rows, width), BF16),
            jax.ShapeDtypeStruct((values.shape[0] - 16, width), F32),
        ],
        scratch_shapes=[pltpu.VMEM((cols, width), BF16)],
        compiler_params=params(24),
        cost_estimate=cost(rows * width, rows * width),
        name="order_next",
    )(scalars, shifted, columns, values)


def take_kernel(scalars, perm_ref, logm_ref, *refs):
    own, from_x, from_y, from_xy, from_core, out_ref, turned_ref, logm_out, group, pick = refs
    side = own.shape[0]
    mine = [own, from_x, from_y, from_xy]
    blocks = [(2 * at, mine[at]) for at in range(4)] + [(2 * at + 1, from_core.at[at]) for at in range(4)]
    for offset, block in blocks:
        first = pl.multiple_of(jnp.bitwise_xor(scalars[COL_AT], offset) * side, side)
        group[pl.ds(first, side), :] = block[...]
    rows = out_ref.shape[0]
    depth = group.shape[0]
    groups = rows // LANES
    index = (perm_ref[...] - scalars[ROW_AT] * rows).astype(F32)
    columns = along_sublanes(jnp.concatenate([index, logm_ref[...]], axis=0))
    step = pick.shape[1]
    vocab = lax.broadcasted_iota(jnp.int32, (LANES, depth), 1).astype(F32)
    for first in range(0, rows, step):
        slot = (first // step) % pick.shape[0]
        for inner in range(0, step, LANES):
            at = (first + inner) // LANES
            pick[slot, pl.ds(inner, LANES), :] = onehot(columns[:, at : at + 1] == vocab)
            logm_out[pl.ds(first + inner, LANES), :] = jnp.broadcast_to(
                columns[:, groups + at : groups + at + 1], (LANES, LANES)
            )
        taken = jnp.dot(pick[slot], group[...], preferred_element_type=F32).astype(BF16)
        out_ref[pl.ds(first, step), :] = taken
        turned_ref[:, pl.ds(first, step)] = taken.T


def take_rows(scalars, row_perm, row_logm, blocks):
    rows = row_perm.shape[0]
    side, width = blocks[0].shape
    return pl.pallas_call(
        take_kernel,
        in_specs=[SCALARS] + [WHOLE] * 7,
        out_specs=[WHOLE] * 3,
        out_shape=[
            jax.ShapeDtypeStruct((rows, width), BF16),
            jax.ShapeDtypeStruct((width, rows), BF16),
            jax.ShapeDtypeStruct((rows, LANES), F32),
        ],
        scratch_shapes=[pltpu.VMEM((8 * side, width), BF16), pltpu.VMEM((2, 512, 8 * side), BF16)],
        compiler_params=params(24),
        cost_estimate=cost(2 * rows * rows * width, 4 * rows * width),
        name="take_rows",
    )(scalars, row_perm.reshape(-1, LANES), row_logm.reshape(-1, LANES), *blocks)


def cells_kernel(has_sum, chunk, wvec_ref, turned_ref, count_ref, aux_ref, logm_ref, *refs):
    if has_sum:
        before_ref, refs = refs[0], refs[1:]
    grad_ref, term_ref, sent_ref, chunk_turned, delta_ref, sum_ref = refs
    chunk_turned[...] = chunk[...].T
    rows = wvec_ref.shape[0]
    width = chunk.shape[0]
    blocks = aux_ref.shape[0] - 8
    tile = rows // blocks
    strip = 32
    col_logm = aux_ref[blocks : blocks + 1, :]

    def score_of(at):
        wvec = wvec_ref[pl.ds(at * tile, tile), :]
        return jnp.dot(wvec, chunk_turned[...], preferred_element_type=F32)

    def delta_of(at, score, first):
        here = pl.ds(at * tile + first, strip)
        count = count_ref[here, :].astype(F32) + 256.0
        safe = jnp.maximum(count, 1.0)
        row_logm = jnp.concatenate([logm_ref[here, :]] * (width // LANES), axis=1)
        gap = score[first : first + strip] + ((row_logm + col_logm) - jnp.log(safe))
        confid = 0.1 + 0.25 * (safe * lax.rsqrt(safe))
        zeroed = 0.5 * jnp.tanh(0.5 * gap) + 0.5
        deriv = jnp.where(count > 0.0, confid * gap, zeroed)
        delta_ref[here, :] = (deriv * aux_ref[at : at + 1, :]).astype(BF16)

    def grad_of(at):
        here = pl.ds(at * tile, tile)
        grad = jnp.dot(delta_ref[here, :], chunk[...], preferred_element_type=F32)
        if has_sum:
            grad = grad + before_ref[here, :]
        grad_ref[here, :] = grad

    def term_of(first, count):
        here = pl.ds(first * tile, count * tile)
        term = jnp.dot(turned_ref[:, here], delta_ref[here, :], preferred_element_type=F32)
        if first:
            term = sum_ref[...] + term
        sum_ref[...] = term

    joined = 2
    scores = {0: score_of(0)}
    for at in range(blocks):
        jobs = []
        if at + 1 < blocks:
            jobs.append(lambda at=at: scores.update({at + 1: score_of(at + 1)}))
        if at:
            jobs.append(lambda at=at: grad_of(at - 1))
        if at and at % joined == 0:
            jobs.append(lambda at=at: term_of(at - joined, joined))
        score = scores.pop(at)
        strips = tile // strip
        for each in range(strips):
            if each % 2 == 0 and jobs:
                jobs.pop(0)()
            delta_of(at, score, each * strip)
    grad_of(blocks - 1)
    term_of(blocks - joined, joined)
    total = sum_ref[...].T
    term_ref[...] = total
    sent_ref[...] = total.astype(BF16)


def cells(chunk, wvec, turned, ordered, aux, logm, before):
    rows, depth = wvec.shape
    width = chunk.shape[0]
    args = [chunk, wvec, turned, ordered, aux, logm]
    aliases = {}
    if before is not None:
        aliases = {len(args): 0}
        args.append(before)
    return pl.pallas_call(
        functools.partial(cells_kernel, before is not None),
        in_specs=[WHOLE] * len(args),
        out_specs=[WHOLE] * 3,
        out_shape=[
            jax.ShapeDtypeStruct((rows, depth), F32),
            jax.ShapeDtypeStruct((width, depth), F32),
            jax.ShapeDtypeStruct((width, depth), BF16),
        ],
        scratch_shapes=[
            pltpu.VMEM((depth, width), BF16),
            pltpu.VMEM((rows, width), BF16),
            pltpu.VMEM((depth, width), F32),
        ],
        input_output_aliases=aliases,
        compiler_params=params(24),
        cost_estimate=cost(rows * width * depth, rows * depth),
        name="cells",
    )(*args)


def put_kernel(offsets, exact, scalars, perm_ref, grad_ref, out_ref):
    grad = grad_ref[...]
    rows, width = grad.shape
    high = grad.astype(BF16)
    moving = high
    if exact:
        moving = jnp.concatenate([high, (grad - high.astype(F32)).astype(BF16)], axis=1)
    side = out_ref.shape[1]
    index = jnp.broadcast_to((perm_ref[...] - scalars[ROW_AT] * rows).astype(F32), (8, rows))[:1]
    vocab = lax.broadcasted_iota(jnp.int32, (side, rows), 0)
    for at, offset in enumerate(offsets):
        base = jnp.bitwise_xor(scalars[COL_AT], offset) * side
        pick = onehot(index == (vocab + base).astype(F32))
        moved = jnp.dot(pick, moving, preferred_element_type=F32)
        if exact:
            moved = moved[:, :width] + moved[:, width:]
        out_ref[at] = moved.astype(out_ref.dtype)


def put_rows(scalars, row_perm, grad, offsets, side, exact):
    width = grad.shape[1]
    return pl.pallas_call(
        functools.partial(put_kernel, offsets, exact),
        in_specs=[SCALARS, WHOLE, WHOLE],
        out_specs=WHOLE,
        out_shape=jax.ShapeDtypeStruct((len(offsets), side, width), F32 if exact else BF16),
        compiler_params=params(24),
        cost_estimate=cost((4096 if exact else 1) * grad.size, grad.size),
        name="put_rows",
    )(scalars, row_perm[None, :], grad)


def swap(value, axis, bit):
    pairs = [(at, at ^ bit) for at in range(lax.axis_size(axis))]
    return lax.ppermute(value, axis, pairs)


def together(values):
    return lax.optimization_barrier(values)


def line_shards(counts, block_mask, row_perm, col_perm, row_logm, col_logm, row_emb, col_emb):
    shard_rows, shard_cols = counts.shape
    side = row_emb.shape[0]
    width = col_emb.shape[0]
    scalars = jnp.stack([lax.axis_index("row"), lax.axis_index("col")]).astype(jnp.int32)

    from_x = swap(row_emb, "col", 2)
    from_y = swap(row_emb, "col", 4)
    from_xy = swap(row_emb, "col", 6)
    near = swap(col_emb, "row", 1)
    cross = swap(col_emb, "row", 2)
    counts = pltpu.with_memory_space_constraint(counts, pltpu.HBM)
    count_far, count_cross, count_near, aux_far, aux_cross, aux_near, shifted, columns, values = order_first(
        scalars, col_perm, block_mask, col_logm, counts, (3, 2, 1), width
    )
    from_x, from_y, from_xy, near, cross, shifted = together((from_x, from_y, from_xy, near, cross, shifted))
    far = swap(cross, "row", 1)
    from_core = swap(jnp.stack([row_emb, from_x, from_y, from_xy]), "col", 1)
    count_own, aux_own = order_next(scalars, shifted, columns, values, 0, width)
    count_own, near = together((count_own, near))
    blocks = [row_emb, from_x, from_y, from_xy, from_core]
    wvec, turned, logm = take_rows(scalars, row_perm, row_logm, blocks)

    grad, term_near, sent_near = cells(near, wvec, turned, count_near, aux_near, logm, None)
    grad, far = together((grad, far))
    grad, _, sent_far = cells(far, wvec, turned, count_far, aux_far, logm, grad)
    got_far = swap(sent_far, "row", 1)
    grad, term_cross, _ = cells(cross, wvec, turned, count_cross, aux_cross, logm, grad)
    got_near = swap(sent_near, "row", 1)
    grad, term_own, _ = cells(col_emb, wvec, turned, count_own, aux_own, logm, grad)

    grad, got_far, got_near = together((grad, got_far, got_near))
    sum_cross = (term_cross + got_far.astype(F32)).astype(BF16)
    got_cross = swap(sum_cross, "row", 2)
    grad, sum_cross = together((grad, sum_cross))
    away = put_rows(scalars, row_perm, grad, (1, 3, 5, 7), side, False)
    core = swap(away, "col", 1)
    grad, away = together((grad, away))
    home = put_rows(scalars, row_perm, grad, (0, 2, 4, 6), side, True)
    both = home + core.astype(F32)
    got_x = swap(both[1].astype(BF16), "col", 2)
    got_y = swap(both[2].astype(BF16), "col", 4)
    got_xy = swap(both[3].astype(BF16), "col", 6)
    row_sum = both[0] + got_x.astype(F32) + got_y.astype(F32) + got_xy.astype(F32)
    col_sum = term_own + got_near.astype(F32) + got_cross.astype(F32)
    row_scale = np.float32(1.0 / np.sqrt(shard_cols * 8))
    col_scale = np.float32(1.0 / np.sqrt(shard_rows * 4))
    return (row_sum * row_scale, col_sum * col_scale)


def solution(mesh):
    in_specs = (
        P("row", "col"),
        P("row", "col"),
        P("row"),
        P("col"),
        P("row"),
        P("col"),
        P(("row", "col"), None),
        P(("col", "row"), None),
    )
    out_specs = (P(("row", "col"), None), P(("col", "row"), None))
    line = mesh.shape["row"] == 4 and mesh.shape["col"] == 8
    body = line_shards if line else plain_shards
    return jax.shard_map(body, mesh=mesh, in_specs=in_specs, out_specs=out_specs, check_vma=False)
```

```python
import functools

import jax
import jax.numpy as jnp
import numpy as np
from jax import lax
from jax.experimental import pallas as pl
from jax.experimental.pallas import tpu as pltpu
from jax.sharding import PartitionSpec as P

F32 = jnp.float32
BF16 = jnp.bfloat16
LANES = 128
MIB = 1 << 20


def cell_delta(score, count, active, row_part, col_part):
    real_count = count.astype(F32)
    safe = jnp.maximum(real_count, 1.0)
    pmi = jnp.log(safe) - row_part[:, None] - col_part[None, :]
    confid = 0.1 + 0.25 * jnp.sqrt(safe)
    positive = confid * (score - pmi)
    zeroed = jax.nn.sigmoid(score - pmi)
    deriv = jnp.where(count > 0, positive, zeroed)
    return (active.astype(F32) * deriv).astype(BF16)


def plain_shards(counts, block_mask, row_perm, col_perm, row_logm, col_logm, row_emb, col_emb):
    shard_rows, shard_cols = counts.shape
    all_cols = shard_cols * lax.axis_size("col")
    all_rows = shard_rows * lax.axis_size("row")
    block_side = shard_rows // block_mask.shape[0]
    row_group = lax.all_gather(row_emb, "col", axis=0, tiled=True)
    col_group = lax.all_gather(col_emb, "row", axis=0, tiled=True)
    row_local = row_perm - lax.axis_index("row") * shard_rows
    col_local = col_perm - lax.axis_index("col") * shard_cols
    wvec = jnp.take(row_group, row_local, axis=0)
    cvec = jnp.take(col_group, col_local, axis=0)
    score = lax.dot_general(wvec, cvec, (((1,), (1,)), ((), ())), preferred_element_type=F32)
    active = jnp.repeat(jnp.repeat(block_mask, block_side, axis=0), block_side, axis=1)
    delta = cell_delta(score, counts, active, row_logm, col_logm)
    gshard = jnp.dot(delta, cvec, preferred_element_type=F32) / jnp.sqrt(F32(all_cols))
    ordered = jnp.zeros(gshard.shape, F32).at[row_local].set(gshard)
    row_grad = lax.psum_scatter(ordered, "col", scatter_dimension=0, tiled=True)
    hshard = lax.dot_general(
        delta, wvec, (((0,), (0,)), ((), ())), preferred_element_type=F32
    ) / jnp.sqrt(F32(all_rows))
    col_ordered = jnp.zeros(hshard.shape, F32).at[col_local].set(hshard)
    col_grad = lax.psum_scatter(col_ordered, "row", scatter_dimension=0, tiled=True)
    return (row_grad, col_grad)


ROW_AT, COL_AT = 0, 1

WHOLE = pl.BlockSpec(memory_space=pltpu.VMEM)
SCALARS = pl.BlockSpec(memory_space=pltpu.SMEM)


def params(mib):
    return pltpu.CompilerParams(vmem_limit_bytes=mib * MIB)


def cost(flops, moved):
    return pl.CostEstimate(flops=flops, bytes_accessed=moved, transcendentals=0)


def onehot(flag):
    return jnp.where(flag, 1.0, 0.0).astype(BF16)


def pieces_of(value):
    high = value.astype(BF16)
    rest = value - high.astype(F32)
    middle = rest.astype(BF16)
    low = (rest - middle.astype(F32)).astype(BF16)
    return high, middle, low


def along_sublanes(value):
    fill = jnp.zeros((LANES - value.shape[0], LANES), F32)
    return jnp.concatenate([value, fill], axis=0).T


def copies(pairs, sems):
    made = [pltpu.make_async_copy(src, dst, sems.at[at]) for at, (src, dst) in enumerate(pairs)]
    for copy in made:
        copy.start()
    return made


def fill_pick(pick, columns, base, groups):
    vocab = (lax.broadcasted_iota(jnp.int32, (LANES, pick.shape[1]), 1) + base).astype(F32)
    for group in groups:
        pick[pl.ds(group * LANES, LANES), :] = onehot(columns[:, group : group + 1] == vocab)


def chunk_base(scalars, offset, width):
    return jnp.bitwise_xor(scalars[ROW_AT], offset) * width


def move_values(values, pick, aux_ref):
    moved = jnp.dot(values, pick[...], preferred_element_type=F32)
    rows = values.shape[0] - 24
    aux_ref[pl.ds(0, rows), :] = moved[:rows]
    aux_ref[pl.ds(rows, 8), :] = moved[rows : rows + 8] + moved[rows + 8 : rows + 16] + moved[rows + 16 :]


def order_first_kernel(offsets, scalars, perm_hbm, mask_hbm, logm_hbm, count_hbm, *refs):
    parts = len(offsets)
    outs, auxes, refs = refs[:parts], refs[parts : 2 * parts], refs[2 * parts :]
    shifted_ref, columns_ref, values_ref, perm, mask_ref, logm_ref, tiles, pick, sems, tile_sems = refs
    depth = pick.shape[1]
    width = pick.shape[2]
    rows = outs[0].shape[0]
    step = tiles.shape[1]
    steps = rows // step

    slots = tiles.shape[0]

    def tile_copy(at):
        slot = lax.rem(at, slots)
        return pltpu.make_async_copy(
            count_hbm.at[pl.ds(pl.multiple_of(at * step, step), step)], tiles.at[slot], tile_sems.at[slot]
        )

    small = copies([(perm_hbm, perm), (mask_hbm, mask_ref), (logm_hbm, logm_ref)], sems)
    for at in range(slots):
        tile_copy(at).start()
    for copy in small:
        copy.wait()
    columns = along_sublanes((perm[...] - scalars[COL_AT] * depth).astype(F32))
    columns_ref[...] = columns
    blocks_r, blocks_c = mask_ref.shape
    mask = mask_ref[...].astype(F32)
    side = (blocks_r, depth // blocks_c)
    active = jnp.concatenate(
        [jnp.broadcast_to(mask[:, at : at + 1], side) for at in range(blocks_c)], axis=1
    )
    logm = jnp.broadcast_to(logm_ref[...], (8, depth))
    values = jnp.concatenate([active, *[piece.astype(F32) for piece in pieces_of(logm)]], axis=0)
    values_ref[...] = values
    values = values.astype(BF16)
    for part, offset in enumerate(offsets):
        fill_pick(pick.at[part], columns, chunk_base(scalars, offset, width), range(depth // LANES))
        move_values(values, pick.at[part], auxes[part])

    @pl.loop(0, steps)
    def _(at):
        here = pl.ds(pl.multiple_of(at * step, step), step)
        tile_copy(at).wait()
        shifted = (tiles[lax.rem(at, slots)] - 256).astype(F32).astype(BF16)
        shifted_ref[here, :] = shifted

        @pl.when(at + slots < steps)
        def _():
            tile_copy(at + slots).start()

        for part in range(parts):
            moved = jnp.dot(shifted, pick[part], preferred_element_type=F32)
            outs[part][here, :] = moved.astype(BF16)


def in_hbm(value):
    return pltpu.with_memory_space_constraint(value, pltpu.HBM)


def order_first(scalars, col_perm, block_mask, col_logm, counts, offsets, width):
    rows, cols = counts.shape
    parts = len(offsets)
    blocks = block_mask.shape[0]
    outside = pl.BlockSpec(memory_space=pltpu.HBM)
    step = 512
    return pl.pallas_call(
        functools.partial(order_first_kernel, offsets),
        in_specs=[SCALARS] + [outside] * 4,
        out_specs=[WHOLE] * (2 * parts + 3),
        out_shape=[jax.ShapeDtypeStruct((rows, width), BF16)] * parts
        + [jax.ShapeDtypeStruct((blocks + 8, width), F32)] * parts
        + [
            jax.ShapeDtypeStruct((rows, cols), BF16),
            jax.ShapeDtypeStruct((LANES, LANES), F32),
            jax.ShapeDtypeStruct((blocks + 24, cols), F32),
        ],
        scratch_shapes=[
            pltpu.VMEM((cols // LANES, LANES), jnp.int32),
            pltpu.VMEM(block_mask.shape, jnp.int32),
            pltpu.VMEM((1, cols), F32),
            pltpu.VMEM((2, step, cols), jnp.int32),
            pltpu.VMEM((parts, cols, width), BF16),
            pltpu.SemaphoreType.DMA((3,)),
            pltpu.SemaphoreType.DMA((2,)),
        ],
        compiler_params=params(28),
        cost_estimate=cost(2 * parts * rows * cols * width, 4 * rows * cols),
        name="order_first",
    )(scalars, *[in_hbm(each) for each in (col_perm.reshape(-1, LANES), block_mask, col_logm[None, :], counts)])


def order_next_kernel(offsets, scalars, shifted_ref, columns_ref, values_ref, *refs):
    parts = len(offsets)
    outs, auxes, pick = refs[:parts], refs[parts : 2 * parts], refs[-1]
    depth, width = pick.shape[1:]
    values = values_ref[...].astype(BF16)
    for part, offset in enumerate(offsets):
        base = chunk_base(scalars, offset, width)
        fill_pick(pick.at[part], columns_ref[...], base, range(depth // LANES))
        move_values(values, pick.at[part], auxes[part])
    step = 512

    @pl.loop(0, shifted_ref.shape[0] // step)
    def _(at):
        here = pl.ds(pl.multiple_of(at * step, step), step)
        for part in range(parts):
            moved = jnp.dot(shifted_ref[here, :], pick[part], preferred_element_type=F32)
            outs[part][here, :] = moved.astype(BF16)


def order_next(scalars, shifted, columns, values, offsets, width):
    rows, cols = shifted.shape
    parts = len(offsets)
    return pl.pallas_call(
        functools.partial(order_next_kernel, offsets),
        in_specs=[SCALARS] + [WHOLE] * 3,
        out_specs=[WHOLE] * (2 * parts),
        out_shape=[jax.ShapeDtypeStruct((rows, width), BF16)] * parts
        + [jax.ShapeDtypeStruct((values.shape[0] - 16, width), F32)] * parts,
        scratch_shapes=[pltpu.VMEM((parts, cols, width), BF16)],
        compiler_params=params(24),
        cost_estimate=cost(rows * width, rows * width),
        name="order_next",
    )(scalars, shifted, columns, values)


def take_kernel(scalars, perm_ref, logm_ref, *refs):
    own, from_x, from_y, from_xy, from_core, out_ref, turned_ref, logm_out, group, pick = refs
    side = own.shape[0]
    mine = [own, from_x, from_y, from_xy]
    blocks = [(2 * at, mine[at]) for at in range(4)] + [(2 * at + 1, from_core.at[at]) for at in range(4)]
    for offset, block in blocks:
        first = pl.multiple_of(jnp.bitwise_xor(scalars[COL_AT], offset) * side, side)
        group[pl.ds(first, side), :] = block[...]
    rows = out_ref.shape[0]
    depth = group.shape[0]
    groups = rows // LANES
    index = (perm_ref[...] - scalars[ROW_AT] * rows).astype(F32)
    columns = along_sublanes(jnp.concatenate([index, logm_ref[...]], axis=0))
    step = pick.shape[1]
    vocab = lax.broadcasted_iota(jnp.int32, (LANES, depth), 1).astype(F32)
    for first in range(0, rows, step):
        slot = (first // step) % pick.shape[0]
        for inner in range(0, step, LANES):
            at = (first + inner) // LANES
            pick[slot, pl.ds(inner, LANES), :] = onehot(columns[:, at : at + 1] == vocab)
            logm_out[pl.ds(first + inner, LANES), :] = jnp.broadcast_to(
                columns[:, groups + at : groups + at + 1], (LANES, LANES)
            )
        taken = jnp.dot(pick[slot], group[...], preferred_element_type=F32).astype(BF16)
        out_ref[pl.ds(first, step), :] = taken
        turned_ref[:, pl.ds(first, step)] = taken.T


def take_rows(scalars, row_perm, row_logm, blocks):
    rows = row_perm.shape[0]
    side, width = blocks[0].shape
    return pl.pallas_call(
        take_kernel,
        in_specs=[SCALARS] + [WHOLE] * 7,
        out_specs=[WHOLE] * 3,
        out_shape=[
            jax.ShapeDtypeStruct((rows, width), BF16),
            jax.ShapeDtypeStruct((width, rows), BF16),
            jax.ShapeDtypeStruct((rows, LANES), F32),
        ],
        scratch_shapes=[pltpu.VMEM((8 * side, width), BF16), pltpu.VMEM((2, 512, 8 * side), BF16)],
        compiler_params=params(24),
        cost_estimate=cost(2 * rows * rows * width, 4 * rows * width),
        name="take_rows",
    )(scalars, row_perm.reshape(-1, LANES), row_logm.reshape(-1, LANES), *blocks)


def cells_kernel(has_sum, chunk, wvec_ref, turned_ref, count_ref, aux_ref, logm_ref, *refs):
    if has_sum:
        before_ref, refs = refs[0], refs[1:]
    grad_ref, term_ref, sent_ref, chunk_turned, delta_ref, sum_ref = refs
    chunk_turned[...] = chunk[...].T
    rows = wvec_ref.shape[0]
    width = chunk.shape[0]
    blocks = aux_ref.shape[0] - 8
    tile = rows // blocks
    col_logm = aux_ref[blocks : blocks + 1, :]

    def rows_at(at, count=1):
        return pl.ds(pl.multiple_of(at * tile, tile), count * tile)

    def score_of(at):
        return jnp.dot(wvec_ref[rows_at(at), :], chunk_turned[...], preferred_element_type=F32)

    def delta_of(at, score):
        here = rows_at(at)
        count = count_ref[here, :].astype(F32) + 256.0
        safe = jnp.maximum(count, 1.0)
        row_logm = jnp.concatenate([logm_ref[here, :]] * (width // LANES), axis=1)
        gap = score + ((row_logm + col_logm) - jnp.log(safe))
        confid = 0.1 + 0.25 * (safe * lax.rsqrt(safe))
        zeroed = 0.5 * jnp.tanh(0.5 * gap) + 0.5
        deriv = jnp.where(count > 0.0, confid * gap, zeroed)
        delta_ref[here, :] = (deriv * aux_ref[pl.ds(at, 1), :]).astype(BF16)

    def grad_of(at):
        here = rows_at(at)
        grad = jnp.dot(delta_ref[here, :], chunk[...], preferred_element_type=F32)
        if has_sum:
            grad = grad + before_ref[here, :]
        grad_ref[here, :] = grad

    def term_of(at, count):
        here = rows_at(at, count)
        sum_ref[...] += jnp.dot(turned_ref[:, here], delta_ref[here, :], preferred_element_type=F32)

    joined = 4
    sum_ref[...] = jnp.zeros_like(sum_ref)

    @pl.loop(0, blocks // joined)
    def _(group):
        first = group * joined
        ahead = score_of(first)
        for at in range(joined):
            score = ahead
            if at + 1 < joined:
                ahead = score_of(first + at + 1)
            delta_of(first + at, score)
            if at:
                grad_of(first + at - 1)
            if at == joined // 2:
                term_of(first, joined // 2)
        grad_of(first + joined - 1)
        term_of(first + joined // 2, joined // 2)

    total = sum_ref[...].T
    term_ref[...] = total
    sent_ref[...] = total.astype(BF16)


def cells(chunk, wvec, turned, ordered, aux, logm, before):
    rows, depth = wvec.shape
    width = chunk.shape[0]
    args = [chunk, wvec, turned, ordered, aux, logm]
    aliases = {}
    if before is not None:
        aliases = {len(args): 0}
        args.append(before)
    return pl.pallas_call(
        functools.partial(cells_kernel, before is not None),
        in_specs=[WHOLE] * len(args),
        out_specs=[WHOLE] * 3,
        out_shape=[
            jax.ShapeDtypeStruct((rows, depth), F32),
            jax.ShapeDtypeStruct((width, depth), F32),
            jax.ShapeDtypeStruct((width, depth), BF16),
        ],
        scratch_shapes=[
            pltpu.VMEM((depth, width), BF16),
            pltpu.VMEM((rows, width), BF16),
            pltpu.VMEM((depth, width), F32),
        ],
        input_output_aliases=aliases,
        compiler_params=params(24),
        cost_estimate=cost(rows * width * depth, rows * depth),
        name="cells",
    )(*args)


def put_kernel(offsets, exact, scalars, perm_ref, grad_ref, out_ref):
    grad = grad_ref[...]
    rows, width = grad.shape
    high = grad.astype(BF16)
    moving = high
    if exact:
        moving = jnp.concatenate([high, (grad - high.astype(F32)).astype(BF16)], axis=1)
    side = out_ref.shape[1]
    index = jnp.broadcast_to((perm_ref[...] - scalars[ROW_AT] * rows).astype(F32), (8, rows))[:1]
    vocab = lax.broadcasted_iota(jnp.int32, (side, rows), 0)
    for at, offset in enumerate(offsets):
        base = jnp.bitwise_xor(scalars[COL_AT], offset) * side
        pick = onehot(index == (vocab + base).astype(F32))
        moved = jnp.dot(pick, moving, preferred_element_type=F32)
        if exact:
            moved = moved[:, :width] + moved[:, width:]
        out_ref[at] = moved.astype(out_ref.dtype)


def put_rows(scalars, row_perm, grad, offsets, side, exact):
    width = grad.shape[1]
    return pl.pallas_call(
        functools.partial(put_kernel, offsets, exact),
        in_specs=[SCALARS, WHOLE, WHOLE],
        out_specs=WHOLE,
        out_shape=jax.ShapeDtypeStruct((len(offsets), side, width), F32 if exact else BF16),
        compiler_params=params(24),
        cost_estimate=cost((4096 if exact else 1) * grad.size, grad.size),
        name="put_rows",
    )(scalars, row_perm[None, :], grad)


def swap(value, axis, bit):
    pairs = [(at, at ^ bit) for at in range(lax.axis_size(axis))]
    return lax.ppermute(value, axis, pairs)


def together(values):
    return lax.optimization_barrier(values)


def line_shards(counts, block_mask, row_perm, col_perm, row_logm, col_logm, row_emb, col_emb):
    shard_rows, shard_cols = counts.shape
    side = row_emb.shape[0]
    width = col_emb.shape[0]
    scalars = jnp.stack([lax.axis_index("row"), lax.axis_index("col")]).astype(jnp.int32)

    cross = swap(col_emb, "row", 2)
    near = swap(col_emb, "row", 1)
    count_far, aux_far, shifted, columns, values = order_first(
        scalars, col_perm, block_mask, col_logm, counts, (3,), width
    )
    ordered = functools.partial(order_next, scalars)
    row_block, shifted = together((row_emb, shifted))
    from_x = swap(row_block, "col", 2)
    from_y = swap(row_block, "col", 4)
    from_xy = swap(row_block, "col", 6)
    count_cross, count_near, aux_cross, aux_near = ordered(shifted, columns, values, (2, 1), width)
    cross, near, from_x, from_y, from_xy, count_near, shifted = together(
        (cross, near, from_x, from_y, from_xy, count_near, shifted)
    )
    far = swap(cross, "row", 1)
    from_core = swap(jnp.stack([row_emb, from_x, from_y, from_xy]), "col", 1)
    count_own, aux_own = ordered(shifted, columns, values, (0,), width)
    count_own, near = together((count_own, near))
    blocks = [row_emb, from_x, from_y, from_xy, from_core]
    wvec, turned, logm = take_rows(scalars, row_perm, row_logm, blocks)

    grad, term_near, sent_near = cells(near, wvec, turned, count_near, aux_near, logm, None)
    grad, far = together((grad, far))
    grad, _, sent_far = cells(far, wvec, turned, count_far, aux_far, logm, grad)
    got_far = swap(sent_far, "row", 1)
    grad, term_cross, _ = cells(cross, wvec, turned, count_cross, aux_cross, logm, grad)
    got_near = swap(sent_near, "row", 1)
    grad, got_near = together((grad, got_near))
    grad, term_own, _ = cells(col_emb, wvec, turned, count_own, aux_own, logm, grad)

    grad, got_far = together((grad, got_far))
    sum_cross = (term_cross + got_far.astype(F32)).astype(BF16)
    got_cross = swap(sum_cross, "row", 2)
    grad, sum_cross = together((grad, sum_cross))
    away = put_rows(scalars, row_perm, grad, (1, 3, 5, 7), side, False)
    core = swap(away, "col", 1)
    grad, away = together((grad, away))
    home = put_rows(scalars, row_perm, grad, (0, 2, 4, 6), side, True)
    both = home + core.astype(F32)
    got_x = swap(both[1].astype(BF16), "col", 2)
    got_y = swap(both[2].astype(BF16), "col", 4)
    got_xy = swap(both[3].astype(BF16), "col", 6)
    row_sum = both[0] + got_x.astype(F32) + got_y.astype(F32) + got_xy.astype(F32)
    col_sum = term_own + got_near.astype(F32) + got_cross.astype(F32)
    row_scale = np.float32(1.0 / np.sqrt(shard_cols * 8))
    col_scale = np.float32(1.0 / np.sqrt(shard_rows * 4))
    return (row_sum * row_scale, col_sum * col_scale)


def solution(mesh):
    in_specs = (
        P("row", "col"),
        P("row", "col"),
        P("row"),
        P("col"),
        P("row"),
        P("col"),
        P(("row", "col"), None),
        P(("col", "row"), None),
    )
    out_specs = (P(("row", "col"), None), P(("col", "row"), None))
    line = mesh.shape["row"] == 4 and mesh.shape["col"] == 8
    body = line_shards if line else plain_shards
    return jax.shard_map(body, mesh=mesh, in_specs=in_specs, out_specs=out_specs, check_vma=False)
```

```python
import functools

import jax
import jax.numpy as jnp
import numpy as np
from jax import lax
from jax.experimental import pallas as pl
from jax.experimental.pallas import tpu as pltpu
from jax.sharding import PartitionSpec as P

F32 = jnp.float32
BF16 = jnp.bfloat16
LANES = 128
MIB = 1 << 20


def cell_delta(score, count, active, row_part, col_part):
    real_count = count.astype(F32)
    safe = jnp.maximum(real_count, 1.0)
    pmi = jnp.log(safe) - row_part[:, None] - col_part[None, :]
    confid = 0.1 + 0.25 * jnp.sqrt(safe)
    positive = confid * (score - pmi)
    zeroed = jax.nn.sigmoid(score - pmi)
    deriv = jnp.where(count > 0, positive, zeroed)
    return (active.astype(F32) * deriv).astype(BF16)


def plain_shards(counts, block_mask, row_perm, col_perm, row_logm, col_logm, row_emb, col_emb):
    shard_rows, shard_cols = counts.shape
    all_cols = shard_cols * lax.axis_size("col")
    all_rows = shard_rows * lax.axis_size("row")
    block_side = shard_rows // block_mask.shape[0]
    row_group = lax.all_gather(row_emb, "col", axis=0, tiled=True)
    col_group = lax.all_gather(col_emb, "row", axis=0, tiled=True)
    row_local = row_perm - lax.axis_index("row") * shard_rows
    col_local = col_perm - lax.axis_index("col") * shard_cols
    wvec = jnp.take(row_group, row_local, axis=0)
    cvec = jnp.take(col_group, col_local, axis=0)
    score = lax.dot_general(wvec, cvec, (((1,), (1,)), ((), ())), preferred_element_type=F32)
    active = jnp.repeat(jnp.repeat(block_mask, block_side, axis=0), block_side, axis=1)
    delta = cell_delta(score, counts, active, row_logm, col_logm)
    gshard = jnp.dot(delta, cvec, preferred_element_type=F32) / jnp.sqrt(F32(all_cols))
    ordered = jnp.zeros(gshard.shape, F32).at[row_local].set(gshard)
    row_grad = lax.psum_scatter(ordered, "col", scatter_dimension=0, tiled=True)
    hshard = lax.dot_general(
        delta, wvec, (((0,), (0,)), ((), ())), preferred_element_type=F32
    ) / jnp.sqrt(F32(all_rows))
    col_ordered = jnp.zeros(hshard.shape, F32).at[col_local].set(hshard)
    col_grad = lax.psum_scatter(col_ordered, "row", scatter_dimension=0, tiled=True)
    return (row_grad, col_grad)


ROW_AT, COL_AT = 0, 1

WHOLE = pl.BlockSpec(memory_space=pltpu.VMEM)
SCALARS = pl.BlockSpec(memory_space=pltpu.SMEM)


def params(mib):
    return pltpu.CompilerParams(vmem_limit_bytes=mib * MIB)


def cost(flops, moved):
    return pl.CostEstimate(flops=flops, bytes_accessed=moved, transcendentals=0)


def onehot(flag):
    return jnp.where(flag, 1.0, 0.0).astype(BF16)


def pieces_of(value):
    high = value.astype(BF16)
    rest = value - high.astype(F32)
    middle = rest.astype(BF16)
    low = (rest - middle.astype(F32)).astype(BF16)
    return high, middle, low


def along_sublanes(value):
    fill = jnp.zeros((LANES - value.shape[0], LANES), F32)
    return jnp.concatenate([value, fill], axis=0).T


def copies(pairs, sems):
    made = [pltpu.make_async_copy(src, dst, sems.at[at]) for at, (src, dst) in enumerate(pairs)]
    for copy in made:
        copy.start()
    return made


def fill_pick(pick, columns, base, groups):
    vocab = (lax.broadcasted_iota(jnp.int32, (LANES, pick.shape[1]), 1) + base).astype(F32)
    for group in groups:
        pick[pl.ds(group * LANES, LANES), :] = onehot(columns[:, group : group + 1] == vocab)


def chunk_base(scalars, offset, width):
    return jnp.bitwise_xor(scalars[ROW_AT], offset) * width


def move_values(values, pick, aux_ref):
    moved = jnp.dot(values, pick[...], preferred_element_type=F32)
    rows = values.shape[0] - 24
    aux_ref[pl.ds(0, rows), :] = moved[:rows]
    aux_ref[pl.ds(rows, 8), :] = moved[rows : rows + 8] + moved[rows + 8 : rows + 16] + moved[rows + 16 :]


def order_first_kernel(offsets, scalars, perm_hbm, mask_hbm, logm_hbm, count_hbm, *refs):
    parts = len(offsets)
    outs, auxes, refs = refs[:parts], refs[parts : 2 * parts], refs[2 * parts :]
    shifted_ref, columns_ref, values_ref, perm, mask_ref, logm_ref, tiles, pick, sems, tile_sems = refs
    depth = pick.shape[1]
    width = pick.shape[2]
    rows = outs[0].shape[0]
    step = tiles.shape[1]
    steps = rows // step

    slots = tiles.shape[0]

    def tile_copy(at):
        slot = lax.rem(at, slots)
        return pltpu.make_async_copy(
            count_hbm.at[pl.ds(pl.multiple_of(at * step, step), step)], tiles.at[slot], tile_sems.at[slot]
        )

    small = copies([(perm_hbm, perm), (mask_hbm, mask_ref), (logm_hbm, logm_ref)], sems)
    for at in range(slots):
        tile_copy(at).start()
    for copy in small:
        copy.wait()
    columns = along_sublanes((perm[...] - scalars[COL_AT] * depth).astype(F32))
    columns_ref[...] = columns
    blocks_r, blocks_c = mask_ref.shape
    mask = mask_ref[...].astype(F32)
    side = (blocks_r, depth // blocks_c)
    active = jnp.concatenate(
        [jnp.broadcast_to(mask[:, at : at + 1], side) for at in range(blocks_c)], axis=1
    )
    logm = jnp.broadcast_to(logm_ref[...], (8, depth))
    values = jnp.concatenate([active, *[piece.astype(F32) for piece in pieces_of(logm)]], axis=0)
    values_ref[...] = values
    values = values.astype(BF16)
    for part, offset in enumerate(offsets):
        fill_pick(pick.at[part], columns, chunk_base(scalars, offset, width), range(depth // LANES))
        move_values(values, pick.at[part], auxes[part])

    @pl.loop(0, steps)
    def _(at):
        here = pl.ds(pl.multiple_of(at * step, step), step)
        tile_copy(at).wait()
        shifted = (tiles[lax.rem(at, slots)] - 256).astype(F32).astype(BF16)
        shifted_ref[here, :] = shifted

        @pl.when(at + slots < steps)
        def _():
            tile_copy(at + slots).start()

        for part in range(parts):
            moved = jnp.dot(shifted, pick[part], preferred_element_type=F32)
            outs[part][here, :] = moved.astype(BF16)


def in_hbm(value):
    return pltpu.with_memory_space_constraint(value, pltpu.HBM)


def order_first(scalars, col_perm, block_mask, col_logm, counts, offsets, width):
    rows, cols = counts.shape
    parts = len(offsets)
    blocks = block_mask.shape[0]
    outside = pl.BlockSpec(memory_space=pltpu.HBM)
    step = 512
    return pl.pallas_call(
        functools.partial(order_first_kernel, offsets),
        in_specs=[SCALARS] + [outside] * 4,
        out_specs=[WHOLE] * (2 * parts + 3),
        out_shape=[jax.ShapeDtypeStruct((rows, width), BF16)] * parts
        + [jax.ShapeDtypeStruct((blocks + 8, width), F32)] * parts
        + [
            jax.ShapeDtypeStruct((rows, cols), BF16),
            jax.ShapeDtypeStruct((LANES, LANES), F32),
            jax.ShapeDtypeStruct((blocks + 24, cols), F32),
        ],
        scratch_shapes=[
            pltpu.VMEM((cols // LANES, LANES), jnp.int32),
            pltpu.VMEM(block_mask.shape, jnp.int32),
            pltpu.VMEM((1, cols), F32),
            pltpu.VMEM((2, step, cols), jnp.int32),
            pltpu.VMEM((parts, cols, width), BF16),
            pltpu.SemaphoreType.DMA((3,)),
            pltpu.SemaphoreType.DMA((2,)),
        ],
        compiler_params=params(28),
        cost_estimate=cost(2 * parts * rows * cols * width, 4 * rows * cols),
        name="order_first",
    )(scalars, *[in_hbm(each) for each in (col_perm.reshape(-1, LANES), block_mask, col_logm[None, :], counts)])


def order_next_kernel(offsets, scalars, shifted_ref, columns_ref, values_ref, *refs):
    parts = len(offsets)
    outs, auxes, pick = refs[:parts], refs[parts : 2 * parts], refs[-1]
    depth, width = pick.shape[1:]
    values = values_ref[...].astype(BF16)
    for part, offset in enumerate(offsets):
        base = chunk_base(scalars, offset, width)
        fill_pick(pick.at[part], columns_ref[...], base, range(depth // LANES))
        move_values(values, pick.at[part], auxes[part])
    step = 512

    @pl.loop(0, shifted_ref.shape[0] // step)
    def _(at):
        here = pl.ds(pl.multiple_of(at * step, step), step)
        for part in range(parts):
            moved = jnp.dot(shifted_ref[here, :], pick[part], preferred_element_type=F32)
            outs[part][here, :] = moved.astype(BF16)


def order_next(scalars, shifted, columns, values, offsets, width):
    rows, cols = shifted.shape
    parts = len(offsets)
    return pl.pallas_call(
        functools.partial(order_next_kernel, offsets),
        in_specs=[SCALARS] + [WHOLE] * 3,
        out_specs=[WHOLE] * (2 * parts),
        out_shape=[jax.ShapeDtypeStruct((rows, width), BF16)] * parts
        + [jax.ShapeDtypeStruct((values.shape[0] - 16, width), F32)] * parts,
        scratch_shapes=[pltpu.VMEM((parts, cols, width), BF16)],
        compiler_params=params(24),
        cost_estimate=cost(rows * width, rows * width),
        name="order_next",
    )(scalars, shifted, columns, values)


def take_kernel(scalars, perm_ref, logm_ref, *refs):
    own, from_x, from_y, from_xy, from_core, out_ref, turned_ref, logm_out, group, pick = refs
    side = own.shape[0]
    mine = [own, from_x, from_y, from_xy]
    blocks = [(2 * at, mine[at]) for at in range(4)] + [(2 * at + 1, from_core.at[at]) for at in range(4)]
    for offset, block in blocks:
        first = pl.multiple_of(jnp.bitwise_xor(scalars[COL_AT], offset) * side, side)
        group[pl.ds(first, side), :] = block[...]
    rows = out_ref.shape[0]
    depth = group.shape[0]
    groups = rows // LANES
    index = (perm_ref[...] - scalars[ROW_AT] * rows).astype(F32)
    columns = along_sublanes(jnp.concatenate([index, logm_ref[...]], axis=0))
    step = pick.shape[1]
    vocab = lax.broadcasted_iota(jnp.int32, (LANES, depth), 1).astype(F32)
    for first in range(0, rows, step):
        slot = (first // step) % pick.shape[0]
        for inner in range(0, step, LANES):
            at = (first + inner) // LANES
            pick[slot, pl.ds(inner, LANES), :] = onehot(columns[:, at : at + 1] == vocab)
            logm_out[pl.ds(first + inner, LANES), :] = jnp.broadcast_to(
                columns[:, groups + at : groups + at + 1], (LANES, LANES)
            )
        taken = jnp.dot(pick[slot], group[...], preferred_element_type=F32).astype(BF16)
        out_ref[pl.ds(first, step), :] = taken
        turned_ref[:, pl.ds(first, step)] = taken.T


def take_rows(scalars, row_perm, row_logm, blocks):
    rows = row_perm.shape[0]
    side, width = blocks[0].shape
    return pl.pallas_call(
        take_kernel,
        in_specs=[SCALARS] + [WHOLE] * 7,
        out_specs=[WHOLE] * 3,
        out_shape=[
            jax.ShapeDtypeStruct((rows, width), BF16),
            jax.ShapeDtypeStruct((width, rows), BF16),
            jax.ShapeDtypeStruct((rows, LANES), F32),
        ],
        scratch_shapes=[pltpu.VMEM((8 * side, width), BF16), pltpu.VMEM((2, 512, 8 * side), BF16)],
        compiler_params=params(24),
        cost_estimate=cost(2 * rows * rows * width, 4 * rows * width),
        name="take_rows",
    )(scalars, row_perm.reshape(-1, LANES), row_logm.reshape(-1, LANES), *blocks)


def cells_kernel(has_sum, pieces, chunk, wvec_ref, turned_ref, count_ref, aux_ref, logm_ref, *refs):
    if has_sum:
        before_ref, refs = refs[0], refs[1:]
    grad_ref, term_ref, sent_refs = refs[0], refs[1], refs[2 : 2 + pieces]
    chunk_turned, delta_ref, sum_ref = refs[2 + pieces :]
    chunk_turned[...] = chunk[...].T
    rows = wvec_ref.shape[0]
    width = chunk.shape[0]
    blocks = aux_ref.shape[0] - 8
    tile = rows // blocks
    joined = delta_ref.shape[0] // tile
    half = joined // 2
    col_logm = aux_ref[blocks : blocks + 1, :]
    sum_ref[...] = jnp.zeros_like(sum_ref)

    @pl.loop(0, blocks // joined)
    def _(group):
        def rows_at(at, count=1):
            return pl.ds(pl.multiple_of((group * joined + at) * tile, tile), count * tile)

        def held(at, count=1):
            return delta_ref[pl.ds(at * tile, count * tile), :]

        def score_of(at):
            return jnp.dot(wvec_ref[rows_at(at), :], chunk_turned[...], preferred_element_type=F32)

        def delta_of(at, score):
            here = rows_at(at)
            count = count_ref[here, :].astype(F32) + 256.0
            log = jnp.log(jnp.maximum(count, 1.0))
            row_logm = jnp.concatenate([logm_ref[here, :]] * (width // LANES), axis=1)
            gap = score + ((row_logm + col_logm) - log)
            confid = 0.1 + 0.25 * jnp.exp2(log * np.float32(0.5 / np.log(2.0)))
            zeroed = 0.5 * jnp.tanh(0.5 * gap) + 0.5
            deriv = jnp.where(count > 0.0, confid * gap, zeroed)
            active = aux_ref[pl.ds(group * joined + at, 1), :]
            delta_ref[pl.ds(at * tile, tile), :] = (deriv * active).astype(BF16)

        def grad_of(at):
            grad = jnp.dot(held(at), chunk[...], preferred_element_type=F32)
            if has_sum:
                grad = grad + before_ref[rows_at(at), :]
            grad_ref[rows_at(at), :] = grad

        def term_of(at):
            turned = turned_ref[:, rows_at(at, half)]
            sum_ref[...] += jnp.dot(turned, held(at, half), preferred_element_type=F32)

        ahead = score_of(0)
        for at in range(joined):
            score = ahead
            if at + 1 < joined:
                ahead = score_of(at + 1)
            delta_of(at, score)
            if at:
                grad_of(at - 1)
            if at == half:
                term_of(0)
        grad_of(joined - 1)
        term_of(half)

    total = sum_ref[...].T
    term_ref[...] = total
    for at, sent_ref in enumerate(sent_refs):
        size = sent_ref.shape[0]
        sent_ref[...] = total[at * size : (at + 1) * size].astype(BF16)


def cells(chunk, wvec, turned, ordered, aux, logm, before, pieces):
    rows, depth = wvec.shape
    width = chunk.shape[0]
    args = [chunk, wvec, turned, ordered, aux, logm]
    aliases = {}
    if before is not None:
        aliases = {len(args): 0}
        args.append(before)
    return pl.pallas_call(
        functools.partial(cells_kernel, before is not None, pieces),
        in_specs=[WHOLE] * len(args),
        out_specs=[WHOLE] * (2 + pieces),
        out_shape=[
            jax.ShapeDtypeStruct((rows, depth), F32),
            jax.ShapeDtypeStruct((width, depth), F32),
        ]
        + [jax.ShapeDtypeStruct((width // pieces, depth), BF16) for _ in range(pieces)],
        scratch_shapes=[
            pltpu.VMEM((depth, width), BF16),
            pltpu.VMEM((rows // 2, width), BF16),
            pltpu.VMEM((depth, width), F32),
        ],
        input_output_aliases=aliases,
        compiler_params=params(24),
        cost_estimate=cost(rows * width, rows * depth),
        name="cells",
    )(*args)


def put_kernel(offsets, exact, scalars, perm_ref, grad_ref, out_ref):
    grad = grad_ref[...]
    rows, width = grad.shape
    high = grad.astype(BF16)
    moving = high
    if exact:
        moving = jnp.concatenate([high, (grad - high.astype(F32)).astype(BF16)], axis=1)
    side = out_ref.shape[1]
    index = jnp.broadcast_to((perm_ref[...] - scalars[ROW_AT] * rows).astype(F32), (8, rows))[:1]
    vocab = lax.broadcasted_iota(jnp.int32, (side, rows), 0)
    for at, offset in enumerate(offsets):
        base = jnp.bitwise_xor(scalars[COL_AT], offset) * side
        pick = onehot(index == (vocab + base).astype(F32))
        moved = jnp.dot(pick, moving, preferred_element_type=F32)
        if exact:
            moved = moved[:, :width] + moved[:, width:]
        out_ref[at] = moved.astype(out_ref.dtype)


def put_rows(scalars, row_perm, grad, offsets, side, exact):
    width = grad.shape[1]
    return pl.pallas_call(
        functools.partial(put_kernel, offsets, exact),
        in_specs=[SCALARS, WHOLE, WHOLE],
        out_specs=WHOLE,
        out_shape=jax.ShapeDtypeStruct((len(offsets), side, width), F32 if exact else BF16),
        compiler_params=params(24),
        cost_estimate=cost((4096 if exact else 1) * grad.size, grad.size),
        name="put_rows",
    )(scalars, row_perm[None, :], grad)


def swap(value, axis, bit):
    pairs = [(at, at ^ bit) for at in range(lax.axis_size(axis))]
    return lax.ppermute(value, axis, pairs)


def together(values):
    return lax.optimization_barrier(values)


def line_shards(counts, block_mask, row_perm, col_perm, row_logm, col_logm, row_emb, col_emb):
    shard_rows, shard_cols = counts.shape
    side = row_emb.shape[0]
    width = col_emb.shape[0]
    scalars = jnp.stack([lax.axis_index("row"), lax.axis_index("col")]).astype(jnp.int32)

    cross = swap(col_emb, "row", 2)
    near = swap(col_emb, "row", 1)
    count_far, aux_far, shifted, columns, values = order_first(
        scalars, col_perm, block_mask, col_logm, counts, (3,), width
    )
    ordered = functools.partial(order_next, scalars)
    row_block, shifted = together((row_emb, shifted))
    from_x = swap(row_block, "col", 2)
    from_y = swap(row_block, "col", 4)
    from_xy = swap(row_block, "col", 6)
    count_cross, count_near, aux_cross, aux_near = ordered(shifted, columns, values, (2, 1), width)
    cross, near, from_x, from_y, from_xy, count_near, shifted = together(
        (cross, near, from_x, from_y, from_xy, count_near, shifted)
    )
    far = swap(cross, "row", 1)
    from_core = swap(jnp.stack([row_emb, from_x, from_y, from_xy]), "col", 1)
    count_own, aux_own = ordered(shifted, columns, values, (0,), width)
    count_own, row_perm = together((count_own, row_perm))
    blocks = [row_emb, from_x, from_y, from_xy, from_core]
    wvec, turned, logm = take_rows(scalars, row_perm, row_logm, blocks)

    grad, _, sent_0, sent_1 = cells(far, wvec, turned, count_far, aux_far, logm, None, 2)
    far_0 = swap(sent_0, "row", 1)
    far_1 = swap(sent_1, "row", 1)
    grad, term_cross = cells(cross, wvec, turned, count_cross, aux_cross, logm, grad, 0)
    grad, far_0 = together((grad, far_0))

    half = width // 2
    sum_0 = (term_cross[:half] + far_0.astype(F32)).astype(BF16)
    cross_0 = swap(sum_0, "row", 2)
    grad, sum_0 = together((grad, sum_0))
    grad, _, sent_near = cells(near, wvec, turned, count_near, aux_near, logm, grad, 1)
    got_near = swap(sent_near, "row", 1)
    grad, term_own = cells(col_emb, wvec, turned, count_own, aux_own, logm, grad, 0)
    grad, far_1, cross_0 = together((grad, far_1, cross_0))
    sum_1 = (term_cross[half:] + far_1.astype(F32)).astype(BF16)
    cross_1 = swap(sum_1, "row", 2)
    grad, sum_1 = together((grad, sum_1))
    away = put_rows(scalars, row_perm, grad, (1, 3, 5, 7), side, False)
    core = swap(away, "col", 1)
    grad, away = together((grad, away))
    home = put_rows(scalars, row_perm, grad, (0, 2, 4, 6), side, True)
    both = home + core.astype(F32)
    got_x = swap(both[1].astype(BF16), "col", 2)
    got_y = swap(both[2].astype(BF16), "col", 4)
    got_xy = swap(both[3].astype(BF16), "col", 6)
    row_sum = both[0] + got_x.astype(F32) + got_y.astype(F32) + got_xy.astype(F32)
    got_cross = jnp.concatenate([cross_0, cross_1]).astype(F32)
    col_sum = term_own + got_near.astype(F32) + got_cross
    row_scale = np.float32(1.0 / np.sqrt(shard_cols * 8))
    col_scale = np.float32(1.0 / np.sqrt(shard_rows * 4))
    return (row_sum * row_scale, col_sum * col_scale)


def solution(mesh):
    in_specs = (
        P("row", "col"),
        P("row", "col"),
        P("row"),
        P("col"),
        P("row"),
        P("col"),
        P(("row", "col"), None),
        P(("col", "row"), None),
    )
    out_specs = (P(("row", "col"), None), P(("col", "row"), None))
    line = mesh.shape["row"] == 4 and mesh.shape["col"] == 8
    body = line_shards if line else plain_shards
    return jax.shard_map(body, mesh=mesh, in_specs=in_specs, out_specs=out_specs, check_vma=False)
```

```python
import functools

import jax
import jax.numpy as jnp
import numpy as np
from jax import lax
from jax.experimental import pallas as pl
from jax.experimental.pallas import tpu as pltpu
from jax.sharding import PartitionSpec as P

F32 = jnp.float32
BF16 = jnp.bfloat16
LANES = 128
MIB = 1 << 20


def cell_delta(score, count, active, row_part, col_part):
    real_count = count.astype(F32)
    safe = jnp.maximum(real_count, 1.0)
    pmi = jnp.log(safe) - row_part[:, None] - col_part[None, :]
    confid = 0.1 + 0.25 * jnp.sqrt(safe)
    positive = confid * (score - pmi)
    zeroed = jax.nn.sigmoid(score - pmi)
    deriv = jnp.where(count > 0, positive, zeroed)
    return (active.astype(F32) * deriv).astype(BF16)


def plain_shards(counts, block_mask, row_perm, col_perm, row_logm, col_logm, row_emb, col_emb):
    shard_rows, shard_cols = counts.shape
    all_cols = shard_cols * lax.axis_size("col")
    all_rows = shard_rows * lax.axis_size("row")
    block_side = shard_rows // block_mask.shape[0]
    row_group = lax.all_gather(row_emb, "col", axis=0, tiled=True)
    col_group = lax.all_gather(col_emb, "row", axis=0, tiled=True)
    row_local = row_perm - lax.axis_index("row") * shard_rows
    col_local = col_perm - lax.axis_index("col") * shard_cols
    wvec = jnp.take(row_group, row_local, axis=0)
    cvec = jnp.take(col_group, col_local, axis=0)
    score = lax.dot_general(wvec, cvec, (((1,), (1,)), ((), ())), preferred_element_type=F32)
    active = jnp.repeat(jnp.repeat(block_mask, block_side, axis=0), block_side, axis=1)
    delta = cell_delta(score, counts, active, row_logm, col_logm)
    gshard = jnp.dot(delta, cvec, preferred_element_type=F32) / jnp.sqrt(F32(all_cols))
    ordered = jnp.zeros(gshard.shape, F32).at[row_local].set(gshard)
    row_grad = lax.psum_scatter(ordered, "col", scatter_dimension=0, tiled=True)
    hshard = lax.dot_general(
        delta, wvec, (((0,), (0,)), ((), ())), preferred_element_type=F32
    ) / jnp.sqrt(F32(all_rows))
    col_ordered = jnp.zeros(hshard.shape, F32).at[col_local].set(hshard)
    col_grad = lax.psum_scatter(col_ordered, "row", scatter_dimension=0, tiled=True)
    return (row_grad, col_grad)


ROW_AT, COL_AT = 0, 1

WHOLE = pl.BlockSpec(memory_space=pltpu.VMEM)
SCALARS = pl.BlockSpec(memory_space=pltpu.SMEM)


def params(mib):
    return pltpu.CompilerParams(vmem_limit_bytes=mib * MIB)


def cost(flops, moved):
    return pl.CostEstimate(flops=flops, bytes_accessed=moved, transcendentals=0)


def onehot(flag):
    return jnp.where(flag, 1.0, 0.0).astype(BF16)


def pieces_of(value):
    high = value.astype(BF16)
    rest = value - high.astype(F32)
    middle = rest.astype(BF16)
    low = (rest - middle.astype(F32)).astype(BF16)
    return high, middle, low


def along_sublanes(value):
    fill = jnp.zeros((LANES - value.shape[0], LANES), F32)
    return jnp.concatenate([value, fill], axis=0).T


def copies(pairs, sems):
    made = [pltpu.make_async_copy(src, dst, sems.at[at]) for at, (src, dst) in enumerate(pairs)]
    for copy in made:
        copy.start()
    return made


def fill_pick(pick, columns, base, groups):
    vocab = (lax.broadcasted_iota(jnp.int32, (LANES, pick.shape[1]), 1) + base).astype(F32)
    for group in groups:
        pick[pl.ds(group * LANES, LANES), :] = onehot(columns[:, group : group + 1] == vocab)


def chunk_base(scalars, offset, width):
    return jnp.bitwise_xor(scalars[ROW_AT], offset) * width


def move_values(values, pick, aux_ref):
    moved = jnp.dot(values, pick[...], preferred_element_type=F32)
    rows = values.shape[0] - 24
    aux_ref[pl.ds(0, rows), :] = moved[:rows]
    aux_ref[pl.ds(rows, 8), :] = moved[rows : rows + 8] + moved[rows + 8 : rows + 16] + moved[rows + 16 :]


def order_first_kernel(offsets, scalars, perm_hbm, mask_hbm, logm_hbm, count_hbm, *refs):
    parts = len(offsets)
    outs, auxes, refs = refs[:parts], refs[parts : 2 * parts], refs[2 * parts :]
    shifted_ref, columns_ref, values_ref, perm, mask_ref, logm_ref, tiles, pick, sems, tile_sems = refs
    depth = pick.shape[1]
    width = pick.shape[2]
    rows = outs[0].shape[0]
    step = tiles.shape[1]
    steps = rows // step

    slots = tiles.shape[0]

    def tile_copy(at):
        slot = lax.rem(at, slots)
        return pltpu.make_async_copy(
            count_hbm.at[pl.ds(pl.multiple_of(at * step, step), step)], tiles.at[slot], tile_sems.at[slot]
        )

    small = copies([(perm_hbm, perm), (mask_hbm, mask_ref), (logm_hbm, logm_ref)], sems)
    for at in range(slots):
        tile_copy(at).start()
    for copy in small:
        copy.wait()
    columns = along_sublanes((perm[...] - scalars[COL_AT] * depth).astype(F32))
    columns_ref[...] = columns
    blocks_r, blocks_c = mask_ref.shape
    mask = mask_ref[...].astype(F32)
    side = (blocks_r, depth // blocks_c)
    active = jnp.concatenate(
        [jnp.broadcast_to(mask[:, at : at + 1], side) for at in range(blocks_c)], axis=1
    )
    logm = jnp.broadcast_to(logm_ref[...], (8, depth))
    values = jnp.concatenate([active, *[piece.astype(F32) for piece in pieces_of(logm)]], axis=0)
    values_ref[...] = values
    values = values.astype(BF16)
    for part, offset in enumerate(offsets):
        fill_pick(pick.at[part], columns, chunk_base(scalars, offset, width), range(depth // LANES))
        move_values(values, pick.at[part], auxes[part])

    @pl.loop(0, steps)
    def _(at):
        here = pl.ds(pl.multiple_of(at * step, step), step)
        tile_copy(at).wait()
        shifted = (tiles[lax.rem(at, slots)] - 256).astype(F32).astype(BF16)
        shifted_ref[here, :] = shifted

        @pl.when(at + slots < steps)
        def _():
            tile_copy(at + slots).start()

        for part in range(parts):
            moved = jnp.dot(shifted, pick[part], preferred_element_type=F32)
            outs[part][here, :] = moved.astype(BF16)


def in_hbm(value):
    return pltpu.with_memory_space_constraint(value, pltpu.HBM)


def order_first(scalars, col_perm, block_mask, col_logm, counts, offsets, width):
    rows, cols = counts.shape
    parts = len(offsets)
    blocks = block_mask.shape[0]
    outside = pl.BlockSpec(memory_space=pltpu.HBM)
    step = 512
    return pl.pallas_call(
        functools.partial(order_first_kernel, offsets),
        in_specs=[SCALARS] + [outside] * 4,
        out_specs=[WHOLE] * (2 * parts + 3),
        out_shape=[jax.ShapeDtypeStruct((rows, width), BF16)] * parts
        + [jax.ShapeDtypeStruct((blocks + 8, width), F32)] * parts
        + [
            jax.ShapeDtypeStruct((rows, cols), BF16),
            jax.ShapeDtypeStruct((LANES, LANES), F32),
            jax.ShapeDtypeStruct((blocks + 24, cols), F32),
        ],
        scratch_shapes=[
            pltpu.VMEM((cols // LANES, LANES), jnp.int32),
            pltpu.VMEM(block_mask.shape, jnp.int32),
            pltpu.VMEM((1, cols), F32),
            pltpu.VMEM((2, step, cols), jnp.int32),
            pltpu.VMEM((parts, cols, width), BF16),
            pltpu.SemaphoreType.DMA((3,)),
            pltpu.SemaphoreType.DMA((2,)),
        ],
        compiler_params=params(28),
        cost_estimate=cost(2 * parts * rows * cols * width, 4 * rows * cols),
        name="order_first",
    )(scalars, *[in_hbm(each) for each in (col_perm.reshape(-1, LANES), block_mask, col_logm[None, :], counts)])


def order_next_kernel(offsets, scalars, shifted_ref, columns_ref, values_ref, *refs):
    parts = len(offsets)
    outs, auxes, pick = refs[:parts], refs[parts : 2 * parts], refs[-1]
    depth, width = pick.shape[1:]
    values = values_ref[...].astype(BF16)
    for part, offset in enumerate(offsets):
        base = chunk_base(scalars, offset, width)
        fill_pick(pick.at[part], columns_ref[...], base, range(depth // LANES))
        move_values(values, pick.at[part], auxes[part])
    step = 512

    @pl.loop(0, shifted_ref.shape[0] // step)
    def _(at):
        here = pl.ds(pl.multiple_of(at * step, step), step)
        for part in range(parts):
            moved = jnp.dot(shifted_ref[here, :], pick[part], preferred_element_type=F32)
            outs[part][here, :] = moved.astype(BF16)


def order_next(scalars, shifted, columns, values, offsets, width):
    rows, cols = shifted.shape
    parts = len(offsets)
    return pl.pallas_call(
        functools.partial(order_next_kernel, offsets),
        in_specs=[SCALARS] + [WHOLE] * 3,
        out_specs=[WHOLE] * (2 * parts),
        out_shape=[jax.ShapeDtypeStruct((rows, width), BF16)] * parts
        + [jax.ShapeDtypeStruct((values.shape[0] - 16, width), F32)] * parts,
        scratch_shapes=[pltpu.VMEM((parts, cols, width), BF16)],
        compiler_params=params(24),
        cost_estimate=cost(rows * width, rows * width),
        name="order_next",
    )(scalars, shifted, columns, values)


def take_kernel(scalars, perm_ref, logm_ref, *refs):
    own, from_x, from_y, from_xy, from_core, out_ref, turned_ref, logm_out, group, pick = refs
    side = own.shape[0]
    mine = [own, from_x, from_y, from_xy]
    blocks = [(2 * at, mine[at]) for at in range(4)] + [(2 * at + 1, from_core.at[at]) for at in range(4)]
    for offset, block in blocks:
        first = pl.multiple_of(jnp.bitwise_xor(scalars[COL_AT], offset) * side, side)
        group[pl.ds(first, side), :] = block[...]
    rows = out_ref.shape[0]
    depth = group.shape[0]
    groups = rows // LANES
    index = (perm_ref[...] - scalars[ROW_AT] * rows).astype(F32)
    columns = along_sublanes(jnp.concatenate([index, logm_ref[...]], axis=0))
    step = pick.shape[1]
    vocab = lax.broadcasted_iota(jnp.int32, (LANES, depth), 1).astype(F32)
    for first in range(0, rows, step):
        slot = (first // step) % pick.shape[0]
        for inner in range(0, step, LANES):
            at = (first + inner) // LANES
            pick[slot, pl.ds(inner, LANES), :] = onehot(columns[:, at : at + 1] == vocab)
            logm_out[pl.ds(first + inner, LANES), :] = jnp.broadcast_to(
                columns[:, groups + at : groups + at + 1], (LANES, LANES)
            )
        taken = jnp.dot(pick[slot], group[...], preferred_element_type=F32).astype(BF16)
        out_ref[pl.ds(first, step), :] = taken
        turned_ref[:, pl.ds(first, step)] = taken.T


def take_rows(scalars, row_perm, row_logm, blocks):
    rows = row_perm.shape[0]
    side, width = blocks[0].shape
    return pl.pallas_call(
        take_kernel,
        in_specs=[SCALARS] + [WHOLE] * 7,
        out_specs=[WHOLE] * 3,
        out_shape=[
            jax.ShapeDtypeStruct((rows, width), BF16),
            jax.ShapeDtypeStruct((width, rows), BF16),
            jax.ShapeDtypeStruct((rows, LANES), F32),
        ],
        scratch_shapes=[pltpu.VMEM((8 * side, width), BF16), pltpu.VMEM((2, 512, 8 * side), BF16)],
        compiler_params=params(24),
        cost_estimate=cost(2 * rows * rows * width, 4 * rows * width),
        name="take_rows",
    )(scalars, row_perm.reshape(-1, LANES), row_logm.reshape(-1, LANES), *blocks)


def chunk_work(
    chunk, wvec_ref, turned_ref, count_ref, aux_ref, logm_ref, before_ref, grad_ref, term_ref, chunk_turned, delta_ref
):
    chunk_turned[...] = chunk[...].T
    rows = wvec_ref.shape[0]
    width = chunk.shape[0]
    blocks = aux_ref.shape[0] - 8
    tile = rows // blocks
    joined = delta_ref.shape[0] // tile
    half = joined // 2
    col_logm = aux_ref[blocks : blocks + 1, :]
    term_ref[...] = jnp.zeros_like(term_ref)

    @pl.loop(0, blocks // joined)
    def _(group):
        def rows_at(at, count=1):
            return pl.ds(pl.multiple_of((group * joined + at) * tile, tile), count * tile)

        def held(at, count=1):
            return delta_ref[pl.ds(at * tile, count * tile), :]

        def score_of(at):
            return jnp.dot(wvec_ref[rows_at(at), :], chunk_turned[...], preferred_element_type=F32)

        def delta_of(at, score):
            here = rows_at(at)
            count = count_ref[here, :].astype(F32) + 256.0
            log = jnp.log(jnp.maximum(count, 1.0))
            row_logm = jnp.concatenate([logm_ref[here, :]] * (width // LANES), axis=1)
            gap = score + ((row_logm + col_logm) - log)
            confid = 0.1 + 0.25 * jnp.exp2(log * np.float32(0.5 / np.log(2.0)))
            zeroed = 0.5 * jnp.tanh(0.5 * gap) + 0.5
            deriv = jnp.where(count > 0.0, confid * gap, zeroed)
            active = aux_ref[pl.ds(group * joined + at, 1), :]
            delta_ref[pl.ds(at * tile, tile), :] = (deriv * active).astype(BF16)

        def grad_of(at):
            grad = jnp.dot(held(at), chunk[...], preferred_element_type=F32)
            if before_ref is not None:
                grad = grad + before_ref[rows_at(at), :]
            grad_ref[rows_at(at), :] = grad

        def term_of(at):
            turned = turned_ref[:, rows_at(at, half)]
            term_ref[...] += jnp.dot(turned, held(at, half), preferred_element_type=F32)

        ahead = score_of(0)
        for at in range(joined):
            score = ahead
            if at + 1 < joined:
                ahead = score_of(at + 1)
            delta_of(at, score)
            if at:
                grad_of(at - 1)
            if at == half:
                term_of(0)
        grad_of(joined - 1)
        term_of(half)


def cells_kernel(has_sum, sends, *refs):
    chunks = len(sends)
    wvec_ref, turned_ref, logm_ref, refs = *refs[:3], refs[3:]
    chunk_refs, count_refs, aux_refs = refs[:chunks], refs[chunks : 2 * chunks], refs[2 * chunks : 3 * chunks]
    refs = refs[3 * chunks :]
    before_ref = None
    if has_sum:
        before_ref, refs = refs[0], refs[1:]
    grad_ref, refs = refs[0], refs[1:]
    chunk_turned, delta_ref, sum_ref = refs[-3:]
    for at, pieces in enumerate(sends):
        term_ref = sum_ref
        if not pieces:
            term_ref, refs = refs[0], refs[1:]
        chunk_work(
            chunk_refs[at], wvec_ref, turned_ref, count_refs[at], aux_refs[at], logm_ref,
            before_ref, grad_ref, term_ref, chunk_turned, delta_ref,
        )
        before_ref = grad_ref
        for piece in range(pieces):
            sent_ref, refs = refs[0], refs[1:]
            size = sent_ref.shape[0]
            sent_ref[...] = term_ref[pl.ds(piece * size, size), :].astype(BF16)


def cells(rows_in, chunks, before, sends):
    wvec = rows_in[0]
    rows, depth = wvec.shape
    width = chunks[0][0].shape[0]
    args = [*rows_in, *[each for kind in zip(*chunks) for each in kind]]
    aliases = {}
    if before is not None:
        aliases = {len(args): 0}
        args.append(before)
    out_shape = [jax.ShapeDtypeStruct((rows, depth), F32)]
    for pieces in sends:
        if pieces:
            out_shape += [jax.ShapeDtypeStruct((depth // pieces, width), BF16) for _ in range(pieces)]
        else:
            out_shape.append(jax.ShapeDtypeStruct((depth, width), F32))
    return pl.pallas_call(
        functools.partial(cells_kernel, before is not None, sends),
        in_specs=[WHOLE] * len(args),
        out_specs=[WHOLE] * len(out_shape),
        out_shape=out_shape,
        scratch_shapes=[
            pltpu.VMEM((depth, width), BF16),
            pltpu.VMEM((rows // 2, width), BF16),
            pltpu.VMEM((depth, width), F32),
        ],
        input_output_aliases=aliases,
        compiler_params=params(24),
        cost_estimate=cost(rows * width, rows * depth),
        name="cells",
    )(*args)


def finish_kernel(scale, *refs):
    own_ref, near_ref, cross_refs, out_ref = refs[0], refs[1], refs[2:-1], refs[-1]
    size = cross_refs[0].shape[0]
    for at, cross_ref in enumerate(cross_refs):
        here = pl.ds(at * size, size)
        total = own_ref[here, :] + near_ref[here, :].astype(F32) + cross_ref[...].astype(F32)
        out_ref[:, here] = (total * scale).T


def finish(scale, own, near, *crosses):
    return pl.pallas_call(
        functools.partial(finish_kernel, scale),
        in_specs=[WHOLE] * (2 + len(crosses)),
        out_specs=WHOLE,
        out_shape=jax.ShapeDtypeStruct(own.shape[::-1], F32),
        compiler_params=params(8),
        cost_estimate=cost(own.size, own.size // 16),
        name="finish",
    )(own, near, *crosses)


def put_kernel(offsets, exact, scalars, perm_ref, grad_ref, out_ref):
    grad = grad_ref[...]
    rows, width = grad.shape
    high = grad.astype(BF16)
    moving = high
    if exact:
        moving = jnp.concatenate([high, (grad - high.astype(F32)).astype(BF16)], axis=1)
    side = out_ref.shape[1]
    index = jnp.broadcast_to((perm_ref[...] - scalars[ROW_AT] * rows).astype(F32), (8, rows))[:1]
    vocab = lax.broadcasted_iota(jnp.int32, (side, rows), 0)
    for at, offset in enumerate(offsets):
        base = jnp.bitwise_xor(scalars[COL_AT], offset) * side
        pick = onehot(index == (vocab + base).astype(F32))
        moved = jnp.dot(pick, moving, preferred_element_type=F32)
        if exact:
            moved = moved[:, :width] + moved[:, width:]
        out_ref[at] = moved.astype(out_ref.dtype)


def put_rows(scalars, row_perm, grad, offsets, side, exact):
    width = grad.shape[1]
    return pl.pallas_call(
        functools.partial(put_kernel, offsets, exact),
        in_specs=[SCALARS, WHOLE, WHOLE],
        out_specs=WHOLE,
        out_shape=jax.ShapeDtypeStruct((len(offsets), side, width), F32 if exact else BF16),
        compiler_params=params(24),
        cost_estimate=cost((4096 if exact and len(offsets) > 1 else 1) * grad.size, grad.size // 16),
        name="put_rows",
    )(scalars, row_perm[None, :], grad)


def swap(value, axis, bit):
    pairs = [(at, at ^ bit) for at in range(lax.axis_size(axis))]
    return lax.ppermute(value, axis, pairs)


def together(values):
    return lax.optimization_barrier(values)


def line_shards(counts, block_mask, row_perm, col_perm, row_logm, col_logm, row_emb, col_emb):
    shard_rows, shard_cols = counts.shape
    side = row_emb.shape[0]
    width = col_emb.shape[0]
    scalars = jnp.stack([lax.axis_index("row"), lax.axis_index("col")]).astype(jnp.int32)

    cross = swap(col_emb, "row", 2)
    near = swap(col_emb, "row", 1)
    count_far, aux_far, shifted, columns, values = order_first(
        scalars, col_perm, block_mask, col_logm, counts, (3,), width
    )
    ordered = functools.partial(order_next, scalars)
    row_block, shifted = together((row_emb, shifted))
    from_x = swap(row_block, "col", 2)
    from_y = swap(row_block, "col", 4)
    from_xy = swap(row_block, "col", 6)
    count_cross, count_near, aux_cross, aux_near = ordered(shifted, columns, values, (2, 1), width)
    cross, near, from_x, from_y, from_xy, count_near, shifted = together(
        (cross, near, from_x, from_y, from_xy, count_near, shifted)
    )
    far = swap(cross, "row", 1)
    from_core = swap(jnp.stack([row_emb, from_x, from_y, from_xy]), "col", 1)
    count_own, aux_own = ordered(shifted, columns, values, (0,), width)
    count_own, row_perm = together((count_own, row_perm))
    blocks = [row_emb, from_x, from_y, from_xy, from_core]
    wvec, turned, logm = take_rows(scalars, row_perm, row_logm, blocks)

    rows_in = (wvec, turned, logm)
    of_far, of_cross = (far, count_far, aux_far), (cross, count_cross, aux_cross)
    of_near, of_own = (near, count_near, aux_near), (col_emb, count_own, aux_own)
    grad, sent_0, sent_1 = cells(rows_in, [of_far], None, (2,))
    far_0 = swap(sent_0, "row", 1)
    far_1 = swap(sent_1, "row", 1)
    grad, term_cross = cells(rows_in, [of_cross], grad, (0,))
    grad, far_0 = together((grad, far_0))

    half = term_cross.shape[0] // 2
    sum_0 = (term_cross[:half] + far_0.astype(F32)).astype(BF16)
    cross_0 = swap(sum_0, "row", 2)
    grad, sum_0 = together((grad, sum_0))
    grad, sent_near, term_own = cells(rows_in, [of_near, of_own], grad, (1, 0))
    got_near = swap(sent_near, "row", 1)
    grad, far_1, cross_0 = together((grad, far_1, cross_0))
    sum_1 = (term_cross[half:] + far_1.astype(F32)).astype(BF16)
    cross_1 = swap(sum_1, "row", 2)
    grad, sum_1 = together((grad, sum_1))

    ordered = functools.partial(put_rows, scalars, row_perm)
    away = ordered(grad, (1, 3, 5, 7), side, False)
    core = swap(away, "col", 1)
    grad, away = together((grad, away))
    both = ordered(grad, (2, 4, 6), side, True) + core[1:].astype(F32)
    sends = [both[at].astype(BF16) for at in range(3)]
    got = [swap(sent, "col", bit) for sent, bit in zip(sends, (2, 4, 6))]
    grad, sends = together((grad, sends))
    home = ordered(grad, (0,), side, True)
    home, term_own = together((home, term_own))
    row_sum = home[0] + core[0].astype(F32)
    for each in got:
        row_sum = row_sum + each.astype(F32)
    row_scale = np.float32(1.0 / np.sqrt(shard_cols * 8))
    col_scale = np.float32(1.0 / np.sqrt(shard_rows * 4))
    return (row_sum * row_scale, finish(col_scale, term_own, got_near, cross_0, cross_1))


def solution(mesh):
    in_specs = (
        P("row", "col"),
        P("row", "col"),
        P("row"),
        P("col"),
        P("row"),
        P("col"),
        P(("row", "col"), None),
        P(("col", "row"), None),
    )
    out_specs = (P(("row", "col"), None), P(("col", "row"), None))
    line = mesh.shape["row"] == 4 and mesh.shape["col"] == 8
    body = line_shards if line else plain_shards
    return jax.shard_map(body, mesh=mesh, in_specs=in_specs, out_specs=out_specs, check_vma=False)
```

```python
import functools

import jax
import jax.numpy as jnp
import numpy as np
from jax import lax
from jax.experimental import pallas as pl
from jax.experimental.pallas import tpu as pltpu
from jax.sharding import PartitionSpec as P

F32 = jnp.float32
BF16 = jnp.bfloat16
LANES = 128
MIB = 1 << 20


def cell_delta(score, count, active, row_part, col_part):
    real_count = count.astype(F32)
    safe = jnp.maximum(real_count, 1.0)
    pmi = jnp.log(safe) - row_part[:, None] - col_part[None, :]
    confid = 0.1 + 0.25 * jnp.sqrt(safe)
    positive = confid * (score - pmi)
    zeroed = jax.nn.sigmoid(score - pmi)
    deriv = jnp.where(count > 0, positive, zeroed)
    return (active.astype(F32) * deriv).astype(BF16)


def plain_shards(counts, block_mask, row_perm, col_perm, row_logm, col_logm, row_emb, col_emb):
    shard_rows, shard_cols = counts.shape
    all_cols = shard_cols * lax.axis_size("col")
    all_rows = shard_rows * lax.axis_size("row")
    block_side = shard_rows // block_mask.shape[0]
    row_group = lax.all_gather(row_emb, "col", axis=0, tiled=True)
    col_group = lax.all_gather(col_emb, "row", axis=0, tiled=True)
    row_local = row_perm - lax.axis_index("row") * shard_rows
    col_local = col_perm - lax.axis_index("col") * shard_cols
    wvec = jnp.take(row_group, row_local, axis=0)
    cvec = jnp.take(col_group, col_local, axis=0)
    score = lax.dot_general(wvec, cvec, (((1,), (1,)), ((), ())), preferred_element_type=F32)
    active = jnp.repeat(jnp.repeat(block_mask, block_side, axis=0), block_side, axis=1)
    delta = cell_delta(score, counts, active, row_logm, col_logm)
    gshard = jnp.dot(delta, cvec, preferred_element_type=F32) / jnp.sqrt(F32(all_cols))
    ordered = jnp.zeros(gshard.shape, F32).at[row_local].set(gshard)
    row_grad = lax.psum_scatter(ordered, "col", scatter_dimension=0, tiled=True)
    hshard = lax.dot_general(
        delta, wvec, (((0,), (0,)), ((), ())), preferred_element_type=F32
    ) / jnp.sqrt(F32(all_rows))
    col_ordered = jnp.zeros(hshard.shape, F32).at[col_local].set(hshard)
    col_grad = lax.psum_scatter(col_ordered, "row", scatter_dimension=0, tiled=True)
    return (row_grad, col_grad)


ROW_AT, COL_AT = 0, 1

WHOLE = pl.BlockSpec(memory_space=pltpu.VMEM)
SCALARS = pl.BlockSpec(memory_space=pltpu.SMEM)


def params(mib):
    return pltpu.CompilerParams(vmem_limit_bytes=mib * MIB)


def cost(flops, moved):
    return pl.CostEstimate(flops=flops, bytes_accessed=moved, transcendentals=0)


def onehot(flag):
    return jnp.where(flag, 1.0, 0.0).astype(BF16)


def pieces_of(value):
    high = value.astype(BF16)
    rest = value - high.astype(F32)
    middle = rest.astype(BF16)
    low = (rest - middle.astype(F32)).astype(BF16)
    return high, middle, low


def along_sublanes(value):
    fill = jnp.zeros((LANES - value.shape[0], LANES), F32)
    return jnp.concatenate([value, fill], axis=0).T


def copies(pairs, sems):
    made = [pltpu.make_async_copy(src, dst, sems.at[at]) for at, (src, dst) in enumerate(pairs)]
    for copy in made:
        copy.start()
    return made


def fill_pick(pick, spread, base, first, count):
    width = pick.shape[1]
    vocab = (lax.broadcasted_iota(jnp.int32, (LANES, width), 1) + base).astype(F32)
    for at in range(0, count, LANES):
        here = pl.ds(pl.multiple_of(first + at, LANES), LANES)
        index = jnp.concatenate([spread[here, :]] * (width // LANES), axis=1)
        pick[here, :] = onehot(index == vocab)


def chunk_base(scalars, offset, width):
    return jnp.bitwise_xor(scalars[ROW_AT], offset) * width


def move_values(values, pick, aux_ref):
    moved = jnp.dot(values, pick[...], preferred_element_type=F32)
    rows = values.shape[0] - 24
    aux_ref[pl.ds(0, rows), :] = moved[:rows]
    aux_ref[pl.ds(rows, 8), :] = moved[rows : rows + 8] + moved[rows + 8 : rows + 16] + moved[rows + 16 :]


def order_first_kernel(offset, scalars, perm_hbm, mask_hbm, logm_hbm, count_hbm, *refs):
    out_ref, aux_ref, shifted_ref, spread_ref, values_ref, refs = *refs[:5], refs[5:]
    perm, mask_ref, logm_ref, tiles, held, pick, sems, tile_sems = refs
    depth, width = pick.shape
    rows = out_ref.shape[0]
    step = tiles.shape[1]
    pairs = rows // step // 2

    def tile_copy(at, slot):
        return pltpu.make_async_copy(
            count_hbm.at[pl.ds(pl.multiple_of(at * step, step), step)], tiles.at[slot], tile_sems.at[slot]
        )

    small = copies([(perm_hbm, perm), (mask_hbm, mask_ref), (logm_hbm, logm_ref)], sems)
    for slot in range(2):
        tile_copy(slot, slot).start()
    for copy in small:
        copy.wait()
    columns = along_sublanes((perm[...] - scalars[COL_AT] * depth).astype(F32))
    for group in range(depth // LANES):
        spread_ref[pl.ds(group * LANES, LANES), :] = jnp.broadcast_to(
            columns[:, group : group + 1], (LANES, LANES)
        )
    blocks_r, blocks_c = mask_ref.shape
    mask = mask_ref[...].astype(F32)
    side = (blocks_r, depth // blocks_c)
    active = jnp.concatenate(
        [jnp.broadcast_to(mask[:, at : at + 1], side) for at in range(blocks_c)], axis=1
    )
    logm = jnp.broadcast_to(logm_ref[...], (8, depth))
    values = jnp.concatenate([active, *[piece.astype(F32) for piece in pieces_of(logm)]], axis=0)
    values_ref[...] = values
    fill_pick(pick, spread_ref, chunk_base(scalars, offset, width), 0, depth)
    move_values(values.astype(BF16), pick, aux_ref)

    def shift(at, slot):
        tile_copy(at, slot).wait()
        shifted = (tiles[slot] - 256).astype(F32).astype(BF16)
        held[slot] = shifted
        shifted_ref[pl.ds(pl.multiple_of(at * step, step), step), :] = shifted

    def move(at, slot):
        moved = jnp.dot(held[slot], pick[...], preferred_element_type=F32)
        out_ref[pl.ds(pl.multiple_of(at * step, step), step), :] = moved.astype(BF16)

    @pl.loop(0, pairs)
    def _(pair):
        shift(2 * pair, 0)
        move(2 * pair, 0)
        shift(2 * pair + 1, 1)

        @pl.when(pair + 1 < pairs)
        def _():
            for slot in range(2):
                tile_copy(2 * pair + 2 + slot, slot).start()

        move(2 * pair + 1, 1)


def in_hbm(value):
    return pltpu.with_memory_space_constraint(value, pltpu.HBM)


def order_first(scalars, col_perm, block_mask, col_logm, counts, offset, width):
    rows, cols = counts.shape
    blocks = block_mask.shape[0]
    outside = pl.BlockSpec(memory_space=pltpu.HBM)
    step = 256
    return pl.pallas_call(
        functools.partial(order_first_kernel, offset),
        in_specs=[SCALARS] + [outside] * 4,
        out_specs=[WHOLE] * 5,
        out_shape=[
            jax.ShapeDtypeStruct((rows, width), BF16),
            jax.ShapeDtypeStruct((blocks + 8, width), F32),
            jax.ShapeDtypeStruct((rows, cols), BF16),
            jax.ShapeDtypeStruct((cols, LANES), F32),
            jax.ShapeDtypeStruct((blocks + 24, cols), F32),
        ],
        scratch_shapes=[
            pltpu.VMEM((cols // LANES, LANES), jnp.int32),
            pltpu.VMEM(block_mask.shape, jnp.int32),
            pltpu.VMEM((1, cols), F32),
            pltpu.VMEM((2, step, cols), jnp.int32),
            pltpu.VMEM((2, step, cols), BF16),
            pltpu.VMEM((cols, width), BF16),
            pltpu.SemaphoreType.DMA((3,)),
            pltpu.SemaphoreType.DMA((2,)),
        ],
        compiler_params=params(24),
        cost_estimate=cost(2 * rows * cols * width, 4 * rows * cols),
        name="order_first",
    )(scalars, *[in_hbm(each) for each in (col_perm.reshape(-1, LANES), block_mask, col_logm[None, :], counts)])


def order_next_kernel(offsets, scalars, shifted_ref, spread_ref, values_ref, *refs):
    parts = len(offsets)
    outs, auxes, picks = refs[:parts], refs[parts : 2 * parts], refs[2 * parts :]
    depth, width = picks[0].shape
    bases = [chunk_base(scalars, offset, width) for offset in offsets]
    values = values_ref[...].astype(BF16)
    step = 512
    steps = shifted_ref.shape[0] // step
    fill_pick(picks[0], spread_ref, bases[0], 0, depth)
    for part in range(parts):
        move_values(values, picks[part], auxes[part])

        @pl.loop(0, steps)
        def _(at):
            here = pl.ds(pl.multiple_of(at * step, step), step)
            moved = jnp.dot(shifted_ref[here, :], picks[part][...], preferred_element_type=F32)
            outs[part][here, :] = moved.astype(BF16)
            if part + 1 < parts:
                fill_pick(picks[part + 1], spread_ref, bases[part + 1], at * (depth // steps), depth // steps)


def order_next(scalars, shifted, spread, values, offsets, width):
    rows, cols = shifted.shape
    parts = len(offsets)
    return pl.pallas_call(
        functools.partial(order_next_kernel, offsets),
        in_specs=[SCALARS] + [WHOLE] * 3,
        out_specs=[WHOLE] * (2 * parts),
        out_shape=[jax.ShapeDtypeStruct((rows, width), BF16)] * parts
        + [jax.ShapeDtypeStruct((values.shape[0] - 16, width), F32)] * parts,
        scratch_shapes=[pltpu.VMEM((cols, width), BF16)] * parts,
        compiler_params=params(24),
        cost_estimate=cost(rows * width, rows * width),
        name="order_next",
    )(scalars, shifted, spread, values)


def take_kernel(scalars, perm_ref, logm_ref, *refs):
    own, from_x, from_y, from_xy, from_core, out_ref, turned_ref, logm_out, group, pick = refs
    side = own.shape[0]
    mine = [own, from_x, from_y, from_xy]
    blocks = [(2 * at, mine[at]) for at in range(4)] + [(2 * at + 1, from_core.at[at]) for at in range(4)]
    for offset, block in blocks:
        first = pl.multiple_of(jnp.bitwise_xor(scalars[COL_AT], offset) * side, side)
        group[pl.ds(first, side), :] = block[...]
    rows = out_ref.shape[0]
    depth = group.shape[0]
    groups = rows // LANES
    index = (perm_ref[...] - scalars[ROW_AT] * rows).astype(F32)
    columns = along_sublanes(jnp.concatenate([index, logm_ref[...]], axis=0))
    step = pick.shape[1]
    vocab = lax.broadcasted_iota(jnp.int32, (LANES, depth), 1).astype(F32)
    for first in range(0, rows, step):
        slot = (first // step) % pick.shape[0]
        for inner in range(0, step, LANES):
            at = (first + inner) // LANES
            pick[slot, pl.ds(inner, LANES), :] = onehot(columns[:, at : at + 1] == vocab)
            logm_out[pl.ds(first + inner, LANES), :] = jnp.broadcast_to(
                columns[:, groups + at : groups + at + 1], (LANES, LANES)
            )
        taken = jnp.dot(pick[slot], group[...], preferred_element_type=F32).astype(BF16)
        out_ref[pl.ds(first, step), :] = taken
        turned_ref[:, pl.ds(first, step)] = taken.T


def take_rows(scalars, row_perm, row_logm, blocks):
    rows = row_perm.shape[0]
    side, width = blocks[0].shape
    return pl.pallas_call(
        take_kernel,
        in_specs=[SCALARS] + [WHOLE] * 7,
        out_specs=[WHOLE] * 3,
        out_shape=[
            jax.ShapeDtypeStruct((rows, width), BF16),
            jax.ShapeDtypeStruct((width, rows), BF16),
            jax.ShapeDtypeStruct((rows, LANES), F32),
        ],
        scratch_shapes=[pltpu.VMEM((8 * side, width), BF16), pltpu.VMEM((2, 512, 8 * side), BF16)],
        compiler_params=params(24),
        cost_estimate=cost(2 * rows * rows * width, 4 * rows * width),
        name="take_rows",
    )(scalars, row_perm.reshape(-1, LANES), row_logm.reshape(-1, LANES), *blocks)


def chunk_work(
    chunk, wvec_ref, turned_ref, count_ref, aux_ref, logm_ref, before_ref, grad_ref, term_ref, chunk_turned, delta_ref
):
    chunk_turned[...] = chunk[...].T
    rows = wvec_ref.shape[0]
    width = chunk.shape[0]
    blocks = aux_ref.shape[0] - 8
    tile = rows // blocks
    joined = delta_ref.shape[0] // tile
    half = joined // 2
    col_logm = aux_ref[blocks : blocks + 1, :]
    term_ref[...] = jnp.zeros_like(term_ref)

    @pl.loop(0, blocks // joined)
    def _(group):
        def rows_at(at, count=1):
            return pl.ds(pl.multiple_of((group * joined + at) * tile, tile), count * tile)

        def held(at, count=1):
            return delta_ref[pl.ds(at * tile, count * tile), :]

        def score_of(at):
            return jnp.dot(wvec_ref[rows_at(at), :], chunk_turned[...], preferred_element_type=F32)

        def delta_of(at, score):
            here = rows_at(at)
            count = count_ref[here, :].astype(F32) + 256.0
            log = jnp.log(jnp.maximum(count, 1.0))
            row_logm = jnp.concatenate([logm_ref[here, :]] * (width // LANES), axis=1)
            gap = score + ((row_logm + col_logm) - log)
            confid = 0.1 + 0.25 * jnp.exp2(log * np.float32(0.5 / np.log(2.0)))
            zeroed = 0.5 * jnp.tanh(0.5 * gap) + 0.5
            deriv = jnp.where(count > 0.0, confid * gap, zeroed)
            active = aux_ref[pl.ds(group * joined + at, 1), :]
            delta_ref[pl.ds(at * tile, tile), :] = (deriv * active).astype(BF16)

        def grad_of(at):
            grad = jnp.dot(held(at), chunk[...], preferred_element_type=F32)
            if before_ref is not None:
                grad = grad + before_ref[rows_at(at), :]
            grad_ref[rows_at(at), :] = grad

        def term_of(at):
            turned = turned_ref[:, rows_at(at, half)]
            term_ref[...] += jnp.dot(turned, held(at, half), preferred_element_type=F32)

        ahead = score_of(0)
        for at in range(joined):
            score = ahead
            if at + 1 < joined:
                ahead = score_of(at + 1)
            delta_of(at, score)
            if at:
                grad_of(at - 1)
            if at == half:
                term_of(0)
        grad_of(joined - 1)
        term_of(half)


def cells_kernel(has_sum, sends, *refs):
    chunks = len(sends)
    wvec_ref, turned_ref, logm_ref, refs = *refs[:3], refs[3:]
    chunk_refs, count_refs, aux_refs = refs[:chunks], refs[chunks : 2 * chunks], refs[2 * chunks : 3 * chunks]
    refs = refs[3 * chunks :]
    before_ref = None
    if has_sum:
        before_ref, refs = refs[0], refs[1:]
    grad_ref, refs = refs[0], refs[1:]
    chunk_turned, delta_ref, sum_ref = refs[-3:]
    for at, pieces in enumerate(sends):
        term_ref = sum_ref
        if not pieces:
            term_ref, refs = refs[0], refs[1:]
        chunk_work(
            chunk_refs[at], wvec_ref, turned_ref, count_refs[at], aux_refs[at], logm_ref,
            before_ref, grad_ref, term_ref, chunk_turned, delta_ref,
        )
        before_ref = grad_ref
        for piece in range(pieces):
            sent_ref, refs = refs[0], refs[1:]
            size = sent_ref.shape[0]
            sent_ref[...] = term_ref[pl.ds(piece * size, size), :].astype(BF16)


def cells(rows_in, chunks, before, sends):
    wvec = rows_in[0]
    rows, depth = wvec.shape
    width = chunks[0][0].shape[0]
    args = [*rows_in, *[each for kind in zip(*chunks) for each in kind]]
    aliases = {}
    if before is not None:
        aliases = {len(args): 0}
        args.append(before)
    out_shape = [jax.ShapeDtypeStruct((rows, depth), F32)]
    for pieces in sends:
        if pieces:
            out_shape += [jax.ShapeDtypeStruct((depth // pieces, width), BF16) for _ in range(pieces)]
        else:
            out_shape.append(jax.ShapeDtypeStruct((depth, width), F32))
    return pl.pallas_call(
        functools.partial(cells_kernel, before is not None, sends),
        in_specs=[WHOLE] * len(args),
        out_specs=[WHOLE] * len(out_shape),
        out_shape=out_shape,
        scratch_shapes=[
            pltpu.VMEM((depth, width), BF16),
            pltpu.VMEM((rows // 2, width), BF16),
            pltpu.VMEM((depth, width), F32),
        ],
        input_output_aliases=aliases,
        compiler_params=params(24),
        cost_estimate=cost(rows * width, rows * depth),
        name="cells",
    )(*args)


def finish_kernel(scale, *refs):
    own_ref, near_ref, cross_refs, out_ref = refs[0], refs[1], refs[2:-1], refs[-1]
    size = cross_refs[0].shape[0]
    for at, cross_ref in enumerate(cross_refs):
        here = pl.ds(at * size, size)
        total = own_ref[here, :] + near_ref[here, :].astype(F32) + cross_ref[...].astype(F32)
        out_ref[:, here] = (total * scale).T


def finish(scale, own, near, *crosses):
    return pl.pallas_call(
        functools.partial(finish_kernel, scale),
        in_specs=[WHOLE] * (2 + len(crosses)),
        out_specs=WHOLE,
        out_shape=jax.ShapeDtypeStruct(own.shape[::-1], F32),
        compiler_params=params(8),
        cost_estimate=cost(own.size, own.size // 16),
        name="finish",
    )(own, near, *crosses)


def put_kernel(offsets, exact, scalars, perm_ref, grad_ref, out_ref, pick):
    grad = grad_ref[...]
    rows, width = grad.shape
    high = grad.astype(BF16)
    moving = high
    if exact:
        moving = jnp.concatenate([high, (grad - high.astype(F32)).astype(BF16)], axis=1)
    side = out_ref.shape[1]
    index = jnp.broadcast_to((perm_ref[...] - scalars[ROW_AT] * rows).astype(F32), (8, rows))[:1]
    vocab = lax.broadcasted_iota(jnp.int32, (side, rows), 0)
    for at, offset in enumerate(offsets):
        base = jnp.bitwise_xor(scalars[COL_AT], offset) * side
        pick[pl.ds(at * side, side), :] = onehot(index == (vocab + base).astype(F32))
    moved = jnp.dot(pick[...], moving, preferred_element_type=F32)
    if exact:
        moved = moved[:, :width] + moved[:, width:]
    out_ref[...] = moved.astype(out_ref.dtype).reshape(out_ref.shape)


def put_rows(scalars, row_perm, grad, offsets, side, exact):
    width = grad.shape[1]
    return pl.pallas_call(
        functools.partial(put_kernel, offsets, exact),
        in_specs=[SCALARS, WHOLE, WHOLE],
        out_specs=WHOLE,
        out_shape=jax.ShapeDtypeStruct((len(offsets), side, width), F32 if exact else BF16),
        scratch_shapes=[pltpu.VMEM((len(offsets) * side, grad.shape[0]), BF16)],
        compiler_params=params(24),
        cost_estimate=cost((4096 if exact and len(offsets) > 1 else 1) * grad.size, grad.size // 16),
        name="put_rows",
    )(scalars, row_perm[None, :], grad)


def swap(value, axis, bit):
    pairs = [(at, at ^ bit) for at in range(lax.axis_size(axis))]
    return lax.ppermute(value, axis, pairs)


def together(values):
    return lax.optimization_barrier(values)


def line_shards(counts, block_mask, row_perm, col_perm, row_logm, col_logm, row_emb, col_emb):
    shard_rows, shard_cols = counts.shape
    side = row_emb.shape[0]
    width = col_emb.shape[0]
    scalars = jnp.stack([lax.axis_index("row"), lax.axis_index("col")]).astype(jnp.int32)

    cross = swap(col_emb, "row", 2)
    near = swap(col_emb, "row", 1)
    count_far, aux_far, shifted, spread, values = order_first(
        scalars, col_perm, block_mask, col_logm, counts, 3, width
    )
    ordered = functools.partial(order_next, scalars)
    row_block, shifted = together((row_emb, shifted))
    from_x = swap(row_block, "col", 2)
    from_y = swap(row_block, "col", 4)
    from_xy = swap(row_block, "col", 6)
    count_cross, count_near, aux_cross, aux_near = ordered(shifted, spread, values, (2, 1), width)
    cross, near, from_x, from_y, from_xy, count_near, shifted = together(
        (cross, near, from_x, from_y, from_xy, count_near, shifted)
    )
    far = swap(cross, "row", 1)
    from_core = swap(jnp.stack([row_emb, from_x, from_y, from_xy]), "col", 1)
    count_own, aux_own = ordered(shifted, spread, values, (0,), width)
    count_own, row_perm = together((count_own, row_perm))
    blocks = [row_emb, from_x, from_y, from_xy, from_core]
    wvec, turned, logm = take_rows(scalars, row_perm, row_logm, blocks)

    rows_in = (wvec, turned, logm)
    of_far, of_cross = (far, count_far, aux_far), (cross, count_cross, aux_cross)
    of_near, of_own = (near, count_near, aux_near), (col_emb, count_own, aux_own)
    grad, sent_0, sent_1 = cells(rows_in, [of_far], None, (2,))
    far_0 = swap(sent_0, "row", 1)
    far_1 = swap(sent_1, "row", 1)
    grad, term_cross = cells(rows_in, [of_cross], grad, (0,))
    grad, far_0 = together((grad, far_0))

    half = term_cross.shape[0] // 2
    sum_0 = (term_cross[:half] + far_0.astype(F32)).astype(BF16)
    cross_0 = swap(sum_0, "row", 2)
    grad, sum_0 = together((grad, sum_0))
    grad, sent_near, term_own = cells(rows_in, [of_near, of_own], grad, (1, 0))
    got_near = swap(sent_near, "row", 1)
    grad, far_1, cross_0 = together((grad, far_1, cross_0))
    sum_1 = (term_cross[half:] + far_1.astype(F32)).astype(BF16)
    cross_1 = swap(sum_1, "row", 2)
    grad, sum_1 = together((grad, sum_1))

    ordered = functools.partial(put_rows, scalars, row_perm)
    away = ordered(grad, (1, 3, 5, 7), side, False)
    core = swap(away, "col", 1)
    grad, away = together((grad, away))
    both = ordered(grad, (2, 4, 6), side, True) + core[1:].astype(F32)
    sends = [both[at].astype(BF16) for at in range(3)]
    got = [swap(sends[at], "col", bit) for at, bit in ((1, 4), (2, 6), (0, 2))]
    grad, sends = together((grad, sends))
    home = ordered(grad, (0,), side, True)
    home, term_own = together((home, term_own))
    row_sum = home[0] + core[0].astype(F32)
    for each in got:
        row_sum = row_sum + each.astype(F32)
    row_scale = np.float32(1.0 / np.sqrt(shard_cols * 8))
    col_scale = np.float32(1.0 / np.sqrt(shard_rows * 4))
    return (row_sum * row_scale, finish(col_scale, term_own, got_near, cross_0, cross_1))


def solution(mesh):
    in_specs = (
        P("row", "col"),
        P("row", "col"),
        P("row"),
        P("col"),
        P("row"),
        P("col"),
        P(("row", "col"), None),
        P(("col", "row"), None),
    )
    out_specs = (P(("row", "col"), None), P(("col", "row"), None))
    line = mesh.shape["row"] == 4 and mesh.shape["col"] == 8
    body = line_shards if line else plain_shards
    return jax.shard_map(body, mesh=mesh, in_specs=in_specs, out_specs=out_specs, check_vma=False)
```

```python
import functools

import jax
import jax.numpy as jnp
import numpy as np
from jax import lax
from jax.experimental import pallas as pl
from jax.experimental.pallas import tpu as pltpu
from jax.sharding import PartitionSpec as P

F32 = jnp.float32
BF16 = jnp.bfloat16
LANES = 128
MIB = 1 << 20


def cell_delta(score, count, active, row_part, col_part):
    real_count = count.astype(F32)
    safe = jnp.maximum(real_count, 1.0)
    pmi = jnp.log(safe) - row_part[:, None] - col_part[None, :]
    confid = 0.1 + 0.25 * jnp.sqrt(safe)
    positive = confid * (score - pmi)
    zeroed = jax.nn.sigmoid(score - pmi)
    deriv = jnp.where(count > 0, positive, zeroed)
    return (active.astype(F32) * deriv).astype(BF16)


def plain_shards(counts, block_mask, row_perm, col_perm, row_logm, col_logm, row_emb, col_emb):
    shard_rows, shard_cols = counts.shape
    all_cols = shard_cols * lax.axis_size("col")
    all_rows = shard_rows * lax.axis_size("row")
    block_side = shard_rows // block_mask.shape[0]
    row_group = lax.all_gather(row_emb, "col", axis=0, tiled=True)
    col_group = lax.all_gather(col_emb, "row", axis=0, tiled=True)
    row_local = row_perm - lax.axis_index("row") * shard_rows
    col_local = col_perm - lax.axis_index("col") * shard_cols
    wvec = jnp.take(row_group, row_local, axis=0)
    cvec = jnp.take(col_group, col_local, axis=0)
    score = lax.dot_general(wvec, cvec, (((1,), (1,)), ((), ())), preferred_element_type=F32)
    active = jnp.repeat(jnp.repeat(block_mask, block_side, axis=0), block_side, axis=1)
    delta = cell_delta(score, counts, active, row_logm, col_logm)
    gshard = jnp.dot(delta, cvec, preferred_element_type=F32) / jnp.sqrt(F32(all_cols))
    ordered = jnp.zeros(gshard.shape, F32).at[row_local].set(gshard)
    row_grad = lax.psum_scatter(ordered, "col", scatter_dimension=0, tiled=True)
    hshard = lax.dot_general(
        delta, wvec, (((0,), (0,)), ((), ())), preferred_element_type=F32
    ) / jnp.sqrt(F32(all_rows))
    col_ordered = jnp.zeros(hshard.shape, F32).at[col_local].set(hshard)
    col_grad = lax.psum_scatter(col_ordered, "row", scatter_dimension=0, tiled=True)
    return (row_grad, col_grad)


ROW_AT, COL_AT = 0, 1

WHOLE = pl.BlockSpec(memory_space=pltpu.VMEM)
SCALARS = pl.BlockSpec(memory_space=pltpu.SMEM)


def params(mib):
    return pltpu.CompilerParams(vmem_limit_bytes=mib * MIB)


def cost(flops, moved):
    return pl.CostEstimate(flops=flops, bytes_accessed=moved, transcendentals=0)


def onehot(flag):
    return jnp.where(flag, 1.0, 0.0).astype(BF16)


def pieces_of(value):
    high = value.astype(BF16)
    rest = value - high.astype(F32)
    middle = rest.astype(BF16)
    low = (rest - middle.astype(F32)).astype(BF16)
    return high, middle, low


def along_sublanes(value):
    fill = jnp.zeros((LANES - value.shape[0], LANES), F32)
    return jnp.concatenate([value, fill], axis=0).T


def copies(pairs, sems):
    made = [pltpu.make_async_copy(src, dst, sems.at[at]) for at, (src, dst) in enumerate(pairs)]
    for copy in made:
        copy.start()
    return made


def fill_pick(pick, columns, base, groups):
    vocab = (lax.broadcasted_iota(jnp.int32, (LANES, pick.shape[1]), 1) + base).astype(F32)
    for group in groups:
        pick[pl.ds(group * LANES, LANES), :] = onehot(columns[:, group : group + 1] == vocab)


def chunk_base(scalars, offset, width):
    return jnp.bitwise_xor(scalars[ROW_AT], offset) * width


def move_values(values, pick, aux_ref):
    moved = jnp.dot(values, pick[...], preferred_element_type=F32)
    rows = values.shape[0] - 24
    aux_ref[pl.ds(0, rows), :] = moved[:rows]
    aux_ref[pl.ds(rows, 8), :] = moved[rows : rows + 8] + moved[rows + 8 : rows + 16] + moved[rows + 16 :]


def order_first_kernel(offsets, scalars, perm_hbm, mask_hbm, logm_hbm, count_hbm, *refs):
    parts = len(offsets)
    outs, auxes, refs = refs[:parts], refs[parts : 2 * parts], refs[2 * parts :]
    shifted_ref, columns_ref, values_ref, perm, mask_ref, logm_ref, tiles, pick, sems, tile_sems = refs
    depth = pick.shape[1]
    width = pick.shape[2]
    rows = outs[0].shape[0]
    step = tiles.shape[1]
    steps = rows // step

    def tile_copy(at):
        return pltpu.make_async_copy(count_hbm.at[pl.ds(at * step, step)], tiles.at[at], tile_sems.at[at])

    small = copies([(perm_hbm, perm), (mask_hbm, mask_ref), (logm_hbm, logm_ref)], sems)
    for at in range(steps):
        tile_copy(at).start()
    for copy in small:
        copy.wait()
    columns = along_sublanes((perm[...] - scalars[COL_AT] * depth).astype(F32))
    columns_ref[...] = columns
    blocks_r, blocks_c = mask_ref.shape
    mask = mask_ref[...].astype(F32)
    side = (blocks_r, depth // blocks_c)
    active = jnp.concatenate(
        [jnp.broadcast_to(mask[:, at : at + 1], side) for at in range(blocks_c)], axis=1
    )
    logm = jnp.broadcast_to(logm_ref[...], (8, depth))
    values = jnp.concatenate([active, *[piece.astype(F32) for piece in pieces_of(logm)]], axis=0)
    values_ref[...] = values
    values = values.astype(BF16)
    for part, offset in enumerate(offsets):
        fill_pick(pick.at[part], columns, chunk_base(scalars, offset, width), range(depth // LANES))
        move_values(values, pick.at[part], auxes[part])

    def shift(at):
        tile_copy(at).wait()
        shifted_ref[pl.ds(at * step, step), :] = (tiles[at] - 256).astype(F32).astype(BF16)

    shift(0)
    for at in range(steps):
        if at + 1 < steps:
            shift(at + 1)
        here = pl.ds(at * step, step)
        for part in range(parts):
            moved = jnp.dot(shifted_ref[here, :], pick[part], preferred_element_type=F32)
            outs[part][here, :] = moved.astype(BF16)


def in_hbm(value):
    return pltpu.with_memory_space_constraint(value, pltpu.HBM)


def order_first(scalars, col_perm, block_mask, col_logm, counts, offsets, width):
    rows, cols = counts.shape
    parts = len(offsets)
    blocks = block_mask.shape[0]
    outside = pl.BlockSpec(memory_space=pltpu.HBM)
    step = 512
    return pl.pallas_call(
        functools.partial(order_first_kernel, offsets),
        in_specs=[SCALARS] + [outside] * 4,
        out_specs=[WHOLE] * (2 * parts + 3),
        out_shape=[jax.ShapeDtypeStruct((rows, width), BF16)] * parts
        + [jax.ShapeDtypeStruct((blocks + 8, width), F32)] * parts
        + [
            jax.ShapeDtypeStruct((rows, cols), BF16),
            jax.ShapeDtypeStruct((LANES, LANES), F32),
            jax.ShapeDtypeStruct((blocks + 24, cols), F32),
        ],
        scratch_shapes=[
            pltpu.VMEM((cols // LANES, LANES), jnp.int32),
            pltpu.VMEM(block_mask.shape, jnp.int32),
            pltpu.VMEM((1, cols), F32),
            pltpu.VMEM((rows // step, step, cols), jnp.int32),
            pltpu.VMEM((parts, cols, width), BF16),
            pltpu.SemaphoreType.DMA((3,)),
            pltpu.SemaphoreType.DMA((rows // step,)),
        ],
        compiler_params=params(28),
        cost_estimate=cost(2 * parts * rows * cols * width, 4 * rows * cols),
        name="order_first",
    )(scalars, *[in_hbm(each) for each in (col_perm.reshape(-1, LANES), block_mask, col_logm[None, :], counts)])


def order_next_kernel(offsets, scalars, shifted_ref, columns_ref, values_ref, *refs):
    parts = len(offsets)
    outs, auxes, pick = refs[:parts], refs[parts : 2 * parts], refs[-1]
    depth, width = pick.shape[1:]
    values = values_ref[...].astype(BF16)
    for part, offset in enumerate(offsets):
        base = chunk_base(scalars, offset, width)
        fill_pick(pick.at[part], columns_ref[...], base, range(depth // LANES))
        move_values(values, pick.at[part], auxes[part])
    step = 512

    @pl.loop(0, shifted_ref.shape[0] // step)
    def _(at):
        here = pl.ds(pl.multiple_of(at * step, step), step)
        for part in range(parts):
            moved = jnp.dot(shifted_ref[here, :], pick[part], preferred_element_type=F32)
            outs[part][here, :] = moved.astype(BF16)


def order_next(scalars, shifted, columns, values, offsets, width):
    rows, cols = shifted.shape
    parts = len(offsets)
    return pl.pallas_call(
        functools.partial(order_next_kernel, offsets),
        in_specs=[SCALARS] + [WHOLE] * 3,
        out_specs=[WHOLE] * (2 * parts),
        out_shape=[jax.ShapeDtypeStruct((rows, width), BF16)] * parts
        + [jax.ShapeDtypeStruct((values.shape[0] - 16, width), F32)] * parts,
        scratch_shapes=[pltpu.VMEM((parts, cols, width), BF16)],
        compiler_params=params(24),
        cost_estimate=cost(rows * width, rows * width),
        name="order_next",
    )(scalars, shifted, columns, values)


def take_kernel(scalars, perm_ref, logm_ref, *refs):
    own, from_x, from_y, from_xy, from_core, out_ref, turned_ref, logm_out, group, pick = refs
    side = own.shape[0]
    mine = [own, from_x, from_y, from_xy]
    blocks = [(2 * at, mine[at]) for at in range(4)] + [(2 * at + 1, from_core.at[at]) for at in range(4)]
    for offset, block in blocks:
        first = pl.multiple_of(jnp.bitwise_xor(scalars[COL_AT], offset) * side, side)
        group[pl.ds(first, side), :] = block[...]
    rows = out_ref.shape[0]
    depth = group.shape[0]
    groups = rows // LANES
    index = (perm_ref[...] - scalars[ROW_AT] * rows).astype(F32)
    columns = along_sublanes(jnp.concatenate([index, logm_ref[...]], axis=0))
    step = pick.shape[1]
    vocab = lax.broadcasted_iota(jnp.int32, (LANES, depth), 1).astype(F32)
    for first in range(0, rows, step):
        slot = (first // step) % pick.shape[0]
        for inner in range(0, step, LANES):
            at = (first + inner) // LANES
            pick[slot, pl.ds(inner, LANES), :] = onehot(columns[:, at : at + 1] == vocab)
            logm_out[pl.ds(first + inner, LANES), :] = jnp.broadcast_to(
                columns[:, groups + at : groups + at + 1], (LANES, LANES)
            )
        taken = jnp.dot(pick[slot], group[...], preferred_element_type=F32).astype(BF16)
        out_ref[pl.ds(first, step), :] = taken
        turned_ref[:, pl.ds(first, step)] = taken.T


def take_rows(scalars, row_perm, row_logm, blocks):
    rows = row_perm.shape[0]
    side, width = blocks[0].shape
    return pl.pallas_call(
        take_kernel,
        in_specs=[SCALARS] + [WHOLE] * 7,
        out_specs=[WHOLE] * 3,
        out_shape=[
            jax.ShapeDtypeStruct((rows, width), BF16),
            jax.ShapeDtypeStruct((width, rows), BF16),
            jax.ShapeDtypeStruct((rows, LANES), F32),
        ],
        scratch_shapes=[pltpu.VMEM((8 * side, width), BF16), pltpu.VMEM((2, 512, 8 * side), BF16)],
        compiler_params=params(24),
        cost_estimate=cost(2 * rows * rows * width, 4 * rows * width),
        name="take_rows",
    )(scalars, row_perm.reshape(-1, LANES), row_logm.reshape(-1, LANES), *blocks)


def chunk_work(
    chunk, wvec_ref, turned_ref, count_ref, aux_ref, logm_ref, before_ref, grad_ref, term_ref, chunk_turned, delta_ref
):
    chunk_turned[...] = chunk[...].T
    rows = wvec_ref.shape[0]
    width = chunk.shape[0]
    blocks = aux_ref.shape[0] - 8
    tile = rows // blocks
    joined = delta_ref.shape[0] // tile
    half = joined // 2
    col_logm = aux_ref[blocks : blocks + 1, :]
    term_ref[...] = jnp.zeros_like(term_ref)

    @pl.loop(0, blocks // joined)
    def _(group):
        def rows_at(at, count=1):
            return pl.ds(pl.multiple_of((group * joined + at) * tile, tile), count * tile)

        def held(at, count=1):
            return delta_ref[pl.ds(at * tile, count * tile), :]

        def score_of(at):
            return jnp.dot(wvec_ref[rows_at(at), :], chunk_turned[...], preferred_element_type=F32)

        def delta_of(at, score):
            here = rows_at(at)
            count = count_ref[here, :].astype(F32) + 256.0
            log = jnp.log(jnp.maximum(count, 1.0))
            row_logm = jnp.concatenate([logm_ref[here, :]] * (width // LANES), axis=1)
            gap = score + ((row_logm + col_logm) - log)
            confid = 0.1 + 0.25 * jnp.exp2(log * np.float32(0.5 / np.log(2.0)))
            zeroed = 0.5 * jnp.tanh(0.5 * gap) + 0.5
            deriv = jnp.where(count > 0.0, confid * gap, zeroed)
            active = aux_ref[pl.ds(group * joined + at, 1), :]
            delta_ref[pl.ds(at * tile, tile), :] = (deriv * active).astype(BF16)

        def grad_of(at):
            grad = jnp.dot(held(at), chunk[...], preferred_element_type=F32)
            if before_ref is not None:
                grad = grad + before_ref[rows_at(at), :]
            grad_ref[rows_at(at), :] = grad

        def term_of(at):
            turned = turned_ref[:, rows_at(at, half)]
            term_ref[...] += jnp.dot(turned, held(at, half), preferred_element_type=F32)

        ahead = score_of(0)
        for at in range(joined):
            score = ahead
            if at + 1 < joined:
                ahead = score_of(at + 1)
            delta_of(at, score)
            if at:
                grad_of(at - 1)
            if at == half:
                term_of(0)
        grad_of(joined - 1)
        term_of(half)


def cells_kernel(has_sum, sends, *refs):
    chunks = len(sends)
    wvec_ref, turned_ref, logm_ref, refs = *refs[:3], refs[3:]
    chunk_refs, count_refs, aux_refs = refs[:chunks], refs[chunks : 2 * chunks], refs[2 * chunks : 3 * chunks]
    refs = refs[3 * chunks :]
    before_ref = None
    if has_sum:
        before_ref, refs = refs[0], refs[1:]
    grad_ref, refs = refs[0], refs[1:]
    chunk_turned, delta_ref, sum_ref = refs[-3:]
    for at, pieces in enumerate(sends):
        term_ref = sum_ref
        if not pieces:
            term_ref, refs = refs[0], refs[1:]
        chunk_work(
            chunk_refs[at], wvec_ref, turned_ref, count_refs[at], aux_refs[at], logm_ref,
            before_ref, grad_ref, term_ref, chunk_turned, delta_ref,
        )
        before_ref = grad_ref
        for piece in range(pieces):
            sent_ref, refs = refs[0], refs[1:]
            size = sent_ref.shape[0]
            sent_ref[...] = term_ref[pl.ds(piece * size, size), :].astype(BF16)


def cells(rows_in, chunks, before, sends):
    wvec = rows_in[0]
    rows, depth = wvec.shape
    width = chunks[0][0].shape[0]
    args = [*rows_in, *[each for kind in zip(*chunks) for each in kind]]
    aliases = {}
    if before is not None:
        aliases = {len(args): 0}
        args.append(before)
    out_shape = [jax.ShapeDtypeStruct((rows, depth), F32)]
    for pieces in sends:
        if pieces:
            out_shape += [jax.ShapeDtypeStruct((depth // pieces, width), BF16) for _ in range(pieces)]
        else:
            out_shape.append(jax.ShapeDtypeStruct((depth, width), F32))
    return pl.pallas_call(
        functools.partial(cells_kernel, before is not None, sends),
        in_specs=[WHOLE] * len(args),
        out_specs=[WHOLE] * len(out_shape),
        out_shape=out_shape,
        scratch_shapes=[
            pltpu.VMEM((depth, width), BF16),
            pltpu.VMEM((rows // 2, width), BF16),
            pltpu.VMEM((depth, width), F32),
        ],
        input_output_aliases=aliases,
        compiler_params=params(24),
        cost_estimate=cost(rows * width, rows * depth),
        name="cells",
    )(*args)


def finish_kernel(scale, *refs):
    own_ref, near_ref, cross_refs, out_ref = refs[0], refs[1], refs[2:-1], refs[-1]
    size = cross_refs[0].shape[0]
    for at, cross_ref in enumerate(cross_refs):
        here = pl.ds(at * size, size)
        total = own_ref[here, :] + near_ref[here, :].astype(F32) + cross_ref[...].astype(F32)
        out_ref[:, here] = (total * scale).T


def finish(scale, own, near, *crosses):
    return pl.pallas_call(
        functools.partial(finish_kernel, scale),
        in_specs=[WHOLE] * (2 + len(crosses)),
        out_specs=WHOLE,
        out_shape=jax.ShapeDtypeStruct(own.shape[::-1], F32),
        compiler_params=params(8),
        cost_estimate=cost(own.size, own.size // 16),
        name="finish",
    )(own, near, *crosses)


def put_kernel(steps, other, exact, scalars, perm_ref, grad_ref, out_ref, pick):
    grad = grad_ref[...]
    rows, width = grad.shape
    high = grad.astype(BF16)
    moving = high
    if exact:
        moving = jnp.concatenate([high, (grad - high.astype(F32)).astype(BF16)], axis=1)
    side = out_ref.shape[1]
    index = jnp.broadcast_to((perm_ref[...] - scalars[ROW_AT] * rows).astype(F32), (8, rows))[:1]
    vocab = lax.broadcasted_iota(jnp.int32, (side, rows), 0)
    own = lax.shift_right_logical(scalars[COL_AT], 1)
    core = jnp.bitwise_and(scalars[COL_AT], 1)
    if other:
        core = 1 - core
    chips = [jnp.bitwise_xor(own, step) for step in steps]
    for at, chip in enumerate(chips):
        base = (2 * chip + core) * side
        pick[pl.ds(at * side, side), :] = onehot(index == (vocab + base).astype(F32))
    moved = jnp.dot(pick[...], moving, preferred_element_type=F32)
    if exact:
        moved = moved[:, :width] + moved[:, width:]
    moved = moved.astype(out_ref.dtype)
    if len(steps) == 1:
        out_ref[0] = moved
        return
    if 0 not in steps:
        out_ref[pl.ds(own, 1)] = jnp.zeros((1, side, width), out_ref.dtype)
    for at, chip in enumerate(chips):
        out_ref[pl.ds(chip, 1)] = moved[at * side : (at + 1) * side][None]


def put_rows(scalars, row_perm, grad, steps, side, other, exact):
    rows, width = grad.shape
    blocks = 1 if len(steps) == 1 else 4
    return pl.pallas_call(
        functools.partial(put_kernel, steps, other, exact),
        in_specs=[SCALARS, WHOLE, WHOLE],
        out_specs=WHOLE,
        out_shape=jax.ShapeDtypeStruct((blocks, side, width), F32 if exact else BF16),
        scratch_shapes=[pltpu.VMEM((len(steps) * side, rows), BF16)],
        compiler_params=params(24),
        cost_estimate=cost((4096 if exact and blocks > 1 else 1) * grad.size, grad.size // 16),
        name="put_rows",
    )(scalars, row_perm[None, :], grad)


def swap(value, axis, bit):
    pairs = [(at, at ^ bit) for at in range(lax.axis_size(axis))]
    return lax.ppermute(value, axis, pairs)


def together(values):
    return lax.optimization_barrier(values)


def line_shards(counts, block_mask, row_perm, col_perm, row_logm, col_logm, row_emb, col_emb):
    shard_rows, shard_cols = counts.shape
    side = row_emb.shape[0]
    width = col_emb.shape[0]
    scalars = jnp.stack([lax.axis_index("row"), lax.axis_index("col")]).astype(jnp.int32)

    cross = swap(col_emb, "row", 2)
    near = swap(col_emb, "row", 1)
    count_far, aux_far, shifted, columns, values = order_first(
        scalars, col_perm, block_mask, col_logm, counts, (3,), width
    )
    ordered = functools.partial(order_next, scalars)
    row_block, shifted = together((row_emb, shifted))
    from_x = swap(row_block, "col", 2)
    from_y = swap(row_block, "col", 4)
    from_xy = swap(row_block, "col", 6)
    count_cross, count_near, aux_cross, aux_near = ordered(shifted, columns, values, (2, 1), width)
    cross, near, from_x, from_y, from_xy, count_near, shifted = together(
        (cross, near, from_x, from_y, from_xy, count_near, shifted)
    )
    far = swap(cross, "row", 1)
    from_core = swap(jnp.stack([row_emb, from_x, from_y, from_xy]), "col", 1)
    count_own, aux_own = ordered(shifted, columns, values, (0,), width)
    count_own, row_perm = together((count_own, row_perm))
    blocks = [row_emb, from_x, from_y, from_xy, from_core]
    wvec, turned, logm = take_rows(scalars, row_perm, row_logm, blocks)

    rows_in = (wvec, turned, logm)
    of_far, of_cross = (far, count_far, aux_far), (cross, count_cross, aux_cross)
    of_near, of_own = (near, count_near, aux_near), (col_emb, count_own, aux_own)
    grad, sent_0, sent_1 = cells(rows_in, [of_far], None, (2,))
    far_0 = swap(sent_0, "row", 1)
    far_1 = swap(sent_1, "row", 1)
    grad, term_cross = cells(rows_in, [of_cross], grad, (0,))
    grad, far_0 = together((grad, far_0))

    half = term_cross.shape[0] // 2
    sum_0 = (term_cross[:half] + far_0.astype(F32)).astype(BF16)
    cross_0 = swap(sum_0, "row", 2)
    grad, sum_0 = together((grad, sum_0))
    grad, sent_near, term_own = cells(rows_in, [of_near, of_own], grad, (1, 0))
    got_near = swap(sent_near, "row", 1)
    grad, far_1, cross_0 = together((grad, far_1, cross_0))
    sum_1 = (term_cross[half:] + far_1.astype(F32)).astype(BF16)
    cross_1 = swap(sum_1, "row", 2)
    grad, sum_1 = together((grad, sum_1))

    put = functools.partial(put_rows, scalars, row_perm)
    away = put(grad, (0, 1, 2, 3), side, True, False)
    core = swap(away, "col", 1)
    grad, away = together((grad, away))
    both = put(grad, (1, 2, 3), side, False, True) + core.astype(F32)
    sends = both.astype(BF16).reshape(4 * side, -1)
    sends, grad = together((sends, grad))
    got = lax.all_to_all(sends, "col", 0, 0, axis_index_groups=[[0, 2, 4, 6], [1, 3, 5, 7]], tiled=True)
    got, term_own = together((got, term_own))
    home = put(grad, (0,), side, False, True)
    chip = lax.axis_index("col") // 2
    row_sum = home[0] + lax.dynamic_index_in_dim(core, chip, 0, False).astype(F32)
    for at in range(4):
        each = got[at * side : (at + 1) * side].astype(F32)
        row_sum = row_sum + jnp.where(chip == at, 0.0, each)
    row_scale = np.float32(1.0 / np.sqrt(shard_cols * 8))
    col_scale = np.float32(1.0 / np.sqrt(shard_rows * 4))
    return (row_sum * row_scale, finish(col_scale, term_own, got_near, cross_0, cross_1))


def solution(mesh):
    in_specs = (
        P("row", "col"),
        P("row", "col"),
        P("row"),
        P("col"),
        P("row"),
        P("col"),
        P(("row", "col"), None),
        P(("col", "row"), None),
    )
    out_specs = (P(("row", "col"), None), P(("col", "row"), None))
    line = mesh.shape["row"] == 4 and mesh.shape["col"] == 8
    body = line_shards if line else plain_shards
    return jax.shard_map(body, mesh=mesh, in_specs=in_specs, out_specs=out_specs, check_vma=False)
```

```python
import functools

import jax
import jax.numpy as jnp
import numpy as np
from jax import lax
from jax.experimental import pallas as pl
from jax.experimental.pallas import tpu as pltpu
from jax.sharding import PartitionSpec as P

F32 = jnp.float32
BF16 = jnp.bfloat16
LANES = 128
MIB = 1 << 20


def cell_delta(score, count, active, row_part, col_part):
    real_count = count.astype(F32)
    safe = jnp.maximum(real_count, 1.0)
    pmi = jnp.log(safe) - row_part[:, None] - col_part[None, :]
    confid = 0.1 + 0.25 * jnp.sqrt(safe)
    positive = confid * (score - pmi)
    zeroed = jax.nn.sigmoid(score - pmi)
    deriv = jnp.where(count > 0, positive, zeroed)
    return (active.astype(F32) * deriv).astype(BF16)


def plain_shards(counts, block_mask, row_perm, col_perm, row_logm, col_logm, row_emb, col_emb):
    shard_rows, shard_cols = counts.shape
    all_cols = shard_cols * lax.axis_size("col")
    all_rows = shard_rows * lax.axis_size("row")
    block_side = shard_rows // block_mask.shape[0]
    row_group = lax.all_gather(row_emb, "col", axis=0, tiled=True)
    col_group = lax.all_gather(col_emb, "row", axis=0, tiled=True)
    row_local = row_perm - lax.axis_index("row") * shard_rows
    col_local = col_perm - lax.axis_index("col") * shard_cols
    wvec = jnp.take(row_group, row_local, axis=0)
    cvec = jnp.take(col_group, col_local, axis=0)
    score = lax.dot_general(wvec, cvec, (((1,), (1,)), ((), ())), preferred_element_type=F32)
    active = jnp.repeat(jnp.repeat(block_mask, block_side, axis=0), block_side, axis=1)
    delta = cell_delta(score, counts, active, row_logm, col_logm)
    gshard = jnp.dot(delta, cvec, preferred_element_type=F32) / jnp.sqrt(F32(all_cols))
    ordered = jnp.zeros(gshard.shape, F32).at[row_local].set(gshard)
    row_grad = lax.psum_scatter(ordered, "col", scatter_dimension=0, tiled=True)
    hshard = lax.dot_general(
        delta, wvec, (((0,), (0,)), ((), ())), preferred_element_type=F32
    ) / jnp.sqrt(F32(all_rows))
    col_ordered = jnp.zeros(hshard.shape, F32).at[col_local].set(hshard)
    col_grad = lax.psum_scatter(col_ordered, "row", scatter_dimension=0, tiled=True)
    return (row_grad, col_grad)


ROW_AT, COL_AT = 0, 1

WHOLE = pl.BlockSpec(memory_space=pltpu.VMEM)
SCALARS = pl.BlockSpec(memory_space=pltpu.SMEM)


def params(mib):
    return pltpu.CompilerParams(vmem_limit_bytes=mib * MIB)


def cost(flops, moved):
    return pl.CostEstimate(flops=flops, bytes_accessed=moved, transcendentals=0)


def onehot(flag):
    return jnp.where(flag, 1.0, 0.0).astype(BF16)


def pieces_of(value):
    high = value.astype(BF16)
    rest = value - high.astype(F32)
    middle = rest.astype(BF16)
    low = (rest - middle.astype(F32)).astype(BF16)
    return high, middle, low


def along_sublanes(value):
    fill = jnp.zeros((LANES - value.shape[0], LANES), F32)
    return jnp.concatenate([value, fill], axis=0).T


def copies(pairs, sems):
    made = [pltpu.make_async_copy(src, dst, sems.at[at]) for at, (src, dst) in enumerate(pairs)]
    for copy in made:
        copy.start()
    return made


def fill_pick(pick, columns, base, groups):
    vocab = (lax.broadcasted_iota(jnp.int32, (LANES, pick.shape[1]), 1) + base).astype(F32)
    for group in groups:
        pick[pl.ds(group * LANES, LANES), :] = onehot(columns[:, group : group + 1] == vocab)


def chunk_base(scalars, offset, width):
    return jnp.bitwise_xor(scalars[ROW_AT], offset) * width


def move_values(values, pick, aux_ref):
    moved = jnp.dot(values, pick[...], preferred_element_type=F32)
    rows = values.shape[0] - 24
    aux_ref[pl.ds(0, rows), :] = moved[:rows]
    aux_ref[pl.ds(rows, 8), :] = moved[rows : rows + 8] + moved[rows + 8 : rows + 16] + moved[rows + 16 :]


def order_first_kernel(offsets, scalars, perm_hbm, mask_hbm, logm_hbm, count_hbm, *refs):
    parts = len(offsets)
    outs, auxes, refs = refs[:parts], refs[parts : 2 * parts], refs[2 * parts :]
    shifted_ref, columns_ref, values_ref, perm, mask_ref, logm_ref, tiles, pick, sems, tile_sems = refs
    depth = pick.shape[1]
    width = pick.shape[2]
    rows = outs[0].shape[0]
    step = tiles.shape[1]
    steps = rows // step

    slots = tiles.shape[0]

    def tile_copy(at):
        slot = lax.rem(at, slots)
        return pltpu.make_async_copy(
            count_hbm.at[pl.ds(pl.multiple_of(at * step, step), step)], tiles.at[slot], tile_sems.at[slot]
        )

    small = copies([(perm_hbm, perm), (mask_hbm, mask_ref), (logm_hbm, logm_ref)], sems)
    for at in range(slots):
        tile_copy(at).start()
    for copy in small:
        copy.wait()
    columns = along_sublanes((perm[...] - scalars[COL_AT] * depth).astype(F32))
    columns_ref[...] = columns
    blocks_r, blocks_c = mask_ref.shape
    mask = mask_ref[...].astype(F32)
    side = (blocks_r, depth // blocks_c)
    active = jnp.concatenate(
        [jnp.broadcast_to(mask[:, at : at + 1], side) for at in range(blocks_c)], axis=1
    )
    logm = jnp.broadcast_to(logm_ref[...], (8, depth))
    values = jnp.concatenate([active, *[piece.astype(F32) for piece in pieces_of(logm)]], axis=0)
    values_ref[...] = values
    values = values.astype(BF16)
    for part, offset in enumerate(offsets):
        fill_pick(pick.at[part], columns, chunk_base(scalars, offset, width), range(depth // LANES))
        move_values(values, pick.at[part], auxes[part])

    @pl.loop(0, steps)
    def _(at):
        here = pl.ds(pl.multiple_of(at * step, step), step)
        tile_copy(at).wait()
        shifted = (tiles[lax.rem(at, slots)] - 256).astype(F32).astype(BF16)
        shifted_ref[here, :] = shifted

        @pl.when(at + slots < steps)
        def _():
            tile_copy(at + slots).start()

        for part in range(parts):
            moved = jnp.dot(shifted, pick[part], preferred_element_type=F32)
            outs[part][here, :] = moved.astype(BF16)


def in_hbm(value):
    return pltpu.with_memory_space_constraint(value, pltpu.HBM)


def order_first(scalars, col_perm, block_mask, col_logm, counts, offsets, width):
    rows, cols = counts.shape
    parts = len(offsets)
    blocks = block_mask.shape[0]
    outside = pl.BlockSpec(memory_space=pltpu.HBM)
    step = 512
    return pl.pallas_call(
        functools.partial(order_first_kernel, offsets),
        in_specs=[SCALARS] + [outside] * 4,
        out_specs=[WHOLE] * (2 * parts + 3),
        out_shape=[jax.ShapeDtypeStruct((rows, width), BF16)] * parts
        + [jax.ShapeDtypeStruct((blocks + 8, width), F32)] * parts
        + [
            jax.ShapeDtypeStruct((rows, cols), BF16),
            jax.ShapeDtypeStruct((LANES, LANES), F32),
            jax.ShapeDtypeStruct((blocks + 24, cols), F32),
        ],
        scratch_shapes=[
            pltpu.VMEM((cols // LANES, LANES), jnp.int32),
            pltpu.VMEM(block_mask.shape, jnp.int32),
            pltpu.VMEM((1, cols), F32),
            pltpu.VMEM((2, step, cols), jnp.int32),
            pltpu.VMEM((parts, cols, width), BF16),
            pltpu.SemaphoreType.DMA((3,)),
            pltpu.SemaphoreType.DMA((2,)),
        ],
        compiler_params=params(28),
        cost_estimate=cost(2 * parts * rows * cols * width, 4 * rows * cols),
        name="order_first",
    )(scalars, *[in_hbm(each) for each in (col_perm.reshape(-1, LANES), block_mask, col_logm[None, :], counts)])


def order_next_kernel(offsets, scalars, shifted_ref, columns_ref, values_ref, *refs):
    parts = len(offsets)
    outs, auxes, pick = refs[:parts], refs[parts : 2 * parts], refs[-1]
    depth, width = pick.shape[1:]
    values = values_ref[...].astype(BF16)
    for part, offset in enumerate(offsets):
        base = chunk_base(scalars, offset, width)
        fill_pick(pick.at[part], columns_ref[...], base, range(depth // LANES))
        move_values(values, pick.at[part], auxes[part])
    step = 512

    @pl.loop(0, shifted_ref.shape[0] // step)
    def _(at):
        here = pl.ds(pl.multiple_of(at * step, step), step)
        for part in range(parts):
            moved = jnp.dot(shifted_ref[here, :], pick[part], preferred_element_type=F32)
            outs[part][here, :] = moved.astype(BF16)


def order_next(scalars, shifted, columns, values, offsets, width):
    rows, cols = shifted.shape
    parts = len(offsets)
    return pl.pallas_call(
        functools.partial(order_next_kernel, offsets),
        in_specs=[SCALARS] + [WHOLE] * 3,
        out_specs=[WHOLE] * (2 * parts),
        out_shape=[jax.ShapeDtypeStruct((rows, width), BF16)] * parts
        + [jax.ShapeDtypeStruct((values.shape[0] - 16, width), F32)] * parts,
        scratch_shapes=[pltpu.VMEM((parts, cols, width), BF16)],
        compiler_params=params(24),
        cost_estimate=cost(rows * width, rows * width),
        name="order_next",
    )(scalars, shifted, columns, values)


def take_kernel(scalars, perm_ref, logm_ref, *refs):
    own, from_x, from_y, from_xy, from_core, out_ref, turned_ref, logm_out, group, pick = refs
    side = own.shape[0]
    mine = [own, from_x, from_y, from_xy]
    blocks = [(2 * at, mine[at]) for at in range(4)] + [(2 * at + 1, from_core.at[at]) for at in range(4)]
    for offset, block in blocks:
        first = pl.multiple_of(jnp.bitwise_xor(scalars[COL_AT], offset) * side, side)
        group[pl.ds(first, side), :] = block[...]
    rows = out_ref.shape[0]
    depth = group.shape[0]
    groups = rows // LANES
    index = (perm_ref[...] - scalars[ROW_AT] * rows).astype(F32)
    columns = along_sublanes(jnp.concatenate([index, logm_ref[...]], axis=0))
    step = pick.shape[1]
    vocab = lax.broadcasted_iota(jnp.int32, (LANES, depth), 1).astype(F32)
    for first in range(0, rows, step):
        slot = (first // step) % pick.shape[0]
        for inner in range(0, step, LANES):
            at = (first + inner) // LANES
            pick[slot, pl.ds(inner, LANES), :] = onehot(columns[:, at : at + 1] == vocab)
            logm_out[pl.ds(first + inner, LANES), :] = jnp.broadcast_to(
                columns[:, groups + at : groups + at + 1], (LANES, LANES)
            )
        taken = jnp.dot(pick[slot], group[...], preferred_element_type=F32).astype(BF16)
        out_ref[pl.ds(first, step), :] = taken
        turned_ref[:, pl.ds(first, step)] = taken.T


def take_rows(scalars, row_perm, row_logm, blocks):
    rows = row_perm.shape[0]
    side, width = blocks[0].shape
    return pl.pallas_call(
        take_kernel,
        in_specs=[SCALARS] + [WHOLE] * 7,
        out_specs=[WHOLE] * 3,
        out_shape=[
            jax.ShapeDtypeStruct((rows, width), BF16),
            jax.ShapeDtypeStruct((width, rows), BF16),
            jax.ShapeDtypeStruct((rows, LANES), F32),
        ],
        scratch_shapes=[pltpu.VMEM((8 * side, width), BF16), pltpu.VMEM((2, 512, 8 * side), BF16)],
        compiler_params=params(24),
        cost_estimate=cost(2 * rows * rows * width, 4 * rows * width),
        name="take_rows",
    )(scalars, row_perm.reshape(-1, LANES), row_logm.reshape(-1, LANES), *blocks)


def cells_kernel(has_sum, sends, *refs):
    chunks = len(sends)
    wvec_ref, turned_ref, logm_ref, refs = *refs[:3], refs[3:]
    chunk_refs, count_refs, aux_refs = refs[:chunks], refs[chunks : 2 * chunks], refs[2 * chunks : 3 * chunks]
    refs = refs[3 * chunks :]
    before_ref = None
    if has_sum:
        before_ref, refs = refs[0], refs[1:]
    grad_ref, outs = refs[0], list(refs[1:-4])
    chunk, chunk_turned, delta_ref, term_ref = refs[-4:]
    rows = wvec_ref.shape[0]
    width = chunk.shape[0]
    blocks = aux_refs[0].shape[0] - 8
    tile = rows // blocks
    joined = delta_ref.shape[0] // tile
    half = joined // 2
    out_refs = [[outs.pop(0) for _ in range(max(pieces, 1))] for pieces in sends]

    def work(which):
        def chosen(several, here):
            value = several[0][here]
            for at in range(1, chunks):
                value = jnp.where(which == at, several[at][here], value)
            return value

        for at in range(chunks):

            @pl.when(which == at)
            def _():
                chunk[...] = chunk_refs[at][...]

        chunk_turned[...] = chunk[...].T
        col_logm = chosen(aux_refs, (pl.ds(blocks, 1), slice(None)))

        def part(group):
            def rows_at(at, count=1):
                return pl.ds(pl.multiple_of((group * joined + at) * tile, tile), count * tile)

            def held(at, count=1):
                return delta_ref[pl.ds(at * tile, count * tile), :]

            def score_of(at):
                return jnp.dot(wvec_ref[rows_at(at), :], chunk_turned[...], preferred_element_type=F32)

            def delta_of(at, score):
                here = (rows_at(at), slice(None))
                count = chosen(count_refs, here).astype(F32) + 256.0
                log = jnp.log(jnp.maximum(count, 1.0))
                row_logm = jnp.concatenate([logm_ref[here]] * (width // LANES), axis=1)
                gap = score + ((row_logm + col_logm) - log)
                confid = 0.1 + 0.25 * jnp.exp2(log * np.float32(0.5 / np.log(2.0)))
                zeroed = 0.5 * jnp.tanh(0.5 * gap) + 0.5
                deriv = jnp.where(count > 0.0, confid * gap, zeroed)
                active = chosen(aux_refs, (pl.ds(group * joined + at, 1), slice(None)))
                delta_ref[pl.ds(at * tile, tile), :] = (deriv * active).astype(BF16)

            def grad_of(at):
                here = (rows_at(at), slice(None))
                grad = jnp.dot(held(at), chunk[...], preferred_element_type=F32)
                if has_sum:
                    before = before_ref[here]
                    if chunks > 1:
                        before = jnp.where(which == 0, before, grad_ref[here])
                    grad = grad + before
                grad_ref[here] = grad

            def term_of(at):
                turned = turned_ref[:, rows_at(at, half)]
                term = jnp.dot(turned, held(at, half), preferred_element_type=F32)
                if joined < blocks or at:
                    term = term_ref[...] + term
                term_ref[...] = term

            ahead = score_of(0)
            for at in range(joined):
                score = ahead
                if at + 1 < joined:
                    ahead = score_of(at + 1)
                delta_of(at, score)
                if at:
                    grad_of(at - 1)
                if at == half:
                    term_of(0)
            grad_of(joined - 1)
            term_of(half)

        if joined < blocks:
            term_ref[...] = jnp.zeros_like(term_ref)
            pl.loop(0, blocks // joined)(part)
        else:
            part(0)

        for at, pieces in enumerate(sends):

            @pl.when(which == at)
            def _():
                for piece, out_ref in enumerate(out_refs[at]):
                    size = out_ref.shape[0]
                    out_ref[...] = term_ref[pl.ds(piece * size, size), :].astype(out_ref.dtype)

    if chunks > 1:
        pl.loop(0, chunks)(work)
    else:
        work(0)


def cells(rows_in, chunks, before, sends):
    wvec = rows_in[0]
    rows, depth = wvec.shape
    width = chunks[0][0].shape[0]
    args = [*rows_in, *[each for kind in zip(*chunks) for each in kind]]
    aliases = {}
    if before is not None:
        aliases = {len(args): 0}
        args.append(before)
    out_shape = [jax.ShapeDtypeStruct((rows, depth), F32)]
    for pieces in sends:
        if pieces:
            out_shape += [jax.ShapeDtypeStruct((depth // pieces, width), BF16) for _ in range(pieces)]
        else:
            out_shape.append(jax.ShapeDtypeStruct((depth, width), F32))
    return pl.pallas_call(
        functools.partial(cells_kernel, before is not None, sends),
        in_specs=[WHOLE] * len(args),
        out_specs=[WHOLE] * len(out_shape),
        out_shape=out_shape,
        scratch_shapes=[
            pltpu.VMEM((width, depth), BF16),
            pltpu.VMEM((depth, width), BF16),
            pltpu.VMEM((rows, width), BF16),
            pltpu.VMEM((depth, width), F32),
        ],
        input_output_aliases=aliases,
        compiler_params=params(24),
        cost_estimate=cost(rows * width, rows * depth),
        name="cells",
    )(*args)


def finish_kernel(scale, *refs):
    own_ref, near_ref, cross_refs, out_ref = refs[0], refs[1], refs[2:-1], refs[-1]
    size = cross_refs[0].shape[0]
    for at, cross_ref in enumerate(cross_refs):
        here = pl.ds(at * size, size)
        total = own_ref[here, :] + near_ref[here, :].astype(F32) + cross_ref[...].astype(F32)
        out_ref[:, here] = (total * scale).T


def finish(scale, own, near, *crosses):
    return pl.pallas_call(
        functools.partial(finish_kernel, scale),
        in_specs=[WHOLE] * (2 + len(crosses)),
        out_specs=WHOLE,
        out_shape=jax.ShapeDtypeStruct(own.shape[::-1], F32),
        compiler_params=params(8),
        cost_estimate=cost(own.size, own.size // 16),
        name="finish",
    )(own, near, *crosses)


def put_kernel(offsets, exact, scalars, perm_ref, grad_ref, out_ref, pick):
    grad = grad_ref[...]
    rows, width = grad.shape
    high = grad.astype(BF16)
    moving = high
    if exact:
        moving = jnp.concatenate([high, (grad - high.astype(F32)).astype(BF16)], axis=1)
    side = out_ref.shape[1]
    index = jnp.broadcast_to((perm_ref[...] - scalars[ROW_AT] * rows).astype(F32), (8, rows))[:1]
    vocab = lax.broadcasted_iota(jnp.int32, (side, rows), 0)
    for at, offset in enumerate(offsets):
        base = jnp.bitwise_xor(scalars[COL_AT], offset) * side
        pick[pl.ds(at * side, side), :] = onehot(index == (vocab + base).astype(F32))
    moved = jnp.dot(pick[...], moving, preferred_element_type=F32)
    if exact:
        moved = moved[:, :width] + moved[:, width:]
    out_ref[...] = moved.astype(out_ref.dtype).reshape(out_ref.shape)


def put_rows(scalars, row_perm, grad, offsets, side, exact):
    width = grad.shape[1]
    return pl.pallas_call(
        functools.partial(put_kernel, offsets, exact),
        in_specs=[SCALARS, WHOLE, WHOLE],
        out_specs=WHOLE,
        out_shape=jax.ShapeDtypeStruct((len(offsets), side, width), F32 if exact else BF16),
        scratch_shapes=[pltpu.VMEM((len(offsets) * side, grad.shape[0]), BF16)],
        compiler_params=params(24),
        cost_estimate=cost((4096 if exact and len(offsets) > 1 else 1) * grad.size, grad.size // 16),
        name="put_rows",
    )(scalars, row_perm[None, :], grad)


def swap(value, axis, bit):
    pairs = [(at, at ^ bit) for at in range(lax.axis_size(axis))]
    return lax.ppermute(value, axis, pairs)


def together(values):
    return lax.optimization_barrier(values)


def line_shards(counts, block_mask, row_perm, col_perm, row_logm, col_logm, row_emb, col_emb):
    shard_rows, shard_cols = counts.shape
    side = row_emb.shape[0]
    width = col_emb.shape[0]
    scalars = jnp.stack([lax.axis_index("row"), lax.axis_index("col")]).astype(jnp.int32)

    cross = swap(col_emb, "row", 2)
    near = swap(col_emb, "row", 1)
    count_far, aux_far, shifted, columns, values = order_first(
        scalars, col_perm, block_mask, col_logm, counts, (3,), width
    )
    ordered = functools.partial(order_next, scalars)
    row_block, shifted = together((row_emb, shifted))
    from_x = swap(row_block, "col", 2)
    from_y = swap(row_block, "col", 4)
    from_xy = swap(row_block, "col", 6)
    count_cross, count_near, aux_cross, aux_near = ordered(shifted, columns, values, (2, 1), width)
    cross, near, from_x, from_y, from_xy, count_near, shifted = together(
        (cross, near, from_x, from_y, from_xy, count_near, shifted)
    )
    far = swap(cross, "row", 1)
    from_core = swap(jnp.stack([row_emb, from_x, from_y, from_xy]), "col", 1)
    count_own, aux_own = ordered(shifted, columns, values, (0,), width)
    count_own, row_perm = together((count_own, row_perm))
    blocks = [row_emb, from_x, from_y, from_xy, from_core]
    wvec, turned, logm = take_rows(scalars, row_perm, row_logm, blocks)

    rows_in = (wvec, turned, logm)
    of_far, of_cross = (far, count_far, aux_far), (cross, count_cross, aux_cross)
    of_near, of_own = (near, count_near, aux_near), (col_emb, count_own, aux_own)
    grad, sent_0, sent_1 = cells(rows_in, [of_far], None, (2,))
    far_0 = swap(sent_0, "row", 1)
    far_1 = swap(sent_1, "row", 1)
    grad, term_cross = cells(rows_in, [of_cross], grad, (0,))
    grad, far_0 = together((grad, far_0))

    half = term_cross.shape[0] // 2
    sum_0 = (term_cross[:half] + far_0.astype(F32)).astype(BF16)
    cross_0 = swap(sum_0, "row", 2)
    grad, sum_0 = together((grad, sum_0))
    grad, sent_near, term_own = cells(rows_in, [of_near, of_own], grad, (1, 0))
    got_near = swap(sent_near, "row", 1)
    grad, far_1, cross_0 = together((grad, far_1, cross_0))
    sum_1 = (term_cross[half:] + far_1.astype(F32)).astype(BF16)
    cross_1 = swap(sum_1, "row", 2)
    grad, sum_1 = together((grad, sum_1))

    ordered = functools.partial(put_rows, scalars, row_perm)
    away = ordered(grad, (1, 3, 5, 7), side, False)
    core = swap(away, "col", 1)
    grad, away = together((grad, away))
    both = ordered(grad, (2, 4, 6), side, True) + core[1:].astype(F32)
    sends = [both[at].astype(BF16) for at in range(3)]
    got = [swap(sends[at], "col", bit) for at, bit in ((1, 4), (2, 6), (0, 2))]
    grad, sends = together((grad, sends))
    home = ordered(grad, (0,), side, True)
    home, term_own = together((home, term_own))
    row_sum = home[0] + core[0].astype(F32)
    for each in got:
        row_sum = row_sum + each.astype(F32)
    row_scale = np.float32(1.0 / np.sqrt(shard_cols * 8))
    col_scale = np.float32(1.0 / np.sqrt(shard_rows * 4))
    return (row_sum * row_scale, finish(col_scale, term_own, got_near, cross_0, cross_1))


def solution(mesh):
    in_specs = (
        P("row", "col"),
        P("row", "col"),
        P("row"),
        P("col"),
        P("row"),
        P("col"),
        P(("row", "col"), None),
        P(("col", "row"), None),
    )
    out_specs = (P(("row", "col"), None), P(("col", "row"), None))
    line = mesh.shape["row"] == 4 and mesh.shape["col"] == 8
    body = line_shards if line else plain_shards
    return jax.shard_map(body, mesh=mesh, in_specs=in_specs, out_specs=out_specs, check_vma=False)
```

```python
import functools

import jax
import jax.numpy as jnp
import numpy as np
from jax import lax
from jax.experimental import pallas as pl
from jax.experimental.pallas import tpu as pltpu
from jax.sharding import PartitionSpec as P

F32 = jnp.float32
BF16 = jnp.bfloat16
LANES = 128
MIB = 1 << 20


def cell_delta(score, count, active, row_part, col_part):
    real_count = count.astype(F32)
    safe = jnp.maximum(real_count, 1.0)
    pmi = jnp.log(safe) - row_part[:, None] - col_part[None, :]
    confid = 0.1 + 0.25 * jnp.sqrt(safe)
    positive = confid * (score - pmi)
    zeroed = jax.nn.sigmoid(score - pmi)
    deriv = jnp.where(count > 0, positive, zeroed)
    return (active.astype(F32) * deriv).astype(BF16)


def plain_shards(counts, block_mask, row_perm, col_perm, row_logm, col_logm, row_emb, col_emb):
    shard_rows, shard_cols = counts.shape
    all_cols = shard_cols * lax.axis_size("col")
    all_rows = shard_rows * lax.axis_size("row")
    block_side = shard_rows // block_mask.shape[0]
    row_group = lax.all_gather(row_emb, "col", axis=0, tiled=True)
    col_group = lax.all_gather(col_emb, "row", axis=0, tiled=True)
    row_local = row_perm - lax.axis_index("row") * shard_rows
    col_local = col_perm - lax.axis_index("col") * shard_cols
    wvec = jnp.take(row_group, row_local, axis=0)
    cvec = jnp.take(col_group, col_local, axis=0)
    score = lax.dot_general(wvec, cvec, (((1,), (1,)), ((), ())), preferred_element_type=F32)
    active = jnp.repeat(jnp.repeat(block_mask, block_side, axis=0), block_side, axis=1)
    delta = cell_delta(score, counts, active, row_logm, col_logm)
    gshard = jnp.dot(delta, cvec, preferred_element_type=F32) / jnp.sqrt(F32(all_cols))
    ordered = jnp.zeros(gshard.shape, F32).at[row_local].set(gshard)
    row_grad = lax.psum_scatter(ordered, "col", scatter_dimension=0, tiled=True)
    hshard = lax.dot_general(
        delta, wvec, (((0,), (0,)), ((), ())), preferred_element_type=F32
    ) / jnp.sqrt(F32(all_rows))
    col_ordered = jnp.zeros(hshard.shape, F32).at[col_local].set(hshard)
    col_grad = lax.psum_scatter(col_ordered, "row", scatter_dimension=0, tiled=True)
    return (row_grad, col_grad)


ROW_AT, COL_AT = 0, 1

WHOLE = pl.BlockSpec(memory_space=pltpu.VMEM)
SCALARS = pl.BlockSpec(memory_space=pltpu.SMEM)


def params(mib):
    return pltpu.CompilerParams(vmem_limit_bytes=mib * MIB)


def cost(flops, moved):
    return pl.CostEstimate(flops=flops, bytes_accessed=moved, transcendentals=0)


def onehot(flag):
    return jnp.where(flag, 1.0, 0.0).astype(BF16)


def pieces_of(value):
    high = value.astype(BF16)
    rest = value - high.astype(F32)
    middle = rest.astype(BF16)
    low = (rest - middle.astype(F32)).astype(BF16)
    return high, middle, low


def along_sublanes(value):
    fill = jnp.zeros((LANES - value.shape[0], LANES), F32)
    return jnp.concatenate([value, fill], axis=0).T


def copies(pairs, sems):
    made = [pltpu.make_async_copy(src, dst, sems.at[at]) for at, (src, dst) in enumerate(pairs)]
    for copy in made:
        copy.start()
    return made


def fill_pick(pick, columns, base, groups):
    vocab = (lax.broadcasted_iota(jnp.int32, (LANES, pick.shape[1]), 1) + base).astype(F32)
    for group in groups:
        pick[pl.ds(group * LANES, LANES), :] = onehot(columns[:, group : group + 1] == vocab)


def chunk_base(scalars, offset, width):
    return jnp.bitwise_xor(scalars[ROW_AT], offset) * width


def move_values(values, pick, aux_ref):
    moved = jnp.dot(values, pick[...], preferred_element_type=F32)
    rows = values.shape[0] - 24
    aux_ref[pl.ds(0, rows), :] = moved[:rows]
    aux_ref[pl.ds(rows, 8), :] = moved[rows : rows + 8] + moved[rows + 8 : rows + 16] + moved[rows + 16 :]


def order_first_kernel(offsets, scalars, perm_hbm, mask_hbm, logm_hbm, count_hbm, *refs):
    parts = len(offsets)
    outs, auxes, refs = refs[:parts], refs[parts : 2 * parts], refs[2 * parts :]
    shifted_ref, columns_ref, values_ref, perm, mask_ref, logm_ref, tiles, pick, sems, tile_sems = refs
    depth = pick.shape[1]
    width = pick.shape[2]
    rows = outs[0].shape[0]
    step = tiles.shape[1]
    steps = rows // step

    slots = tiles.shape[0]

    def tile_copy(at):
        slot = lax.rem(at, slots)
        return pltpu.make_async_copy(
            count_hbm.at[pl.ds(pl.multiple_of(at * step, step), step)], tiles.at[slot], tile_sems.at[slot]
        )

    small = copies([(perm_hbm, perm), (mask_hbm, mask_ref), (logm_hbm, logm_ref)], sems)
    for at in range(slots):
        tile_copy(at).start()
    for copy in small:
        copy.wait()
    columns = along_sublanes((perm[...] - scalars[COL_AT] * depth).astype(F32))
    columns_ref[...] = columns
    blocks_r, blocks_c = mask_ref.shape
    mask = mask_ref[...].astype(F32)
    side = (blocks_r, depth // blocks_c)
    active = jnp.concatenate(
        [jnp.broadcast_to(mask[:, at : at + 1], side) for at in range(blocks_c)], axis=1
    )
    logm = jnp.broadcast_to(logm_ref[...], (8, depth))
    values = jnp.concatenate([active, *[piece.astype(F32) for piece in pieces_of(logm)]], axis=0)
    values_ref[...] = values
    values = values.astype(BF16)
    for part, offset in enumerate(offsets):
        fill_pick(pick.at[part], columns, chunk_base(scalars, offset, width), range(depth // LANES))
        move_values(values, pick.at[part], auxes[part])

    @pl.loop(0, steps)
    def _(at):
        here = pl.ds(pl.multiple_of(at * step, step), step)
        tile_copy(at).wait()
        shifted = (tiles[lax.rem(at, slots)] - 256).astype(F32).astype(BF16)
        shifted_ref[here, :] = shifted

        @pl.when(at + slots < steps)
        def _():
            tile_copy(at + slots).start()

        for part in range(parts):
            moved = jnp.dot(shifted, pick[part], preferred_element_type=F32)
            outs[part][here, :] = moved.astype(BF16)


def in_hbm(value):
    return pltpu.with_memory_space_constraint(value, pltpu.HBM)


def order_first(scalars, col_perm, block_mask, col_logm, counts, offsets, width):
    rows, cols = counts.shape
    parts = len(offsets)
    blocks = block_mask.shape[0]
    outside = pl.BlockSpec(memory_space=pltpu.HBM)
    step = 512
    return pl.pallas_call(
        functools.partial(order_first_kernel, offsets),
        in_specs=[SCALARS] + [outside] * 4,
        out_specs=[WHOLE] * (2 * parts + 3),
        out_shape=[jax.ShapeDtypeStruct((rows, width), BF16)] * parts
        + [jax.ShapeDtypeStruct((blocks + 8, width), F32)] * parts
        + [
            jax.ShapeDtypeStruct((rows, cols), BF16),
            jax.ShapeDtypeStruct((LANES, LANES), F32),
            jax.ShapeDtypeStruct((blocks + 24, cols), F32),
        ],
        scratch_shapes=[
            pltpu.VMEM((cols // LANES, LANES), jnp.int32),
            pltpu.VMEM(block_mask.shape, jnp.int32),
            pltpu.VMEM((1, cols), F32),
            pltpu.VMEM((2, step, cols), jnp.int32),
            pltpu.VMEM((parts, cols, width), BF16),
            pltpu.SemaphoreType.DMA((3,)),
            pltpu.SemaphoreType.DMA((2,)),
        ],
        compiler_params=params(28),
        cost_estimate=cost(2 * parts * rows * cols * width, 4 * rows * cols),
        name="order_first",
    )(scalars, *[in_hbm(each) for each in (col_perm.reshape(-1, LANES), block_mask, col_logm[None, :], counts)])


def order_next_kernel(offsets, scalars, shifted_ref, columns_ref, values_ref, *refs):
    parts = len(offsets)
    outs, auxes, pick = refs[:parts], refs[parts : 2 * parts], refs[-1]
    depth, width = pick.shape[1:]
    values = values_ref[...].astype(BF16)
    for part, offset in enumerate(offsets):
        base = chunk_base(scalars, offset, width)
        fill_pick(pick.at[part], columns_ref[...], base, range(depth // LANES))
        move_values(values, pick.at[part], auxes[part])
    step = 512

    @pl.loop(0, shifted_ref.shape[0] // step)
    def _(at):
        here = pl.ds(pl.multiple_of(at * step, step), step)
        for part in range(parts):
            moved = jnp.dot(shifted_ref[here, :], pick[part], preferred_element_type=F32)
            outs[part][here, :] = moved.astype(BF16)


def order_next(scalars, shifted, columns, values, offsets, width):
    rows, cols = shifted.shape
    parts = len(offsets)
    return pl.pallas_call(
        functools.partial(order_next_kernel, offsets),
        in_specs=[SCALARS] + [WHOLE] * 3,
        out_specs=[WHOLE] * (2 * parts),
        out_shape=[jax.ShapeDtypeStruct((rows, width), BF16)] * parts
        + [jax.ShapeDtypeStruct((values.shape[0] - 16, width), F32)] * parts,
        scratch_shapes=[pltpu.VMEM((parts, cols, width), BF16)],
        compiler_params=params(24),
        cost_estimate=cost(rows * width, rows * width),
        name="order_next",
    )(scalars, shifted, columns, values)


def take_kernel(scalars, perm_ref, logm_ref, *refs):
    own, from_x, from_y, from_xy, from_core, out_ref, turned_ref, logm_out, group, pick = refs
    side = own.shape[0]
    mine = [own, from_x, from_y, from_xy]
    blocks = [(2 * at, mine[at]) for at in range(4)] + [(2 * at + 1, from_core.at[at]) for at in range(4)]
    for offset, block in blocks:
        first = pl.multiple_of(jnp.bitwise_xor(scalars[COL_AT], offset) * side, side)
        group[pl.ds(first, side), :] = block[...]
    rows = out_ref.shape[0]
    depth = group.shape[0]
    groups = rows // LANES
    index = (perm_ref[...] - scalars[ROW_AT] * rows).astype(F32)
    columns = along_sublanes(jnp.concatenate([index, logm_ref[...]], axis=0))
    step = pick.shape[1]
    vocab = lax.broadcasted_iota(jnp.int32, (LANES, depth), 1).astype(F32)
    for first in range(0, rows, step):
        slot = (first // step) % pick.shape[0]
        for inner in range(0, step, LANES):
            at = (first + inner) // LANES
            pick[slot, pl.ds(inner, LANES), :] = onehot(columns[:, at : at + 1] == vocab)
            logm_out[pl.ds(first + inner, LANES), :] = jnp.broadcast_to(
                columns[:, groups + at : groups + at + 1], (LANES, LANES)
            )
        taken = jnp.dot(pick[slot], group[...], preferred_element_type=F32).astype(BF16)
        out_ref[pl.ds(first, step), :] = taken
        turned_ref[:, pl.ds(first, step)] = taken.T


def take_rows(scalars, row_perm, row_logm, blocks):
    rows = row_perm.shape[0]
    side, width = blocks[0].shape
    return pl.pallas_call(
        take_kernel,
        in_specs=[SCALARS] + [WHOLE] * 7,
        out_specs=[WHOLE] * 3,
        out_shape=[
            jax.ShapeDtypeStruct((rows, width), BF16),
            jax.ShapeDtypeStruct((width, rows), BF16),
            jax.ShapeDtypeStruct((rows, LANES), F32),
        ],
        scratch_shapes=[pltpu.VMEM((8 * side, width), BF16), pltpu.VMEM((2, 512, 8 * side), BF16)],
        compiler_params=params(24),
        cost_estimate=cost(2 * rows * rows * width, 4 * rows * width),
        name="take_rows",
    )(scalars, row_perm.reshape(-1, LANES), row_logm.reshape(-1, LANES), *blocks)


def cells_kernel(others, pieces, *refs):
    wvec_ref, turned_ref, logm_ref, chunk, count_ref, aux_ref, refs = *refs[:6], refs[6:]
    chunk_refs, delta_refs, refs = refs[:others], refs[others : 2 * others], refs[2 * others :]
    main_ref, out_refs, refs = refs[0], refs[1 : 1 + max(pieces, 1)], refs[1 + max(pieces, 1) :]
    chunk_turned, term_ref, refs = refs[0], refs[1], refs[2:]
    chunk_turned[...] = chunk[...].T
    rows = wvec_ref.shape[0]
    width = chunk.shape[0]
    blocks = aux_ref.shape[0] - 8
    tile = rows // blocks
    col_logm = aux_ref[pl.ds(blocks, 1), :]
    if others:
        delta_ref, stack = refs
        for at, ref in enumerate([*chunk_refs, chunk]):
            stack[pl.ds(at * width, width), :] = ref[...]
    else:
        delta_ref = main_ref
    joined = delta_ref.shape[0] // tile
    half = joined // 2

    def part(group):
        def rows_at(at, count=1):
            return pl.ds(pl.multiple_of((group * joined + at) * tile, tile), count * tile)

        def held(at, count=1):
            return delta_ref[pl.ds(at * tile, count * tile), :]

        def score_of(at):
            return jnp.dot(wvec_ref[rows_at(at), :], chunk_turned[...], preferred_element_type=F32)

        def delta_of(at, score):
            here = rows_at(at)
            count = count_ref[here, :].astype(F32) + 256.0
            log = jnp.log(jnp.maximum(count, 1.0))
            row_logm = jnp.concatenate([logm_ref[here, :]] * (width // LANES), axis=1)
            gap = score + ((row_logm + col_logm) - log)
            confid = 0.1 + 0.25 * jnp.exp2(log * np.float32(0.5 / np.log(2.0)))
            zeroed = 0.5 * jnp.tanh(0.5 * gap) + 0.5
            deriv = jnp.where(count > 0.0, confid * gap, zeroed)
            active = aux_ref[pl.ds(group * joined + at, 1), :]
            delta_ref[pl.ds(at * tile, tile), :] = (deriv * active).astype(BF16)

        def grad_of(at, count):
            here = rows_at(at, count)
            deltas = jnp.concatenate([ref[here, :] for ref in delta_refs] + [held(at, count)], axis=1)
            main_ref[here, :] = jnp.dot(deltas, stack[...], preferred_element_type=F32)

        def term_of(at):
            turned = turned_ref[:, rows_at(at, half)]
            term = jnp.dot(turned, held(at, half), preferred_element_type=F32)
            if joined < blocks or at:
                term = term_ref[...] + term
            term_ref[...] = term

        ahead = score_of(0)
        for at in range(joined):
            score = ahead
            if at + 1 < joined:
                ahead = score_of(at + 1)
            delta_of(at, score)
            if at == half:
                term_of(0)
                if others:
                    grad_of(0, half)
        term_of(half)
        if others:
            grad_of(half, half)

    if joined < blocks:
        term_ref[...] = jnp.zeros_like(term_ref)
        pl.loop(0, blocks // joined)(part)
    else:
        part(0)
    for piece, out_ref in enumerate(out_refs):
        size = out_ref.shape[0]
        out_ref[...] = term_ref[pl.ds(piece * size, size), :].astype(out_ref.dtype)


def cells(rows_in, chunk, pieces, others=()):
    wvec = rows_in[0]
    rows, depth = wvec.shape
    width = chunk[0].shape[0]
    args = [*rows_in, *chunk, *[each for each, _ in others], *[delta for _, delta in others]]
    if others:
        main = jax.ShapeDtypeStruct((rows, depth), F32)
        scratch = [pltpu.VMEM((rows // 2, width), BF16), pltpu.VMEM(((len(others) + 1) * width, depth), BF16)]
    else:
        main = jax.ShapeDtypeStruct((rows, width), BF16)
        scratch = []
    if pieces:
        outs = [jax.ShapeDtypeStruct((depth // pieces, width), BF16) for _ in range(pieces)]
    else:
        outs = [jax.ShapeDtypeStruct((depth, width), F32)]
    return pl.pallas_call(
        functools.partial(cells_kernel, len(others), pieces),
        in_specs=[WHOLE] * len(args),
        out_specs=[WHOLE] * (1 + len(outs)),
        out_shape=[main, *outs],
        scratch_shapes=[pltpu.VMEM((depth, width), BF16), pltpu.VMEM((depth, width), F32), *scratch],
        compiler_params=params(24),
        cost_estimate=cost(rows * width, rows * depth),
        name="cells",
    )(*args)


def finish_kernel(scale, *refs):
    own_ref, near_ref, cross_refs, out_ref = refs[0], refs[1], refs[2:-1], refs[-1]
    size = cross_refs[0].shape[0]
    for at, cross_ref in enumerate(cross_refs):
        here = pl.ds(at * size, size)
        total = own_ref[here, :] + near_ref[here, :].astype(F32) + cross_ref[...].astype(F32)
        out_ref[:, here] = (total * scale).T


def finish(scale, own, near, *crosses):
    return pl.pallas_call(
        functools.partial(finish_kernel, scale),
        in_specs=[WHOLE] * (2 + len(crosses)),
        out_specs=WHOLE,
        out_shape=jax.ShapeDtypeStruct(own.shape[::-1], F32),
        compiler_params=params(8),
        cost_estimate=cost(own.size, own.size // 16),
        name="finish",
    )(own, near, *crosses)


def put_kernel(offsets, exact, scalars, perm_ref, grad_ref, out_ref, pick):
    grad = grad_ref[...]
    rows, width = grad.shape
    high = grad.astype(BF16)
    moving = high
    if exact:
        moving = jnp.concatenate([high, (grad - high.astype(F32)).astype(BF16)], axis=1)
    side = out_ref.shape[1]
    index = jnp.broadcast_to((perm_ref[...] - scalars[ROW_AT] * rows).astype(F32), (8, rows))[:1]
    vocab = lax.broadcasted_iota(jnp.int32, (side, rows), 0)
    for at, offset in enumerate(offsets):
        base = jnp.bitwise_xor(scalars[COL_AT], offset) * side
        pick[pl.ds(at * side, side), :] = onehot(index == (vocab + base).astype(F32))
    moved = jnp.dot(pick[...], moving, preferred_element_type=F32)
    if exact:
        moved = moved[:, :width] + moved[:, width:]
    out_ref[...] = moved.astype(out_ref.dtype).reshape(out_ref.shape)


def put_rows(scalars, row_perm, grad, offsets, side, exact):
    width = grad.shape[1]
    return pl.pallas_call(
        functools.partial(put_kernel, offsets, exact),
        in_specs=[SCALARS, WHOLE, WHOLE],
        out_specs=WHOLE,
        out_shape=jax.ShapeDtypeStruct((len(offsets), side, width), F32 if exact else BF16),
        scratch_shapes=[pltpu.VMEM((len(offsets) * side, grad.shape[0]), BF16)],
        compiler_params=params(24),
        cost_estimate=cost((4096 if exact and len(offsets) > 1 else 1) * grad.size, grad.size // 16),
        name="put_rows",
    )(scalars, row_perm[None, :], grad)


def swap(value, axis, bit):
    pairs = [(at, at ^ bit) for at in range(lax.axis_size(axis))]
    return lax.ppermute(value, axis, pairs)


def together(values):
    return lax.optimization_barrier(values)


def line_shards(counts, block_mask, row_perm, col_perm, row_logm, col_logm, row_emb, col_emb):
    shard_rows, shard_cols = counts.shape
    side = row_emb.shape[0]
    width = col_emb.shape[0]
    scalars = jnp.stack([lax.axis_index("row"), lax.axis_index("col")]).astype(jnp.int32)

    cross = swap(col_emb, "row", 2)
    near = swap(col_emb, "row", 1)
    count_far, aux_far, shifted, columns, values = order_first(
        scalars, col_perm, block_mask, col_logm, counts, (3,), width
    )
    ordered = functools.partial(order_next, scalars)
    row_block, shifted = together((row_emb, shifted))
    from_x = swap(row_block, "col", 2)
    from_y = swap(row_block, "col", 4)
    from_xy = swap(row_block, "col", 6)
    count_cross, count_near, aux_cross, aux_near = ordered(shifted, columns, values, (2, 1), width)
    cross, near, from_x, from_y, from_xy, count_near, shifted = together(
        (cross, near, from_x, from_y, from_xy, count_near, shifted)
    )
    far = swap(cross, "row", 1)
    from_core = swap(jnp.stack([row_emb, from_x, from_y, from_xy]), "col", 1)
    count_own, aux_own = ordered(shifted, columns, values, (0,), width)
    count_own, row_perm = together((count_own, row_perm))
    blocks = [row_emb, from_x, from_y, from_xy, from_core]
    wvec, turned, logm = take_rows(scalars, row_perm, row_logm, blocks)

    rows_in = (wvec, turned, logm)
    of_far, of_cross = (far, count_far, aux_far), (cross, count_cross, aux_cross)
    of_near, of_own = (near, count_near, aux_near), (col_emb, count_own, aux_own)
    delta_far, sent_0, sent_1 = cells(rows_in, of_far, 2)
    far_0 = swap(sent_0, "row", 1)
    far_1 = swap(sent_1, "row", 1)
    rows_in, delta_far = together((rows_in, delta_far))
    delta_cross, term_cross = cells(rows_in, of_cross, 0)
    rows_in, term_cross, far_0 = together((rows_in, term_cross, far_0))

    half = term_cross.shape[0] // 2
    sum_0 = (term_cross[:half] + far_0.astype(F32)).astype(BF16)
    rows_in, sum_0 = together((rows_in, sum_0))
    cross_0 = swap(sum_0, "row", 2)
    delta_near, sent_near = cells(rows_in, of_near, 1)
    got_near = swap(sent_near, "row", 1)
    others = ((far, delta_far), (cross, delta_cross), (near, delta_near))
    grad, term_own = cells(rows_in, of_own, 0, others)
    grad, far_1, cross_0 = together((grad, far_1, cross_0))
    sum_1 = (term_cross[half:] + far_1.astype(F32)).astype(BF16)
    cross_1 = swap(sum_1, "row", 2)
    grad, sum_1 = together((grad, sum_1))

    ordered = functools.partial(put_rows, scalars, row_perm)
    away = ordered(grad, (1, 3, 5, 7), side, False)
    core = swap(away, "col", 1)
    grad, away = together((grad, away))
    both = ordered(grad, (2, 4, 6), side, True) + core[1:].astype(F32)
    sends = [both[at].astype(BF16) for at in range(3)]
    got = [swap(sends[at], "col", bit) for at, bit in ((1, 4), (2, 6), (0, 2))]
    grad, sends = together((grad, sends))
    home = ordered(grad, (0,), side, True)
    home, term_own = together((home, term_own))
    row_sum = home[0] + core[0].astype(F32)
    for each in got:
        row_sum = row_sum + each.astype(F32)
    row_scale = np.float32(1.0 / np.sqrt(shard_cols * 8))
    col_scale = np.float32(1.0 / np.sqrt(shard_rows * 4))
    return (row_sum * row_scale, finish(col_scale, term_own, got_near, cross_0, cross_1))


def solution(mesh):
    in_specs = (
        P("row", "col"),
        P("row", "col"),
        P("row"),
        P("col"),
        P("row"),
        P("col"),
        P(("row", "col"), None),
        P(("col", "row"), None),
    )
    out_specs = (P(("row", "col"), None), P(("col", "row"), None))
    line = mesh.shape["row"] == 4 and mesh.shape["col"] == 8
    body = line_shards if line else plain_shards
    return jax.shard_map(body, mesh=mesh, in_specs=in_specs, out_specs=out_specs, check_vma=False)
```

```python
import functools

import jax
import jax.numpy as jnp
import numpy as np
from jax import lax
from jax.experimental import pallas as pl
from jax.experimental.pallas import tpu as pltpu
from jax.sharding import PartitionSpec as P

F32 = jnp.float32
BF16 = jnp.bfloat16
LANES = 128
MIB = 1 << 20


def cell_delta(score, count, active, row_part, col_part):
    real_count = count.astype(F32)
    safe = jnp.maximum(real_count, 1.0)
    pmi = jnp.log(safe) - row_part[:, None] - col_part[None, :]
    confid = 0.1 + 0.25 * jnp.sqrt(safe)
    positive = confid * (score - pmi)
    zeroed = jax.nn.sigmoid(score - pmi)
    deriv = jnp.where(count > 0, positive, zeroed)
    return (active.astype(F32) * deriv).astype(BF16)


def plain_shards(counts, block_mask, row_perm, col_perm, row_logm, col_logm, row_emb, col_emb):
    shard_rows, shard_cols = counts.shape
    all_cols = shard_cols * lax.axis_size("col")
    all_rows = shard_rows * lax.axis_size("row")
    block_side = shard_rows // block_mask.shape[0]
    row_group = lax.all_gather(row_emb, "col", axis=0, tiled=True)
    col_group = lax.all_gather(col_emb, "row", axis=0, tiled=True)
    row_local = row_perm - lax.axis_index("row") * shard_rows
    col_local = col_perm - lax.axis_index("col") * shard_cols
    wvec = jnp.take(row_group, row_local, axis=0)
    cvec = jnp.take(col_group, col_local, axis=0)
    score = lax.dot_general(wvec, cvec, (((1,), (1,)), ((), ())), preferred_element_type=F32)
    active = jnp.repeat(jnp.repeat(block_mask, block_side, axis=0), block_side, axis=1)
    delta = cell_delta(score, counts, active, row_logm, col_logm)
    gshard = jnp.dot(delta, cvec, preferred_element_type=F32) / jnp.sqrt(F32(all_cols))
    ordered = jnp.zeros(gshard.shape, F32).at[row_local].set(gshard)
    row_grad = lax.psum_scatter(ordered, "col", scatter_dimension=0, tiled=True)
    hshard = lax.dot_general(
        delta, wvec, (((0,), (0,)), ((), ())), preferred_element_type=F32
    ) / jnp.sqrt(F32(all_rows))
    col_ordered = jnp.zeros(hshard.shape, F32).at[col_local].set(hshard)
    col_grad = lax.psum_scatter(col_ordered, "row", scatter_dimension=0, tiled=True)
    return (row_grad, col_grad)


ROW_AT, COL_AT = 0, 1

WHOLE = pl.BlockSpec(memory_space=pltpu.VMEM)
SCALARS = pl.BlockSpec(memory_space=pltpu.SMEM)


def params(mib):
    return pltpu.CompilerParams(vmem_limit_bytes=mib * MIB)


def cost(flops, moved):
    return pl.CostEstimate(flops=flops, bytes_accessed=moved, transcendentals=0)


def onehot(flag):
    return jnp.where(flag, 1.0, 0.0).astype(BF16)


def pieces_of(value):
    high = value.astype(BF16)
    rest = value - high.astype(F32)
    middle = rest.astype(BF16)
    low = (rest - middle.astype(F32)).astype(BF16)
    return high, middle, low


def along_sublanes(value):
    fill = jnp.zeros((LANES - value.shape[0], LANES), F32)
    return jnp.concatenate([value, fill], axis=0).T


def copies(pairs, sems):
    made = [pltpu.make_async_copy(src, dst, sems.at[at]) for at, (src, dst) in enumerate(pairs)]
    for copy in made:
        copy.start()
    return made


def fill_pick(pick, columns, base, groups):
    vocab = (lax.broadcasted_iota(jnp.int32, (LANES, pick.shape[1]), 1) + base).astype(F32)
    for group in groups:
        pick[pl.ds(group * LANES, LANES), :] = onehot(columns[:, group : group + 1] == vocab)


def chunk_base(scalars, offset, width):
    return jnp.bitwise_xor(scalars[ROW_AT], offset) * width


def move_values(values, pick, aux_ref):
    moved = jnp.dot(values, pick[...], preferred_element_type=F32)
    rows = values.shape[0] - 24
    aux_ref[pl.ds(0, rows), :] = moved[:rows]
    aux_ref[pl.ds(rows, 8), :] = moved[rows : rows + 8] + moved[rows + 8 : rows + 16] + moved[rows + 16 :]


def order_first_kernel(offsets, scalars, perm_hbm, mask_hbm, logm_hbm, count_hbm, *refs):
    parts = len(offsets)
    outs, auxes, refs = refs[:parts], refs[parts : 2 * parts], refs[2 * parts :]
    shifted_ref, columns_ref, values_ref, perm, mask_ref, logm_ref, tiles, pick, sems, tile_sems = refs
    depth = pick.shape[1]
    width = pick.shape[2]
    rows = outs[0].shape[0]
    step = tiles.shape[1]
    steps = rows // step

    slots = tiles.shape[0]

    def tile_copy(at):
        slot = lax.rem(at, slots)
        return pltpu.make_async_copy(
            count_hbm.at[pl.ds(pl.multiple_of(at * step, step), step)], tiles.at[slot], tile_sems.at[slot]
        )

    small = copies([(perm_hbm, perm), (mask_hbm, mask_ref), (logm_hbm, logm_ref)], sems)
    tile_copy(0).start()
    for copy in small:
        copy.wait()
    columns = along_sublanes((perm[...] - scalars[COL_AT] * depth).astype(F32))
    columns_ref[...] = columns
    blocks_r, blocks_c = mask_ref.shape
    mask = mask_ref[...].astype(F32)
    side = (blocks_r, depth // blocks_c)
    active = jnp.concatenate(
        [jnp.broadcast_to(mask[:, at : at + 1], side) for at in range(blocks_c)], axis=1
    )
    logm = jnp.broadcast_to(logm_ref[...], (8, depth))
    values = jnp.concatenate([active, *[piece.astype(F32) for piece in pieces_of(logm)]], axis=0)
    values_ref[...] = values
    values = values.astype(BF16)
    for part, offset in enumerate(offsets):
        fill_pick(pick.at[part], columns, chunk_base(scalars, offset, width), range(depth // LANES))
        move_values(values, pick.at[part], auxes[part])
    tile_copy(1).start()

    @pl.loop(0, steps)
    def _(at):
        here = pl.ds(pl.multiple_of(at * step, step), step)
        tile_copy(at).wait()
        shifted = (tiles[lax.rem(at, slots)] - 256).astype(F32).astype(BF16)
        shifted_ref[here, :] = shifted

        @pl.when(at + slots < steps)
        def _():
            tile_copy(at + slots).start()

        for part in range(parts):
            moved = jnp.dot(shifted, pick[part], preferred_element_type=F32)
            outs[part][here, :] = moved.astype(BF16)


def in_hbm(value):
    return pltpu.with_memory_space_constraint(value, pltpu.HBM)


def order_first(scalars, col_perm, block_mask, col_logm, counts, offsets, width):
    rows, cols = counts.shape
    parts = len(offsets)
    blocks = block_mask.shape[0]
    outside = pl.BlockSpec(memory_space=pltpu.HBM)
    step = 512
    return pl.pallas_call(
        functools.partial(order_first_kernel, offsets),
        in_specs=[SCALARS] + [outside] * 4,
        out_specs=[WHOLE] * (2 * parts + 3),
        out_shape=[jax.ShapeDtypeStruct((rows, width), BF16)] * parts
        + [jax.ShapeDtypeStruct((blocks + 8, width), F32)] * parts
        + [
            jax.ShapeDtypeStruct((rows, cols), BF16),
            jax.ShapeDtypeStruct((LANES, LANES), F32),
            jax.ShapeDtypeStruct((blocks + 24, cols), F32),
        ],
        scratch_shapes=[
            pltpu.VMEM((cols // LANES, LANES), jnp.int32),
            pltpu.VMEM(block_mask.shape, jnp.int32),
            pltpu.VMEM((1, cols), F32),
            pltpu.VMEM((2, step, cols), jnp.int32),
            pltpu.VMEM((parts, cols, width), BF16),
            pltpu.SemaphoreType.DMA((3,)),
            pltpu.SemaphoreType.DMA((2,)),
        ],
        compiler_params=params(28),
        cost_estimate=cost(2 * parts * rows * cols * width, 4 * rows * cols),
        name="order_first",
    )(scalars, *[in_hbm(each) for each in (col_perm.reshape(-1, LANES), block_mask, col_logm[None, :], counts)])


def order_next_kernel(offsets, scalars, shifted_ref, columns_ref, values_ref, *refs):
    parts = len(offsets)
    outs, auxes, pick = refs[:parts], refs[parts : 2 * parts], refs[-1]
    depth, width = pick.shape[1:]
    values = values_ref[...].astype(BF16)
    for part, offset in enumerate(offsets):
        base = chunk_base(scalars, offset, width)
        fill_pick(pick.at[part], columns_ref[...], base, range(depth // LANES))
        move_values(values, pick.at[part], auxes[part])
    step = 512

    @pl.loop(0, shifted_ref.shape[0] // step)
    def _(at):
        here = pl.ds(pl.multiple_of(at * step, step), step)
        for part in range(parts):
            moved = jnp.dot(shifted_ref[here, :], pick[part], preferred_element_type=F32)
            outs[part][here, :] = moved.astype(BF16)


def order_next(scalars, shifted, columns, values, offsets, width):
    rows, cols = shifted.shape
    parts = len(offsets)
    return pl.pallas_call(
        functools.partial(order_next_kernel, offsets),
        in_specs=[SCALARS] + [WHOLE] * 3,
        out_specs=[WHOLE] * (2 * parts),
        out_shape=[jax.ShapeDtypeStruct((rows, width), BF16)] * parts
        + [jax.ShapeDtypeStruct((values.shape[0] - 16, width), F32)] * parts,
        scratch_shapes=[pltpu.VMEM((parts, cols, width), BF16)],
        compiler_params=params(24),
        cost_estimate=cost(rows * width, rows * width),
        name="order_next",
    )(scalars, shifted, columns, values)


def take_kernel(scalars, perm_ref, logm_ref, *refs):
    own, from_x, from_y, from_xy, from_core, out_ref, turned_ref, logm_out, group, pick = refs
    side = own.shape[0]
    mine = [own, from_x, from_y, from_xy]
    blocks = [(2 * at, mine[at]) for at in range(4)] + [(2 * at + 1, from_core.at[at]) for at in range(4)]
    for offset, block in blocks:
        first = pl.multiple_of(jnp.bitwise_xor(scalars[COL_AT], offset) * side, side)
        group[pl.ds(first, side), :] = block[...]
    rows = out_ref.shape[0]
    depth = group.shape[0]
    groups = rows // LANES
    index = (perm_ref[...] - scalars[ROW_AT] * rows).astype(F32)
    columns = along_sublanes(jnp.concatenate([index, logm_ref[...]], axis=0))
    step = pick.shape[1]
    vocab = lax.broadcasted_iota(jnp.int32, (LANES, depth), 1).astype(F32)
    for first in range(0, rows, step):
        slot = (first // step) % pick.shape[0]
        for inner in range(0, step, LANES):
            at = (first + inner) // LANES
            pick[slot, pl.ds(inner, LANES), :] = onehot(columns[:, at : at + 1] == vocab)
            logm_out[pl.ds(first + inner, LANES), :] = jnp.broadcast_to(
                columns[:, groups + at : groups + at + 1], (LANES, LANES)
            )
        taken = jnp.dot(pick[slot], group[...], preferred_element_type=F32).astype(BF16)
        out_ref[pl.ds(first, step), :] = taken
        turned_ref[:, pl.ds(first, step)] = taken.T


def take_rows(scalars, row_perm, row_logm, blocks):
    rows = row_perm.shape[0]
    side, width = blocks[0].shape
    return pl.pallas_call(
        take_kernel,
        in_specs=[SCALARS] + [WHOLE] * 7,
        out_specs=[WHOLE] * 3,
        out_shape=[
            jax.ShapeDtypeStruct((rows, width), BF16),
            jax.ShapeDtypeStruct((width, rows), BF16),
            jax.ShapeDtypeStruct((rows, LANES), F32),
        ],
        scratch_shapes=[pltpu.VMEM((8 * side, width), BF16), pltpu.VMEM((2, 512, 8 * side), BF16)],
        compiler_params=params(24),
        cost_estimate=cost(2 * rows * rows * width, 4 * rows * width),
        name="take_rows",
    )(scalars, row_perm.reshape(-1, LANES), row_logm.reshape(-1, LANES), *blocks)


def cells_kernel(others, pieces, *refs):
    wvec_ref, turned_ref, logm_ref, chunk, count_ref, aux_ref, refs = *refs[:6], refs[6:]
    chunk_refs, delta_refs, refs = refs[:others], refs[others : 2 * others], refs[2 * others :]
    outs = max(len(pieces), 1)
    main_ref, out_refs, refs = refs[0], refs[1 : 1 + outs], refs[1 + outs :]
    chunk_turned, term_ref, refs = refs[0], refs[1], refs[2:]
    chunk_turned[...] = chunk[...].T
    rows = wvec_ref.shape[0]
    width = chunk.shape[0]
    blocks = aux_ref.shape[0] - 8
    tile = rows // blocks
    col_logm = aux_ref[pl.ds(blocks, 1), :]
    if others:
        delta_ref, stack = refs
        for at, ref in enumerate([*chunk_refs, chunk]):
            stack[pl.ds(at * width, width), :] = ref[...]
    else:
        delta_ref = main_ref
    joined = delta_ref.shape[0] // tile
    half = joined // 2

    def part(group):
        def rows_at(at, count=1):
            return pl.ds(pl.multiple_of((group * joined + at) * tile, tile), count * tile)

        def held(at, count=1):
            return delta_ref[pl.ds(at * tile, count * tile), :]

        def score_of(at):
            return jnp.dot(wvec_ref[rows_at(at), :], chunk_turned[...], preferred_element_type=F32)

        def delta_of(at, score):
            here = rows_at(at)
            count = count_ref[here, :].astype(F32) + 256.0
            log = jnp.log(jnp.maximum(count, 1.0))
            row_logm = jnp.concatenate([logm_ref[here, :]] * (width // LANES), axis=1)
            gap = score + ((row_logm + col_logm) - log)
            confid = 0.1 + 0.25 * jnp.exp2(log * np.float32(0.5 / np.log(2.0)))
            zeroed = 0.5 * jnp.tanh(0.5 * gap) + 0.5
            deriv = jnp.where(count > 0.0, confid * gap, zeroed)
            active = aux_ref[pl.ds(group * joined + at, 1), :]
            delta_ref[pl.ds(at * tile, tile), :] = (deriv * active).astype(BF16)

        def grad_of(at, count):
            here = rows_at(at, count)
            deltas = jnp.concatenate([ref[here, :] for ref in delta_refs] + [held(at, count)], axis=1)
            main_ref[here, :] = jnp.dot(deltas, stack[...], preferred_element_type=F32)

        def term_of(at):
            turned = turned_ref[:, rows_at(at, half)]
            term = jnp.dot(turned, held(at, half), preferred_element_type=F32)
            if joined < blocks or at:
                term = term_ref[...] + term
            term_ref[...] = term

        ahead = score_of(0)
        for at in range(joined):
            score = ahead
            if at + 1 < joined:
                ahead = score_of(at + 1)
            delta_of(at, score)
            if at == half:
                term_of(0)
                if others:
                    grad_of(0, half)
        term_of(half)
        if others:
            grad_of(half, half)

    if joined < blocks:
        term_ref[...] = jnp.zeros_like(term_ref)
        pl.loop(0, blocks // joined)(part)
    else:
        part(0)
    first = 0
    for out_ref in out_refs:
        out_ref[...] = term_ref[pl.ds(first, out_ref.shape[0]), :].astype(out_ref.dtype)
        first += out_ref.shape[0]


def cells(rows_in, chunk, pieces=(), others=()):
    wvec = rows_in[0]
    rows, depth = wvec.shape
    width = chunk[0].shape[0]
    args = [*rows_in, *chunk, *[each for each, _ in others], *[delta for _, delta in others]]
    if others:
        main = jax.ShapeDtypeStruct((rows, depth), F32)
        scratch = [pltpu.VMEM((rows // 2, width), BF16), pltpu.VMEM(((len(others) + 1) * width, depth), BF16)]
    else:
        main = jax.ShapeDtypeStruct((rows, width), BF16)
        scratch = []
    if pieces:
        outs = [jax.ShapeDtypeStruct((size, width), BF16) for size in pieces]
    else:
        outs = [jax.ShapeDtypeStruct((depth, width), F32)]
    return pl.pallas_call(
        functools.partial(cells_kernel, len(others), pieces),
        in_specs=[WHOLE] * len(args),
        out_specs=[WHOLE] * (1 + len(outs)),
        out_shape=[main, *outs],
        scratch_shapes=[pltpu.VMEM((depth, width), BF16), pltpu.VMEM((depth, width), F32), *scratch],
        compiler_params=params(24),
        cost_estimate=cost(rows * width, rows * depth),
        name="cells",
    )(*args)


def finish_kernel(scale, *refs):
    own_ref, near_ref, cross_refs, out_ref, sum_ref = refs[0], refs[1], refs[2:-2], refs[-2], refs[-1]
    first = 0
    for cross_ref in cross_refs:
        here = pl.ds(first, cross_ref.shape[0])
        first += cross_ref.shape[0]
        total = own_ref[here, :] + near_ref[here, :].astype(F32) + cross_ref[...].astype(F32)
        sum_ref[here, :] = total * scale
    out_ref[...] = sum_ref[...].T


def finish(scale, own, near, *crosses):
    return pl.pallas_call(
        functools.partial(finish_kernel, scale),
        in_specs=[WHOLE] * (2 + len(crosses)),
        out_specs=WHOLE,
        out_shape=jax.ShapeDtypeStruct(own.shape[::-1], F32),
        scratch_shapes=[pltpu.VMEM(own.shape, F32)],
        compiler_params=params(8),
        cost_estimate=cost(own.size, own.size // 16),
        name="finish",
    )(own, near, *crosses)


def put_kernel(offsets, exact, scalars, perm_ref, grad_ref, out_ref, pick):
    grad = grad_ref[...]
    rows, width = grad.shape
    high = grad.astype(BF16)
    moving = high
    if exact:
        moving = jnp.concatenate([high, (grad - high.astype(F32)).astype(BF16)], axis=1)
    side = out_ref.shape[1]
    index = jnp.broadcast_to((perm_ref[...] - scalars[ROW_AT] * rows).astype(F32), (8, rows))[:1]
    vocab = lax.broadcasted_iota(jnp.int32, (side, rows), 0)
    for at, offset in enumerate(offsets):
        base = jnp.bitwise_xor(scalars[COL_AT], offset) * side
        pick[pl.ds(at * side, side), :] = onehot(index == (vocab + base).astype(F32))
    moved = jnp.dot(pick[...], moving, preferred_element_type=F32)
    if exact:
        moved = moved[:, :width] + moved[:, width:]
    out_ref[...] = moved.astype(out_ref.dtype).reshape(out_ref.shape)


def put_rows(scalars, row_perm, grad, offsets, side, exact):
    width = grad.shape[1]
    return pl.pallas_call(
        functools.partial(put_kernel, offsets, exact),
        in_specs=[SCALARS, WHOLE, WHOLE],
        out_specs=WHOLE,
        out_shape=jax.ShapeDtypeStruct((len(offsets), side, width), F32 if exact else BF16),
        scratch_shapes=[pltpu.VMEM((len(offsets) * side, grad.shape[0]), BF16)],
        compiler_params=params(24),
        cost_estimate=cost((4096 if exact and len(offsets) > 1 else 1) * grad.size, grad.size // 16),
        name="put_rows",
    )(scalars, row_perm[None, :], grad)


def swap(value, axis, bit):
    pairs = [(at, at ^ bit) for at in range(lax.axis_size(axis))]
    return lax.ppermute(value, axis, pairs)


def together(values):
    return lax.optimization_barrier(values)


def line_shards(counts, block_mask, row_perm, col_perm, row_logm, col_logm, row_emb, col_emb):
    shard_rows, shard_cols = counts.shape
    side = row_emb.shape[0]
    width = col_emb.shape[0]
    scalars = jnp.stack([lax.axis_index("row"), lax.axis_index("col")]).astype(jnp.int32)

    cross = swap(col_emb, "row", 2)
    near = swap(col_emb, "row", 1)
    count_far, aux_far, shifted, columns, values = order_first(
        scalars, col_perm, block_mask, col_logm, counts, (3,), width
    )
    ordered = functools.partial(order_next, scalars)
    row_block, shifted = together((row_emb, shifted))
    from_x = swap(row_block, "col", 2)
    from_y = swap(row_block, "col", 4)
    from_xy = swap(row_block, "col", 6)
    count_cross, count_near, aux_cross, aux_near = ordered(shifted, columns, values, (2, 1), width)
    cross, near, from_x, from_y, from_xy, count_near, shifted = together(
        (cross, near, from_x, from_y, from_xy, count_near, shifted)
    )
    far = swap(cross, "row", 1)
    from_core = swap(jnp.stack([row_emb, from_x, from_y, from_xy]), "col", 1)
    count_own, aux_own = ordered(shifted, columns, values, (0,), width)
    count_own, row_perm = together((count_own, row_perm))
    blocks = [row_emb, from_x, from_y, from_xy, from_core]
    wvec, turned, logm = take_rows(scalars, row_perm, row_logm, blocks)

    rows_in = (wvec, turned, logm)
    of_far, of_cross = (far, count_far, aux_far), (cross, count_cross, aux_cross)
    of_near, of_own = (near, count_near, aux_near), (col_emb, count_own, aux_own)
    depth = col_emb.shape[1]
    early = depth * 5 // 16
    delta_far, sent_0, sent_1 = cells(rows_in, of_far, (early, depth - early))
    far_0 = swap(sent_0, "row", 1)
    far_1 = swap(sent_1, "row", 1)
    rows_in, delta_far = together((rows_in, delta_far))
    delta_cross, term_cross = cells(rows_in, of_cross)
    rows_in, delta_cross = together((rows_in, delta_cross))
    delta_near, sent_near = cells(rows_in, of_near, (depth,))
    got_near = swap(sent_near, "row", 1)
    rows_in, delta_near, far_0 = together((rows_in, delta_near, far_0))

    sum_0 = (term_cross[:early] + far_0.astype(F32)).astype(BF16)
    rows_in, sum_0 = together((rows_in, sum_0))
    cross_0 = swap(sum_0, "row", 2)
    others = ((far, delta_far), (cross, delta_cross), (near, delta_near))
    grad, term_own = cells(rows_in, of_own, (), others)
    grad, far_1, cross_0 = together((grad, far_1, cross_0))
    sum_1 = (term_cross[early:] + far_1.astype(F32)).astype(BF16)
    cross_1 = swap(sum_1, "row", 2)
    grad, sum_1 = together((grad, sum_1))

    ordered = functools.partial(put_rows, scalars, row_perm)
    away = ordered(grad, (1, 3, 5, 7), side, False)
    core = swap(away, "col", 1)
    grad, away = together((grad, away))
    both = ordered(grad, (2, 4, 6), side, True) + core[1:].astype(F32)
    sends = [both[at].astype(BF16) for at in range(3)]
    got = [swap(sends[at], "col", bit) for at, bit in ((1, 4), (2, 6), (0, 2))]
    grad, sends = together((grad, sends))
    home = ordered(grad, (0,), side, True)
    home, term_own = together((home, term_own))
    row_sum = home[0] + core[0].astype(F32)
    for each in got:
        row_sum = row_sum + each.astype(F32)
    row_scale = np.float32(1.0 / np.sqrt(shard_cols * 8))
    col_scale = np.float32(1.0 / np.sqrt(shard_rows * 4))
    return (row_sum * row_scale, finish(col_scale, term_own, got_near, cross_0, cross_1))


def solution(mesh):
    in_specs = (
        P("row", "col"),
        P("row", "col"),
        P("row"),
        P("col"),
        P("row"),
        P("col"),
        P(("row", "col"), None),
        P(("col", "row"), None),
    )
    out_specs = (P(("row", "col"), None), P(("col", "row"), None))
    line = mesh.shape["row"] == 4 and mesh.shape["col"] == 8
    body = line_shards if line else plain_shards
    return jax.shard_map(body, mesh=mesh, in_specs=in_specs, out_specs=out_specs, check_vma=False)
```

```python
import functools

import jax
import jax.numpy as jnp
import numpy as np
from jax import lax
from jax.experimental import pallas as pl
from jax.experimental.pallas import tpu as pltpu
from jax.sharding import PartitionSpec as P

F32 = jnp.float32
BF16 = jnp.bfloat16
LANES = 128
MIB = 1 << 20


def cell_delta(score, count, active, row_part, col_part):
    real_count = count.astype(F32)
    safe = jnp.maximum(real_count, 1.0)
    pmi = jnp.log(safe) - row_part[:, None] - col_part[None, :]
    confid = 0.1 + 0.25 * jnp.sqrt(safe)
    positive = confid * (score - pmi)
    zeroed = jax.nn.sigmoid(score - pmi)
    deriv = jnp.where(count > 0, positive, zeroed)
    return (active.astype(F32) * deriv).astype(BF16)


def plain_shards(counts, block_mask, row_perm, col_perm, row_logm, col_logm, row_emb, col_emb):
    shard_rows, shard_cols = counts.shape
    all_cols = shard_cols * lax.axis_size("col")
    all_rows = shard_rows * lax.axis_size("row")
    block_side = shard_rows // block_mask.shape[0]
    row_group = lax.all_gather(row_emb, "col", axis=0, tiled=True)
    col_group = lax.all_gather(col_emb, "row", axis=0, tiled=True)
    row_local = row_perm - lax.axis_index("row") * shard_rows
    col_local = col_perm - lax.axis_index("col") * shard_cols
    wvec = jnp.take(row_group, row_local, axis=0)
    cvec = jnp.take(col_group, col_local, axis=0)
    score = lax.dot_general(wvec, cvec, (((1,), (1,)), ((), ())), preferred_element_type=F32)
    active = jnp.repeat(jnp.repeat(block_mask, block_side, axis=0), block_side, axis=1)
    delta = cell_delta(score, counts, active, row_logm, col_logm)
    gshard = jnp.dot(delta, cvec, preferred_element_type=F32) / jnp.sqrt(F32(all_cols))
    ordered = jnp.zeros(gshard.shape, F32).at[row_local].set(gshard)
    row_grad = lax.psum_scatter(ordered, "col", scatter_dimension=0, tiled=True)
    hshard = lax.dot_general(
        delta, wvec, (((0,), (0,)), ((), ())), preferred_element_type=F32
    ) / jnp.sqrt(F32(all_rows))
    col_ordered = jnp.zeros(hshard.shape, F32).at[col_local].set(hshard)
    col_grad = lax.psum_scatter(col_ordered, "row", scatter_dimension=0, tiled=True)
    return (row_grad, col_grad)


ROW_AT, COL_AT = 0, 1

WHOLE = pl.BlockSpec(memory_space=pltpu.VMEM)
SCALARS = pl.BlockSpec(memory_space=pltpu.SMEM)


def params(mib):
    return pltpu.CompilerParams(vmem_limit_bytes=mib * MIB)


def cost(flops, moved):
    return pl.CostEstimate(flops=flops, bytes_accessed=moved, transcendentals=0)


def onehot(flag):
    return jnp.where(flag, 1.0, 0.0).astype(BF16)


def pieces_of(value):
    high = value.astype(BF16)
    rest = value - high.astype(F32)
    middle = rest.astype(BF16)
    low = (rest - middle.astype(F32)).astype(BF16)
    return high, middle, low


def along_sublanes(value):
    fill = jnp.zeros((LANES - value.shape[0], LANES), F32)
    return jnp.concatenate([value, fill], axis=0).T


def copies(pairs, sems):
    made = [pltpu.make_async_copy(src, dst, sems.at[at]) for at, (src, dst) in enumerate(pairs)]
    for copy in made:
        copy.start()
    return made


def fill_pick(pick, columns, base, groups):
    vocab = (lax.broadcasted_iota(jnp.int32, (LANES, pick.shape[1]), 1) + base).astype(F32)
    for group in groups:
        pick[pl.ds(group * LANES, LANES), :] = onehot(columns[:, group : group + 1] == vocab)


def chunk_base(scalars, offset, width):
    return jnp.bitwise_xor(scalars[ROW_AT], offset) * width


def move_values(values, pick, aux_ref):
    moved = jnp.dot(values, pick[...], preferred_element_type=F32)
    rows = values.shape[0] - 24
    aux_ref[pl.ds(0, rows), :] = moved[:rows]
    aux_ref[pl.ds(rows, 8), :] = moved[rows : rows + 8] + moved[rows + 8 : rows + 16] + moved[rows + 16 :]


def order_first_kernel(offsets, scalars, perm_hbm, mask_hbm, logm_hbm, count_hbm, *refs):
    parts = len(offsets)
    outs, auxes, refs = refs[:parts], refs[parts : 2 * parts], refs[2 * parts :]
    shifted_ref, columns_ref, values_ref, perm, mask_ref, logm_ref, tiles, pick, sems, tile_sems = refs
    depth = pick.shape[1]
    width = pick.shape[2]
    rows = outs[0].shape[0]
    step = tiles.shape[1]
    steps = rows // step

    slots = tiles.shape[0]

    def tile_copy(at):
        slot = lax.rem(at, slots)
        return pltpu.make_async_copy(
            count_hbm.at[pl.ds(pl.multiple_of(at * step, step), step)], tiles.at[slot], tile_sems.at[slot]
        )

    small = copies([(perm_hbm, perm), (mask_hbm, mask_ref), (logm_hbm, logm_ref)], sems)
    tile_copy(0).start()
    for copy in small:
        copy.wait()
    columns = along_sublanes((perm[...] - scalars[COL_AT] * depth).astype(F32))
    columns_ref[...] = columns
    blocks_r, blocks_c = mask_ref.shape
    mask = mask_ref[...].astype(F32)
    side = (blocks_r, depth // blocks_c)
    active = jnp.concatenate(
        [jnp.broadcast_to(mask[:, at : at + 1], side) for at in range(blocks_c)], axis=1
    )
    logm = jnp.broadcast_to(logm_ref[...], (8, depth))
    values = jnp.concatenate([active, *[piece.astype(F32) for piece in pieces_of(logm)]], axis=0)
    values_ref[...] = values
    values = values.astype(BF16)
    for part, offset in enumerate(offsets):
        fill_pick(pick.at[part], columns, chunk_base(scalars, offset, width), range(depth // LANES))
        move_values(values, pick.at[part], auxes[part])
    tile_copy(1).start()

    @pl.loop(0, steps)
    def _(at):
        here = pl.ds(pl.multiple_of(at * step, step), step)
        tile_copy(at).wait()
        shifted = (tiles[lax.rem(at, slots)] - 256).astype(F32).astype(BF16)
        shifted_ref[here, :] = shifted

        @pl.when(at + slots < steps)
        def _():
            tile_copy(at + slots).start()

        for part in range(parts):
            moved = jnp.dot(shifted, pick[part], preferred_element_type=F32)
            outs[part][here, :] = moved.astype(BF16)


def in_hbm(value):
    return pltpu.with_memory_space_constraint(value, pltpu.HBM)


def order_first(scalars, col_perm, block_mask, col_logm, counts, offsets, width):
    rows, cols = counts.shape
    parts = len(offsets)
    blocks = block_mask.shape[0]
    outside = pl.BlockSpec(memory_space=pltpu.HBM)
    step = 512
    return pl.pallas_call(
        functools.partial(order_first_kernel, offsets),
        in_specs=[SCALARS] + [outside] * 4,
        out_specs=[WHOLE] * (2 * parts + 3),
        out_shape=[jax.ShapeDtypeStruct((rows, width), BF16)] * parts
        + [jax.ShapeDtypeStruct((blocks + 8, width), F32)] * parts
        + [
            jax.ShapeDtypeStruct((rows, cols), BF16),
            jax.ShapeDtypeStruct((LANES, LANES), F32),
            jax.ShapeDtypeStruct((blocks + 24, cols), F32),
        ],
        scratch_shapes=[
            pltpu.VMEM((cols // LANES, LANES), jnp.int32),
            pltpu.VMEM(block_mask.shape, jnp.int32),
            pltpu.VMEM((1, cols), F32),
            pltpu.VMEM((2, step, cols), jnp.int32),
            pltpu.VMEM((parts, cols, width), BF16),
            pltpu.SemaphoreType.DMA((3,)),
            pltpu.SemaphoreType.DMA((2,)),
        ],
        compiler_params=params(28),
        cost_estimate=cost(2 * parts * rows * cols * width, 4 * rows * cols),
        name="order_first",
    )(scalars, *[in_hbm(each) for each in (col_perm.reshape(-1, LANES), block_mask, col_logm[None, :], counts)])


def order_next_kernel(offsets, scalars, shifted_ref, columns_ref, values_ref, *refs):
    parts = len(offsets)
    outs, auxes, pick = refs[:parts], refs[parts : 2 * parts], refs[-1]
    depth, width = pick.shape[1:]
    values = values_ref[...].astype(BF16)
    for part, offset in enumerate(offsets):
        base = chunk_base(scalars, offset, width)
        fill_pick(pick.at[part], columns_ref[...], base, range(depth // LANES))
        move_values(values, pick.at[part], auxes[part])
    step = 512

    @pl.loop(0, shifted_ref.shape[0] // step)
    def _(at):
        here = pl.ds(pl.multiple_of(at * step, step), step)
        for part in range(parts):
            moved = jnp.dot(shifted_ref[here, :], pick[part], preferred_element_type=F32)
            outs[part][here, :] = moved.astype(BF16)


def order_next(scalars, shifted, columns, values, offsets, width):
    rows, cols = shifted.shape
    parts = len(offsets)
    return pl.pallas_call(
        functools.partial(order_next_kernel, offsets),
        in_specs=[SCALARS] + [WHOLE] * 3,
        out_specs=[WHOLE] * (2 * parts),
        out_shape=[jax.ShapeDtypeStruct((rows, width), BF16)] * parts
        + [jax.ShapeDtypeStruct((values.shape[0] - 16, width), F32)] * parts,
        scratch_shapes=[pltpu.VMEM((parts, cols, width), BF16)],
        compiler_params=params(24),
        cost_estimate=cost(rows * width, rows * width),
        name="order_next",
    )(scalars, shifted, columns, values)


def take_kernel(scalars, perm_ref, logm_ref, *refs):
    own, from_x, from_y, from_xy, from_core, out_ref, turned_ref, logm_out, group, pick = refs
    side = own.shape[0]
    mine = [own, from_x, from_y, from_xy]
    blocks = [(2 * at, mine[at]) for at in range(4)] + [(2 * at + 1, from_core.at[at]) for at in range(4)]
    for offset, block in blocks:
        first = pl.multiple_of(jnp.bitwise_xor(scalars[COL_AT], offset) * side, side)
        group[pl.ds(first, side), :] = block[...]
    rows = out_ref.shape[0]
    depth = group.shape[0]
    groups = rows // LANES
    index = (perm_ref[...] - scalars[ROW_AT] * rows).astype(F32)
    columns = along_sublanes(jnp.concatenate([index, logm_ref[...]], axis=0))
    step = pick.shape[1]
    vocab = lax.broadcasted_iota(jnp.int32, (LANES, depth), 1).astype(F32)
    for first in range(0, rows, step):
        slot = (first // step) % pick.shape[0]
        for inner in range(0, step, LANES):
            at = (first + inner) // LANES
            pick[slot, pl.ds(inner, LANES), :] = onehot(columns[:, at : at + 1] == vocab)
            logm_out[pl.ds(first + inner, LANES), :] = jnp.broadcast_to(
                columns[:, groups + at : groups + at + 1], (LANES, LANES)
            )
        taken = jnp.dot(pick[slot], group[...], preferred_element_type=F32).astype(BF16)
        out_ref[pl.ds(first, step), :] = taken
        turned_ref[:, pl.ds(first, step)] = taken.T


def take_rows(scalars, row_perm, row_logm, blocks):
    rows = row_perm.shape[0]
    side, width = blocks[0].shape
    return pl.pallas_call(
        take_kernel,
        in_specs=[SCALARS] + [WHOLE] * 7,
        out_specs=[WHOLE] * 3,
        out_shape=[
            jax.ShapeDtypeStruct((rows, width), BF16),
            jax.ShapeDtypeStruct((width, rows), BF16),
            jax.ShapeDtypeStruct((rows, LANES), F32),
        ],
        scratch_shapes=[pltpu.VMEM((8 * side, width), BF16), pltpu.VMEM((2, 512, 8 * side), BF16)],
        compiler_params=params(24),
        cost_estimate=cost(2 * rows * rows * width, 4 * rows * width),
        name="take_rows",
    )(scalars, row_perm.reshape(-1, LANES), row_logm.reshape(-1, LANES), *blocks)


def cells_kernel(others, pieces, *refs):
    wvec_ref, turned_ref, logm_ref, chunk, count_ref, aux_ref, refs = *refs[:6], refs[6:]
    chunk_refs, delta_refs, refs = refs[:others], refs[others : 2 * others], refs[2 * others :]
    outs = max(len(pieces), 1)
    main_ref, out_refs, refs = refs[0], refs[1 : 1 + outs], refs[1 + outs :]
    chunk_turned, term_ref, refs = refs[0], refs[1], refs[2:]
    chunk_turned[...] = chunk[...].T
    rows = wvec_ref.shape[0]
    width = chunk.shape[0]
    blocks = aux_ref.shape[0] - 8
    tile = rows // blocks
    col_logm = aux_ref[pl.ds(blocks, 1), :]
    if others:
        delta_ref, stack = refs
        for at, ref in enumerate([*chunk_refs, chunk]):
            stack[pl.ds(at * width, width), :] = ref[...]
    else:
        delta_ref = main_ref
    joined = delta_ref.shape[0] // tile
    half = joined // 2

    def part(group):
        def rows_at(at, count=1):
            return pl.ds(pl.multiple_of((group * joined + at) * tile, tile), count * tile)

        def held(at, count=1):
            return delta_ref[pl.ds(at * tile, count * tile), :]

        def score_of(at):
            return jnp.dot(wvec_ref[rows_at(at), :], chunk_turned[...], preferred_element_type=F32)

        def delta_of(at, score):
            here = rows_at(at)
            count = count_ref[here, :].astype(F32) + 256.0
            log = jnp.log(jnp.maximum(count, 1.0))
            row_logm = jnp.concatenate([logm_ref[here, :]] * (width // LANES), axis=1)
            gap = score + ((row_logm + col_logm) - log)
            confid = 0.1 + 0.25 * jnp.exp2(log * np.float32(0.5 / np.log(2.0)))
            zeroed = 0.5 * jnp.tanh(0.5 * gap) + 0.5
            deriv = jnp.where(count > 0.0, confid * gap, zeroed)
            active = aux_ref[pl.ds(group * joined + at, 1), :]
            delta_ref[pl.ds(at * tile, tile), :] = (deriv * active).astype(BF16)

        def grad_of(at, count):
            here = rows_at(at, count)
            deltas = jnp.concatenate([ref[here, :] for ref in delta_refs] + [held(at, count)], axis=1)
            main_ref[here, :] = jnp.dot(deltas, stack[...], preferred_element_type=F32)

        def term_of(at):
            turned = turned_ref[:, rows_at(at, half)]
            term = jnp.dot(turned, held(at, half), preferred_element_type=F32)
            if joined < blocks or at:
                term = term_ref[...] + term
            term_ref[...] = term

        ahead = score_of(0)
        for at in range(joined):
            score = ahead
            if at + 1 < joined:
                ahead = score_of(at + 1)
            delta_of(at, score)
            if at == half:
                term_of(0)
                if others:
                    grad_of(0, half)
        term_of(half)
        if others:
            grad_of(half, half)

    if joined < blocks:
        term_ref[...] = jnp.zeros_like(term_ref)
        pl.loop(0, blocks // joined)(part)
    else:
        part(0)
    first = 0
    for out_ref in out_refs:
        out_ref[...] = term_ref[pl.ds(first, out_ref.shape[0]), :].astype(out_ref.dtype)
        first += out_ref.shape[0]


def cells(rows_in, chunk, pieces=(), others=()):
    wvec = rows_in[0]
    rows, depth = wvec.shape
    width = chunk[0].shape[0]
    args = [*rows_in, *chunk, *[each for each, _ in others], *[delta for _, delta in others]]
    if others:
        main = jax.ShapeDtypeStruct((rows, depth), F32)
        scratch = [pltpu.VMEM((rows // 2, width), BF16), pltpu.VMEM(((len(others) + 1) * width, depth), BF16)]
    else:
        main = jax.ShapeDtypeStruct((rows, width), BF16)
        scratch = []
    if pieces:
        outs = [jax.ShapeDtypeStruct((size, width), BF16) for size in pieces]
    else:
        outs = [jax.ShapeDtypeStruct((depth, width), F32)]
    return pl.pallas_call(
        functools.partial(cells_kernel, len(others), pieces),
        in_specs=[WHOLE] * len(args),
        out_specs=[WHOLE] * (1 + len(outs)),
        out_shape=[main, *outs],
        scratch_shapes=[pltpu.VMEM((depth, width), BF16), pltpu.VMEM((depth, width), F32), *scratch],
        compiler_params=params(24),
        cost_estimate=cost(rows, rows),
        name="cells",
    )(*args)


def finish_kernel(scale, *refs):
    own_ref, near_ref, cross_refs, out_ref, sum_ref = refs[0], refs[1], refs[2:-2], refs[-2], refs[-1]
    first = 0
    for cross_ref in cross_refs:
        here = pl.ds(first, cross_ref.shape[0])
        first += cross_ref.shape[0]
        total = own_ref[here, :] + near_ref[here, :].astype(F32) + cross_ref[...].astype(F32)
        sum_ref[here, :] = total * scale
    out_ref[...] = sum_ref[...].T


def finish(scale, own, near, *crosses):
    return pl.pallas_call(
        functools.partial(finish_kernel, scale),
        in_specs=[WHOLE] * (2 + len(crosses)),
        out_specs=WHOLE,
        out_shape=jax.ShapeDtypeStruct(own.shape[::-1], F32),
        scratch_shapes=[pltpu.VMEM(own.shape, F32)],
        compiler_params=params(8),
        cost_estimate=cost(own.size, own.size // 16),
        name="finish",
    )(own, near, *crosses)


def put_kernel(offsets, exact, scalars, perm_ref, grad_ref, out_ref, pick):
    grad = grad_ref[...]
    rows, width = grad.shape
    high = grad.astype(BF16)
    moving = high
    if exact:
        moving = jnp.concatenate([high, (grad - high.astype(F32)).astype(BF16)], axis=1)
    side = out_ref.shape[1]
    index = jnp.broadcast_to((perm_ref[...] - scalars[ROW_AT] * rows).astype(F32), (8, rows))[:1]
    vocab = lax.broadcasted_iota(jnp.int32, (side, rows), 0)
    for at, offset in enumerate(offsets):
        base = jnp.bitwise_xor(scalars[COL_AT], offset) * side
        pick[pl.ds(at * side, side), :] = onehot(index == (vocab + base).astype(F32))
    moved = jnp.dot(pick[...], moving, preferred_element_type=F32)
    if exact:
        moved = moved[:, :width] + moved[:, width:]
    out_ref[...] = moved.astype(out_ref.dtype).reshape(out_ref.shape)


def put_rows(scalars, row_perm, grad, offsets, side, exact):
    width = grad.shape[1]
    return pl.pallas_call(
        functools.partial(put_kernel, offsets, exact),
        in_specs=[SCALARS, WHOLE, WHOLE],
        out_specs=WHOLE,
        out_shape=jax.ShapeDtypeStruct((len(offsets), side, width), F32 if exact else BF16),
        scratch_shapes=[pltpu.VMEM((len(offsets) * side, grad.shape[0]), BF16)],
        compiler_params=params(24),
        cost_estimate=cost((16384 if exact and len(offsets) > 1 else 1) * grad.size, grad.size // 16),
        name="put_rows",
    )(scalars, row_perm[None, :], grad)


def swap(value, axis, bit):
    pairs = [(at, at ^ bit) for at in range(lax.axis_size(axis))]
    return lax.ppermute(value, axis, pairs)


def together(values):
    return lax.optimization_barrier(values)


def line_shards(counts, block_mask, row_perm, col_perm, row_logm, col_logm, row_emb, col_emb):
    shard_rows, shard_cols = counts.shape
    side = row_emb.shape[0]
    width = col_emb.shape[0]
    scalars = jnp.stack([lax.axis_index("row"), lax.axis_index("col")]).astype(jnp.int32)

    cross = swap(col_emb, "row", 2)
    near = swap(col_emb, "row", 1)
    count_far, aux_far, shifted, columns, values = order_first(
        scalars, col_perm, block_mask, col_logm, counts, (3,), width
    )
    ordered = functools.partial(order_next, scalars)
    row_block, shifted = together((row_emb, shifted))
    from_x = swap(row_block, "col", 2)
    from_y = swap(row_block, "col", 4)
    from_xy = swap(row_block, "col", 6)
    count_cross, count_near, aux_cross, aux_near = ordered(shifted, columns, values, (2, 1), width)
    cross, near, from_x, from_y, from_xy, count_near, shifted = together(
        (cross, near, from_x, from_y, from_xy, count_near, shifted)
    )
    far = swap(cross, "row", 1)
    from_core = swap(jnp.stack([row_emb, from_x, from_y, from_xy]), "col", 1)
    count_own, aux_own = ordered(shifted, columns, values, (0,), width)
    count_own, row_perm = together((count_own, row_perm))
    blocks = [row_emb, from_x, from_y, from_xy, from_core]
    wvec, turned, logm = take_rows(scalars, row_perm, row_logm, blocks)

    rows_in = (wvec, turned, logm)
    of_far, of_cross = (far, count_far, aux_far), (cross, count_cross, aux_cross)
    of_near, of_own = (near, count_near, aux_near), (col_emb, count_own, aux_own)
    depth = col_emb.shape[1]
    early = depth * 5 // 16
    delta_far, sent_0, sent_1 = cells(rows_in, of_far, (early, depth - early))
    far_0 = swap(sent_0, "row", 1)
    far_1 = swap(sent_1, "row", 1)
    rows_in, delta_far = together((rows_in, delta_far))
    delta_cross, term_cross = cells(rows_in, of_cross)
    rows_in, delta_cross = together((rows_in, delta_cross))
    delta_near, sent_near = cells(rows_in, of_near, (depth,))
    got_near = swap(sent_near, "row", 1)
    rows_in, delta_near, far_0 = together((rows_in, delta_near, far_0))

    sum_0 = (term_cross[:early] + far_0.astype(F32)).astype(BF16)
    rows_in, sum_0 = together((rows_in, sum_0))
    cross_0 = swap(sum_0, "row", 2)
    others = ((far, delta_far), (cross, delta_cross), (near, delta_near))
    grad, term_own = cells(rows_in, of_own, (), others)
    grad, far_1, cross_0 = together((grad, far_1, cross_0))
    sum_1 = (term_cross[early:] + far_1.astype(F32)).astype(BF16)
    cross_1 = swap(sum_1, "row", 2)
    grad, sum_1 = together((grad, sum_1))

    ordered = functools.partial(put_rows, scalars, row_perm)
    away = ordered(grad, (1, 3, 5, 7), side, False)
    core = swap(away, "col", 1)
    grad, away, got_near = together((grad, away, got_near))
    both = ordered(grad, (2, 4, 6), side, True) + core[1:].astype(F32)
    sends = [both[at].astype(BF16) for at in range(3)]
    got = [swap(sends[at], "col", bit) for at, bit in ((1, 4), (2, 6), (0, 2))]
    grad, sends = together((grad, sends))
    home = ordered(grad, (0,), side, True)
    home, term_own = together((home, term_own))
    row_sum = home[0] + core[0].astype(F32)
    for each in got:
        row_sum = row_sum + each.astype(F32)
    row_scale = np.float32(1.0 / np.sqrt(shard_cols * 8))
    col_scale = np.float32(1.0 / np.sqrt(shard_rows * 4))
    return (row_sum * row_scale, finish(col_scale, term_own, got_near, cross_0, cross_1))


def solution(mesh):
    in_specs = (
        P("row", "col"),
        P("row", "col"),
        P("row"),
        P("col"),
        P("row"),
        P("col"),
        P(("row", "col"), None),
        P(("col", "row"), None),
    )
    out_specs = (P(("row", "col"), None), P(("col", "row"), None))
    line = mesh.shape["row"] == 4 and mesh.shape["col"] == 8
    body = line_shards if line else plain_shards
    return jax.shard_map(body, mesh=mesh, in_specs=in_specs, out_specs=out_specs, check_vma=False)
```

```python
import functools

import jax
import jax.numpy as jnp
import numpy as np
from jax import lax
from jax.experimental import pallas as pl
from jax.experimental.pallas import tpu as pltpu
from jax.sharding import PartitionSpec as P

F32 = jnp.float32
BF16 = jnp.bfloat16
LANES = 128
MIB = 1 << 20


def cell_delta(score, count, active, row_part, col_part):
    real_count = count.astype(F32)
    safe = jnp.maximum(real_count, 1.0)
    pmi = jnp.log(safe) - row_part[:, None] - col_part[None, :]
    confid = 0.1 + 0.25 * jnp.sqrt(safe)
    positive = confid * (score - pmi)
    zeroed = jax.nn.sigmoid(score - pmi)
    deriv = jnp.where(count > 0, positive, zeroed)
    return (active.astype(F32) * deriv).astype(BF16)


def plain_shards(counts, block_mask, row_perm, col_perm, row_logm, col_logm, row_emb, col_emb):
    shard_rows, shard_cols = counts.shape
    all_cols = shard_cols * lax.axis_size("col")
    all_rows = shard_rows * lax.axis_size("row")
    block_side = shard_rows // block_mask.shape[0]
    row_group = lax.all_gather(row_emb, "col", axis=0, tiled=True)
    col_group = lax.all_gather(col_emb, "row", axis=0, tiled=True)
    row_local = row_perm - lax.axis_index("row") * shard_rows
    col_local = col_perm - lax.axis_index("col") * shard_cols
    wvec = jnp.take(row_group, row_local, axis=0)
    cvec = jnp.take(col_group, col_local, axis=0)
    score = lax.dot_general(wvec, cvec, (((1,), (1,)), ((), ())), preferred_element_type=F32)
    active = jnp.repeat(jnp.repeat(block_mask, block_side, axis=0), block_side, axis=1)
    delta = cell_delta(score, counts, active, row_logm, col_logm)
    gshard = jnp.dot(delta, cvec, preferred_element_type=F32) / jnp.sqrt(F32(all_cols))
    ordered = jnp.zeros(gshard.shape, F32).at[row_local].set(gshard)
    row_grad = lax.psum_scatter(ordered, "col", scatter_dimension=0, tiled=True)
    hshard = lax.dot_general(
        delta, wvec, (((0,), (0,)), ((), ())), preferred_element_type=F32
    ) / jnp.sqrt(F32(all_rows))
    col_ordered = jnp.zeros(hshard.shape, F32).at[col_local].set(hshard)
    col_grad = lax.psum_scatter(col_ordered, "row", scatter_dimension=0, tiled=True)
    return (row_grad, col_grad)


ROW_AT, COL_AT = 0, 1

WHOLE = pl.BlockSpec(memory_space=pltpu.VMEM)
SCALARS = pl.BlockSpec(memory_space=pltpu.SMEM)


def params(mib):
    return pltpu.CompilerParams(vmem_limit_bytes=mib * MIB)


def cost(flops, moved):
    return pl.CostEstimate(flops=flops, bytes_accessed=moved, transcendentals=0)


def onehot(flag):
    return jnp.where(flag, 1.0, 0.0).astype(BF16)


def pieces_of(value):
    high = value.astype(BF16)
    rest = value - high.astype(F32)
    middle = rest.astype(BF16)
    low = (rest - middle.astype(F32)).astype(BF16)
    return high, middle, low


def along_sublanes(value):
    fill = jnp.zeros((LANES - value.shape[0], LANES), F32)
    return jnp.concatenate([value, fill], axis=0).T


def copies(pairs, sems):
    made = [pltpu.make_async_copy(src, dst, sems.at[at]) for at, (src, dst) in enumerate(pairs)]
    for copy in made:
        copy.start()
    return made


def fill_pick(pick, columns, base, groups):
    vocab = (lax.broadcasted_iota(jnp.int32, (LANES, pick.shape[1]), 1) + base).astype(F32)
    for group in groups:
        pick[pl.ds(group * LANES, LANES), :] = onehot(columns[:, group : group + 1] == vocab)


def chunk_base(scalars, offset, width):
    return jnp.bitwise_xor(scalars[ROW_AT], offset) * width


def move_values(values, pick, aux_ref):
    moved = jnp.dot(values, pick[...], preferred_element_type=F32)
    rows = values.shape[0] - 24
    aux_ref[pl.ds(0, rows), :] = moved[:rows]
    aux_ref[pl.ds(rows, 8), :] = moved[rows : rows + 8] + moved[rows + 8 : rows + 16] + moved[rows + 16 :]


def order_first_kernel(offsets, scalars, perm_hbm, mask_hbm, logm_hbm, count_hbm, *refs):
    parts = len(offsets)
    outs, auxes, refs = refs[:parts], refs[parts : 2 * parts], refs[2 * parts :]
    shifted_ref, columns_ref, values_ref, perm, mask_ref, logm_ref, tiles, pick, sems, tile_sems = refs
    depth = pick.shape[1]
    width = pick.shape[2]
    rows = outs[0].shape[0]
    step = tiles.shape[1]
    steps = rows // step

    slots = tiles.shape[0]

    def tile_copy(at):
        slot = lax.rem(at, slots)
        return pltpu.make_async_copy(
            count_hbm.at[pl.ds(pl.multiple_of(at * step, step), step)], tiles.at[slot], tile_sems.at[slot]
        )

    small = copies([(perm_hbm, perm), (mask_hbm, mask_ref), (logm_hbm, logm_ref)], sems)
    tile_copy(0).start()
    for copy in small:
        copy.wait()
    columns = along_sublanes((perm[...] - scalars[COL_AT] * depth).astype(F32))
    columns_ref[...] = columns
    blocks_r, blocks_c = mask_ref.shape
    mask = mask_ref[...].astype(F32)
    side = (blocks_r, depth // blocks_c)
    active = jnp.concatenate(
        [jnp.broadcast_to(mask[:, at : at + 1], side) for at in range(blocks_c)], axis=1
    )
    logm = jnp.broadcast_to(logm_ref[...], (8, depth))
    values = jnp.concatenate([active, *[piece.astype(F32) for piece in pieces_of(logm)]], axis=0)
    values_ref[...] = values
    values = values.astype(BF16)
    for part, offset in enumerate(offsets):
        fill_pick(pick.at[part], columns, chunk_base(scalars, offset, width), range(depth // LANES))
        move_values(values, pick.at[part], auxes[part])
    tile_copy(1).start()

    @pl.loop(0, steps)
    def _(at):
        here = pl.ds(pl.multiple_of(at * step, step), step)
        tile_copy(at).wait()
        shifted = (tiles[lax.rem(at, slots)] - 256).astype(F32).astype(BF16)
        shifted_ref[here, :] = shifted

        @pl.when(at + slots < steps)
        def _():
            tile_copy(at + slots).start()

        for part in range(parts):
            moved = jnp.dot(shifted, pick[part], preferred_element_type=F32)
            outs[part][here, :] = moved.astype(BF16)


def in_hbm(value):
    return pltpu.with_memory_space_constraint(value, pltpu.HBM)


def order_first(scalars, col_perm, block_mask, col_logm, counts, offsets, width):
    rows, cols = counts.shape
    parts = len(offsets)
    blocks = block_mask.shape[0]
    outside = pl.BlockSpec(memory_space=pltpu.HBM)
    step = 512
    return pl.pallas_call(
        functools.partial(order_first_kernel, offsets),
        in_specs=[SCALARS] + [outside] * 4,
        out_specs=[WHOLE] * (2 * parts + 3),
        out_shape=[jax.ShapeDtypeStruct((rows, width), BF16)] * parts
        + [jax.ShapeDtypeStruct((blocks + 8, width), F32)] * parts
        + [
            jax.ShapeDtypeStruct((rows, cols), BF16),
            jax.ShapeDtypeStruct((LANES, LANES), F32),
            jax.ShapeDtypeStruct((blocks + 24, cols), F32),
        ],
        scratch_shapes=[
            pltpu.VMEM((cols // LANES, LANES), jnp.int32),
            pltpu.VMEM(block_mask.shape, jnp.int32),
            pltpu.VMEM((1, cols), F32),
            pltpu.VMEM((2, step, cols), jnp.int32),
            pltpu.VMEM((parts, cols, width), BF16),
            pltpu.SemaphoreType.DMA((3,)),
            pltpu.SemaphoreType.DMA((2,)),
        ],
        compiler_params=params(28),
        cost_estimate=cost(2 * parts * rows * cols * width, 4 * rows * cols),
        name="order_first",
    )(scalars, *[in_hbm(each) for each in (col_perm.reshape(-1, LANES), block_mask, col_logm[None, :], counts)])


def order_next_kernel(offsets, scalars, shifted_ref, columns_ref, values_ref, *refs):
    parts = len(offsets)
    outs, auxes, pick = refs[:parts], refs[parts : 2 * parts], refs[-1]
    depth, width = pick.shape[1:]
    values = values_ref[...].astype(BF16)
    for part, offset in enumerate(offsets):
        base = chunk_base(scalars, offset, width)
        fill_pick(pick.at[part], columns_ref[...], base, range(depth // LANES))
        move_values(values, pick.at[part], auxes[part])
    step = 512

    @pl.loop(0, shifted_ref.shape[0] // step)
    def _(at):
        here = pl.ds(pl.multiple_of(at * step, step), step)
        for part in range(parts):
            moved = jnp.dot(shifted_ref[here, :], pick[part], preferred_element_type=F32)
            outs[part][here, :] = moved.astype(BF16)


def order_next(scalars, shifted, columns, values, offsets, width):
    rows, cols = shifted.shape
    parts = len(offsets)
    return pl.pallas_call(
        functools.partial(order_next_kernel, offsets),
        in_specs=[SCALARS] + [WHOLE] * 3,
        out_specs=[WHOLE] * (2 * parts),
        out_shape=[jax.ShapeDtypeStruct((rows, width), BF16)] * parts
        + [jax.ShapeDtypeStruct((values.shape[0] - 16, width), F32)] * parts,
        scratch_shapes=[pltpu.VMEM((parts, cols, width), BF16)],
        compiler_params=params(24),
        cost_estimate=cost(rows * width, rows * width),
        name="order_next",
    )(scalars, shifted, columns, values)


def take_kernel(scalars, perm_ref, logm_ref, *refs):
    own, from_x, from_y, from_xy, from_core, out_ref, turned_ref, logm_out, group, pick = refs
    side = own.shape[0]
    mine = [own, from_x, from_y, from_xy]
    blocks = [(2 * at, mine[at]) for at in range(4)] + [(2 * at + 1, from_core.at[at]) for at in range(4)]
    for offset, block in blocks:
        first = pl.multiple_of(jnp.bitwise_xor(scalars[COL_AT], offset) * side, side)
        group[pl.ds(first, side), :] = block[...]
    rows = out_ref.shape[0]
    depth = group.shape[0]
    groups = rows // LANES
    index = (perm_ref[...] - scalars[ROW_AT] * rows).astype(F32)
    columns = along_sublanes(jnp.concatenate([index, logm_ref[...]], axis=0))
    step = pick.shape[1]
    vocab = lax.broadcasted_iota(jnp.int32, (LANES, depth), 1).astype(F32)
    for first in range(0, rows, step):
        slot = (first // step) % pick.shape[0]
        for inner in range(0, step, LANES):
            at = (first + inner) // LANES
            pick[slot, pl.ds(inner, LANES), :] = onehot(columns[:, at : at + 1] == vocab)
            logm_out[pl.ds(first + inner, LANES), :] = jnp.broadcast_to(
                columns[:, groups + at : groups + at + 1], (LANES, LANES)
            )
        taken = jnp.dot(pick[slot], group[...], preferred_element_type=F32).astype(BF16)
        out_ref[pl.ds(first, step), :] = taken
        turned_ref[:, pl.ds(first, step)] = taken.T


def take_rows(scalars, row_perm, row_logm, blocks):
    rows = row_perm.shape[0]
    side, width = blocks[0].shape
    return pl.pallas_call(
        take_kernel,
        in_specs=[SCALARS] + [WHOLE] * 7,
        out_specs=[WHOLE] * 3,
        out_shape=[
            jax.ShapeDtypeStruct((rows, width), BF16),
            jax.ShapeDtypeStruct((width, rows), BF16),
            jax.ShapeDtypeStruct((rows, LANES), F32),
        ],
        scratch_shapes=[pltpu.VMEM((8 * side, width), BF16), pltpu.VMEM((2, 512, 8 * side), BF16)],
        compiler_params=params(24),
        cost_estimate=cost(2 * rows * rows * width, 4 * rows * width),
        name="take_rows",
    )(scalars, row_perm.reshape(-1, LANES), row_logm.reshape(-1, LANES), *blocks)


def cells_kernel(others, pieces, *refs):
    wvec_ref, turned_ref, logm_ref, chunk, count_ref, aux_ref, refs = *refs[:6], refs[6:]
    chunk_refs, delta_refs, refs = refs[:others], refs[others : 2 * others], refs[2 * others :]
    outs = max(len(pieces), 1)
    main_ref, out_refs, refs = refs[0], refs[1 : 1 + outs], refs[1 + outs :]
    chunk_turned, term_ref, refs = refs[0], refs[1], refs[2:]
    chunk_turned[...] = chunk[...].T
    rows = wvec_ref.shape[0]
    width = chunk.shape[0]
    blocks = aux_ref.shape[0] - 8
    tile = rows // blocks
    col_logm = aux_ref[pl.ds(blocks, 1), :]
    if others:
        delta_ref, stack = refs
        for at, ref in enumerate([*chunk_refs, chunk]):
            stack[pl.ds(at * width, width), :] = ref[...]
    else:
        delta_ref = main_ref
    joined = delta_ref.shape[0] // tile
    half = joined // 2

    def part(group):
        def rows_at(at, count=1):
            return pl.ds(pl.multiple_of((group * joined + at) * tile, tile), count * tile)

        def held(at, count=1):
            return delta_ref[pl.ds(at * tile, count * tile), :]

        def score_of(at):
            return jnp.dot(wvec_ref[rows_at(at), :], chunk_turned[...], preferred_element_type=F32)

        def delta_of(at, score):
            here = rows_at(at)
            count = count_ref[here, :].astype(F32) + 256.0
            log = jnp.log(jnp.maximum(count, 1.0))
            row_logm = jnp.concatenate([logm_ref[here, :]] * (width // LANES), axis=1)
            gap = score + ((row_logm + col_logm) - log)
            confid = 0.1 + 0.25 * jnp.exp2(log * np.float32(0.5 / np.log(2.0)))
            zeroed = 0.5 * jnp.tanh(0.5 * gap) + 0.5
            deriv = jnp.where(count > 0.0, confid * gap, zeroed)
            active = aux_ref[pl.ds(group * joined + at, 1), :]
            delta_ref[pl.ds(at * tile, tile), :] = (deriv * active).astype(BF16)

        def grad_of(at, count):
            here = rows_at(at, count)
            deltas = jnp.concatenate([ref[here, :] for ref in delta_refs] + [held(at, count)], axis=1)
            main_ref[here, :] = jnp.dot(deltas, stack[...], preferred_element_type=F32)

        def term_of(at):
            turned = turned_ref[:, rows_at(at, half)]
            term = jnp.dot(turned, held(at, half), preferred_element_type=F32)
            if joined < blocks or at:
                term = term_ref[...] + term
            term_ref[...] = term

        ahead = score_of(0)
        for at in range(joined):
            score = ahead
            if at + 1 < joined:
                ahead = score_of(at + 1)
            delta_of(at, score)
            if at == half:
                term_of(0)
                if others:
                    grad_of(0, half)
        term_of(half)
        if others:
            grad_of(half, half)

    if joined < blocks:
        term_ref[...] = jnp.zeros_like(term_ref)
        pl.loop(0, blocks // joined)(part)
    else:
        part(0)
    first = 0
    for out_ref in out_refs:
        out_ref[...] = term_ref[pl.ds(first, out_ref.shape[0]), :].astype(out_ref.dtype)
        first += out_ref.shape[0]


def cells(rows_in, chunk, pieces=(), others=()):
    wvec = rows_in[0]
    rows, depth = wvec.shape
    width = chunk[0].shape[0]
    args = [*rows_in, *chunk, *[each for each, _ in others], *[delta for _, delta in others]]
    if others:
        main = jax.ShapeDtypeStruct((rows, depth), F32)
        scratch = [pltpu.VMEM((rows // 2, width), BF16), pltpu.VMEM(((len(others) + 1) * width, depth), BF16)]
    else:
        main = jax.ShapeDtypeStruct((rows, width), BF16)
        scratch = []
    if pieces:
        outs = [jax.ShapeDtypeStruct((size, width), BF16) for size in pieces]
    else:
        outs = [jax.ShapeDtypeStruct((depth, width), F32)]
    return pl.pallas_call(
        functools.partial(cells_kernel, len(others), pieces),
        in_specs=[WHOLE] * len(args),
        out_specs=[WHOLE] * (1 + len(outs)),
        out_shape=[main, *outs],
        scratch_shapes=[pltpu.VMEM((depth, width), BF16), pltpu.VMEM((depth, width), F32), *scratch],
        compiler_params=params(24),
        cost_estimate=cost(rows * width, rows * depth),
        name="cells",
    )(*args)


def finish_kernel(scale, *refs):
    own_ref, near_ref, cross_refs, out_ref, sum_ref = refs[0], refs[1], refs[2:-2], refs[-2], refs[-1]
    first = 0
    for cross_ref in cross_refs:
        here = pl.ds(first, cross_ref.shape[0])
        first += cross_ref.shape[0]
        total = own_ref[here, :] + near_ref[here, :].astype(F32) + cross_ref[...].astype(F32)
        sum_ref[here, :] = total * scale
    out_ref[...] = sum_ref[...].T


def finish(scale, own, near, *crosses):
    return pl.pallas_call(
        functools.partial(finish_kernel, scale),
        in_specs=[WHOLE] * (2 + len(crosses)),
        out_specs=WHOLE,
        out_shape=jax.ShapeDtypeStruct(own.shape[::-1], F32),
        scratch_shapes=[pltpu.VMEM(own.shape, F32)],
        compiler_params=params(8),
        cost_estimate=cost(own.size, own.size // 16),
        name="finish",
    )(own, near, *crosses)


def put_kernel(offsets, exact, scalars, perm_ref, grad_ref, out_ref, pick):
    grad = grad_ref[...]
    rows, width = grad.shape
    high = grad.astype(BF16)
    moving = high
    if exact:
        moving = jnp.concatenate([high, (grad - high.astype(F32)).astype(BF16)], axis=1)
    side = out_ref.shape[1]
    index = jnp.broadcast_to((perm_ref[...] - scalars[ROW_AT] * rows).astype(F32), (8, rows))[:1]
    vocab = lax.broadcasted_iota(jnp.int32, (side, rows), 0)
    for at, offset in enumerate(offsets):
        base = jnp.bitwise_xor(scalars[COL_AT], offset) * side
        pick[pl.ds(at * side, side), :] = onehot(index == (vocab + base).astype(F32))
    moved = jnp.dot(pick[...], moving, preferred_element_type=F32)
    if exact:
        moved = moved[:, :width] + moved[:, width:]
    out_ref[...] = moved.astype(out_ref.dtype).reshape(out_ref.shape)


def put_rows(scalars, row_perm, grad, offsets, side, exact):
    width = grad.shape[1]
    return pl.pallas_call(
        functools.partial(put_kernel, offsets, exact),
        in_specs=[SCALARS, WHOLE, WHOLE],
        out_specs=WHOLE,
        out_shape=jax.ShapeDtypeStruct((len(offsets), side, width), F32 if exact else BF16),
        scratch_shapes=[pltpu.VMEM((len(offsets) * side, grad.shape[0]), BF16)],
        compiler_params=params(24),
        cost_estimate=cost((16384 if exact and len(offsets) > 1 else 1) * grad.size, grad.size // 16),
        name="put_rows",
    )(scalars, row_perm[None, :], grad)


def swap(value, axis, bit):
    pairs = [(at, at ^ bit) for at in range(lax.axis_size(axis))]
    return lax.ppermute(value, axis, pairs)


def together(values):
    return lax.optimization_barrier(values)


def line_shards(counts, block_mask, row_perm, col_perm, row_logm, col_logm, row_emb, col_emb):
    shard_rows, shard_cols = counts.shape
    side = row_emb.shape[0]
    width = col_emb.shape[0]
    scalars = jnp.stack([lax.axis_index("row"), lax.axis_index("col")]).astype(jnp.int32)

    cross = swap(col_emb, "row", 2)
    near = swap(col_emb, "row", 1)
    count_far, aux_far, shifted, columns, values = order_first(
        scalars, col_perm, block_mask, col_logm, counts, (3,), width
    )
    ordered = functools.partial(order_next, scalars)
    row_block, shifted = together((row_emb, shifted))
    from_x = swap(row_block, "col", 2)
    from_y = swap(row_block, "col", 4)
    from_xy = swap(row_block, "col", 6)
    count_cross, count_near, aux_cross, aux_near = ordered(shifted, columns, values, (2, 1), width)
    cross, near, from_x, from_y, from_xy, count_near, shifted = together(
        (cross, near, from_x, from_y, from_xy, count_near, shifted)
    )
    far = swap(cross, "row", 1)
    from_core = swap(jnp.stack([row_emb, from_x, from_y, from_xy]), "col", 1)
    count_own, aux_own = ordered(shifted, columns, values, (0,), width)
    count_own, row_perm = together((count_own, row_perm))
    blocks = [row_emb, from_x, from_y, from_xy, from_core]
    wvec, turned, logm = take_rows(scalars, row_perm, row_logm, blocks)

    rows_in = (wvec, turned, logm)
    of_far, of_cross = (far, count_far, aux_far), (cross, count_cross, aux_cross)
    of_near, of_own = (near, count_near, aux_near), (col_emb, count_own, aux_own)
    depth = col_emb.shape[1]
    early = depth * 5 // 16
    delta_far, sent_0, sent_1 = cells(rows_in, of_far, (early, depth - early))
    far_0 = swap(sent_0, "row", 1)
    far_1 = swap(sent_1, "row", 1)
    rows_in, delta_far = together((rows_in, delta_far))
    delta_cross, term_cross = cells(rows_in, of_cross)
    rows_in, delta_cross = together((rows_in, delta_cross))
    delta_near, sent_near = cells(rows_in, of_near, (depth,))
    got_near = swap(sent_near, "row", 1)
    rows_in, delta_near, far_0 = together((rows_in, delta_near, far_0))

    sum_0 = (term_cross[:early] + far_0.astype(F32)).astype(BF16)
    rows_in, sum_0 = together((rows_in, sum_0))
    cross_0 = swap(sum_0, "row", 2)
    others = ((far, delta_far), (cross, delta_cross), (near, delta_near))
    grad, term_own = cells(rows_in, of_own, (), others)
    grad, far_1, cross_0 = together((grad, far_1, cross_0))
    sum_1 = (term_cross[early:] + far_1.astype(F32)).astype(BF16)
    cross_1 = swap(sum_1, "row", 2)
    grad, sum_1 = together((grad, sum_1))

    ordered = functools.partial(put_rows, scalars, row_perm)
    away = ordered(grad, (1, 3, 5, 7), side, False)
    core = swap(away, "col", 1)
    grad, away = together((grad, away))
    both = ordered(grad, (2, 4, 6), side, True) + core[1:].astype(F32)
    sends = [both[at].astype(BF16) for at in range(3)]
    got = [swap(sends[at], "col", bit) for at, bit in ((1, 4), (2, 6), (0, 2))]
    grad, sends = together((grad, sends))
    home = ordered(grad, (0,), side, True)
    home, term_own = together((home, term_own))
    row_sum = home[0] + core[0].astype(F32)
    for each in got:
        row_sum = row_sum + each.astype(F32)
    row_scale = np.float32(1.0 / np.sqrt(shard_cols * 8))
    col_scale = np.float32(1.0 / np.sqrt(shard_rows * 4))
    return (row_sum * row_scale, finish(col_scale, term_own, got_near, cross_0, cross_1))


def solution(mesh):
    in_specs = (
        P("row", "col"),
        P("row", "col"),
        P("row"),
        P("col"),
        P("row"),
        P("col"),
        P(("row", "col"), None),
        P(("col", "row"), None),
    )
    out_specs = (P(("row", "col"), None), P(("col", "row"), None))
    line = mesh.shape["row"] == 4 and mesh.shape["col"] == 8
    body = line_shards if line else plain_shards
    return jax.shard_map(body, mesh=mesh, in_specs=in_specs, out_specs=out_specs, check_vma=False)
```

```python
import functools

import jax
import jax.numpy as jnp
import numpy as np
from jax import lax
from jax.experimental import pallas as pl
from jax.experimental.pallas import tpu as pltpu
from jax.sharding import PartitionSpec as P

F32 = jnp.float32
BF16 = jnp.bfloat16
LANES = 128
MIB = 1 << 20


def cell_delta(score, count, active, row_part, col_part):
    real_count = count.astype(F32)
    safe = jnp.maximum(real_count, 1.0)
    pmi = jnp.log(safe) - row_part[:, None] - col_part[None, :]
    confid = 0.1 + 0.25 * jnp.sqrt(safe)
    positive = confid * (score - pmi)
    zeroed = jax.nn.sigmoid(score - pmi)
    deriv = jnp.where(count > 0, positive, zeroed)
    return (active.astype(F32) * deriv).astype(BF16)


def plain_shards(counts, block_mask, row_perm, col_perm, row_logm, col_logm, row_emb, col_emb):
    shard_rows, shard_cols = counts.shape
    all_cols = shard_cols * lax.axis_size("col")
    all_rows = shard_rows * lax.axis_size("row")
    block_side = shard_rows // block_mask.shape[0]
    row_group = lax.all_gather(row_emb, "col", axis=0, tiled=True)
    col_group = lax.all_gather(col_emb, "row", axis=0, tiled=True)
    row_local = row_perm - lax.axis_index("row") * shard_rows
    col_local = col_perm - lax.axis_index("col") * shard_cols
    wvec = jnp.take(row_group, row_local, axis=0)
    cvec = jnp.take(col_group, col_local, axis=0)
    score = lax.dot_general(wvec, cvec, (((1,), (1,)), ((), ())), preferred_element_type=F32)
    active = jnp.repeat(jnp.repeat(block_mask, block_side, axis=0), block_side, axis=1)
    delta = cell_delta(score, counts, active, row_logm, col_logm)
    gshard = jnp.dot(delta, cvec, preferred_element_type=F32) / jnp.sqrt(F32(all_cols))
    ordered = jnp.zeros(gshard.shape, F32).at[row_local].set(gshard)
    row_grad = lax.psum_scatter(ordered, "col", scatter_dimension=0, tiled=True)
    hshard = lax.dot_general(
        delta, wvec, (((0,), (0,)), ((), ())), preferred_element_type=F32
    ) / jnp.sqrt(F32(all_rows))
    col_ordered = jnp.zeros(hshard.shape, F32).at[col_local].set(hshard)
    col_grad = lax.psum_scatter(col_ordered, "row", scatter_dimension=0, tiled=True)
    return (row_grad, col_grad)


ROW_AT, COL_AT = 0, 1

WHOLE = pl.BlockSpec(memory_space=pltpu.VMEM)
SCALARS = pl.BlockSpec(memory_space=pltpu.SMEM)


def params(mib):
    return pltpu.CompilerParams(vmem_limit_bytes=mib * MIB)


def cost(flops, moved):
    return pl.CostEstimate(flops=flops, bytes_accessed=moved, transcendentals=0)


def onehot(flag):
    return jnp.where(flag, 1.0, 0.0).astype(BF16)


def pieces_of(value):
    high = value.astype(BF16)
    rest = value - high.astype(F32)
    middle = rest.astype(BF16)
    low = (rest - middle.astype(F32)).astype(BF16)
    return high, middle, low


def along_sublanes(value):
    fill = jnp.zeros((LANES - value.shape[0], LANES), F32)
    return jnp.concatenate([value, fill], axis=0).T


def copies(pairs, sems):
    made = [pltpu.make_async_copy(src, dst, sems.at[at]) for at, (src, dst) in enumerate(pairs)]
    for copy in made:
        copy.start()
    return made


def fill_pick(pick, columns, base, groups):
    vocab = (lax.broadcasted_iota(jnp.int32, (LANES, pick.shape[1]), 1) + base).astype(F32)
    for group in groups:
        pick[pl.ds(group * LANES, LANES), :] = onehot(columns[:, group : group + 1] == vocab)


def chunk_base(scalars, offset, width):
    return jnp.bitwise_xor(scalars[ROW_AT], offset) * width


def move_values(values, pick, aux_ref):
    moved = jnp.dot(values, pick[...], preferred_element_type=F32)
    rows = values.shape[0] - 24
    aux_ref[pl.ds(0, rows), :] = moved[:rows]
    aux_ref[pl.ds(rows, 8), :] = moved[rows : rows + 8] + moved[rows + 8 : rows + 16] + moved[rows + 16 :]


def order_first_kernel(offsets, scalars, perm_hbm, mask_hbm, logm_hbm, count_hbm, *refs):
    parts = len(offsets)
    outs, auxes, refs = refs[:parts], refs[parts : 2 * parts], refs[2 * parts :]
    shifted_ref, columns_ref, values_ref, perm, mask_ref, logm_ref, tiles, pick, sems, tile_sems = refs
    depth = pick.shape[1]
    width = pick.shape[2]
    rows = outs[0].shape[0]
    step = tiles.shape[1]
    steps = rows // step

    slots = tiles.shape[0]

    def tile_copy(at):
        slot = lax.rem(at, slots)
        return pltpu.make_async_copy(
            count_hbm.at[pl.ds(pl.multiple_of(at * step, step), step)], tiles.at[slot], tile_sems.at[slot]
        )

    small = copies([(perm_hbm, perm), (mask_hbm, mask_ref), (logm_hbm, logm_ref)], sems)
    tile_copy(0).start()
    for copy in small:
        copy.wait()
    columns = along_sublanes((perm[...] - scalars[COL_AT] * depth).astype(F32))
    columns_ref[...] = columns
    blocks_r, blocks_c = mask_ref.shape
    mask = mask_ref[...].astype(F32)
    side = (blocks_r, depth // blocks_c)
    active = jnp.concatenate(
        [jnp.broadcast_to(mask[:, at : at + 1], side) for at in range(blocks_c)], axis=1
    )
    logm = jnp.broadcast_to(logm_ref[...], (8, depth))
    values = jnp.concatenate([active, *[piece.astype(F32) for piece in pieces_of(logm)]], axis=0)
    values_ref[...] = values
    values = values.astype(BF16)
    for part, offset in enumerate(offsets):
        fill_pick(pick.at[part], columns, chunk_base(scalars, offset, width), range(depth // LANES))
        move_values(values, pick.at[part], auxes[part])
    tile_copy(1).start()

    @pl.loop(0, steps)
    def _(at):
        here = pl.ds(pl.multiple_of(at * step, step), step)
        tile_copy(at).wait()
        shifted = (tiles[lax.rem(at, slots)] - 256).astype(F32).astype(BF16)
        shifted_ref[here, :] = shifted

        @pl.when(at + slots < steps)
        def _():
            tile_copy(at + slots).start()

        for part in range(parts):
            moved = jnp.dot(shifted, pick[part], preferred_element_type=F32)
            outs[part][here, :] = moved.astype(BF16)


def in_hbm(value):
    return pltpu.with_memory_space_constraint(value, pltpu.HBM)


def order_first(scalars, col_perm, block_mask, col_logm, counts, offsets, width):
    rows, cols = counts.shape
    parts = len(offsets)
    blocks = block_mask.shape[0]
    outside = pl.BlockSpec(memory_space=pltpu.HBM)
    step = 512
    return pl.pallas_call(
        functools.partial(order_first_kernel, offsets),
        in_specs=[SCALARS] + [outside] * 4,
        out_specs=[WHOLE] * (2 * parts + 3),
        out_shape=[jax.ShapeDtypeStruct((rows, width), BF16)] * parts
        + [jax.ShapeDtypeStruct((blocks + 8, width), F32)] * parts
        + [
            jax.ShapeDtypeStruct((rows, cols), BF16),
            jax.ShapeDtypeStruct((LANES, LANES), F32),
            jax.ShapeDtypeStruct((blocks + 24, cols), F32),
        ],
        scratch_shapes=[
            pltpu.VMEM((cols // LANES, LANES), jnp.int32),
            pltpu.VMEM(block_mask.shape, jnp.int32),
            pltpu.VMEM((1, cols), F32),
            pltpu.VMEM((2, step, cols), jnp.int32),
            pltpu.VMEM((parts, cols, width), BF16),
            pltpu.SemaphoreType.DMA((3,)),
            pltpu.SemaphoreType.DMA((2,)),
        ],
        compiler_params=params(28),
        cost_estimate=cost(2 * parts * rows * cols * width, 4 * rows * cols),
        name="order_first",
    )(scalars, *[in_hbm(each) for each in (col_perm.reshape(-1, LANES), block_mask, col_logm[None, :], counts)])


def order_next_kernel(offsets, scalars, shifted_ref, columns_ref, values_ref, *refs):
    parts = len(offsets)
    outs, auxes, pick = refs[:parts], refs[parts : 2 * parts], refs[-1]
    depth, width = pick.shape[1:]
    values = values_ref[...].astype(BF16)
    for part, offset in enumerate(offsets):
        base = chunk_base(scalars, offset, width)
        fill_pick(pick.at[part], columns_ref[...], base, range(depth // LANES))
        move_values(values, pick.at[part], auxes[part])
    step = 512

    @pl.loop(0, shifted_ref.shape[0] // step)
    def _(at):
        here = pl.ds(pl.multiple_of(at * step, step), step)
        for part in range(parts):
            moved = jnp.dot(shifted_ref[here, :], pick[part], preferred_element_type=F32)
            outs[part][here, :] = moved.astype(BF16)


def order_next(scalars, shifted, columns, values, offsets, width):
    rows, cols = shifted.shape
    parts = len(offsets)
    return pl.pallas_call(
        functools.partial(order_next_kernel, offsets),
        in_specs=[SCALARS] + [WHOLE] * 3,
        out_specs=[WHOLE] * (2 * parts),
        out_shape=[jax.ShapeDtypeStruct((rows, width), BF16)] * parts
        + [jax.ShapeDtypeStruct((values.shape[0] - 16, width), F32)] * parts,
        scratch_shapes=[pltpu.VMEM((parts, cols, width), BF16)],
        compiler_params=params(24),
        cost_estimate=cost((16384 if parts == 1 else 1) * rows * width, rows * width),
        name="order_next",
    )(scalars, shifted, columns, values)


def take_kernel(scalars, perm_ref, logm_ref, *refs):
    own, from_x, from_y, from_xy, from_core, out_ref, turned_ref, logm_out, group, pick = refs
    side = own.shape[0]
    mine = [own, from_x, from_y, from_xy]
    blocks = [(2 * at, mine[at]) for at in range(4)] + [(2 * at + 1, from_core.at[at]) for at in range(4)]
    for offset, block in blocks:
        first = pl.multiple_of(jnp.bitwise_xor(scalars[COL_AT], offset) * side, side)
        group[pl.ds(first, side), :] = block[...]
    rows = out_ref.shape[0]
    depth = group.shape[0]
    groups = rows // LANES
    index = (perm_ref[...] - scalars[ROW_AT] * rows).astype(F32)
    columns = along_sublanes(jnp.concatenate([index, logm_ref[...]], axis=0))
    step = pick.shape[1]
    vocab = lax.broadcasted_iota(jnp.int32, (LANES, depth), 1).astype(F32)
    for first in range(0, rows, step):
        slot = (first // step) % pick.shape[0]
        for inner in range(0, step, LANES):
            at = (first + inner) // LANES
            pick[slot, pl.ds(inner, LANES), :] = onehot(columns[:, at : at + 1] == vocab)
            logm_out[pl.ds(first + inner, LANES), :] = jnp.broadcast_to(
                columns[:, groups + at : groups + at + 1], (LANES, LANES)
            )
        taken = jnp.dot(pick[slot], group[...], preferred_element_type=F32).astype(BF16)
        out_ref[pl.ds(first, step), :] = taken
        turned_ref[:, pl.ds(first, step)] = taken.T


def take_rows(scalars, row_perm, row_logm, blocks):
    rows = row_perm.shape[0]
    side, width = blocks[0].shape
    return pl.pallas_call(
        take_kernel,
        in_specs=[SCALARS] + [WHOLE] * 7,
        out_specs=[WHOLE] * 3,
        out_shape=[
            jax.ShapeDtypeStruct((rows, width), BF16),
            jax.ShapeDtypeStruct((width, rows), BF16),
            jax.ShapeDtypeStruct((rows, LANES), F32),
        ],
        scratch_shapes=[pltpu.VMEM((8 * side, width), BF16), pltpu.VMEM((2, 512, 8 * side), BF16)],
        compiler_params=params(24),
        cost_estimate=cost(2 * rows * rows * width, 4 * rows * width),
        name="take_rows",
    )(scalars, row_perm.reshape(-1, LANES), row_logm.reshape(-1, LANES), *blocks)


def cells_kernel(others, pieces, *refs):
    wvec_ref, turned_ref, logm_ref, chunk, count_ref, aux_ref, refs = *refs[:6], refs[6:]
    chunk_refs, delta_refs, refs = refs[:others], refs[others : 2 * others], refs[2 * others :]
    outs = max(len(pieces), 1)
    main_ref, out_refs, refs = refs[0], refs[1 : 1 + outs], refs[1 + outs :]
    chunk_turned, term_ref, refs = refs[0], refs[1], refs[2:]
    chunk_turned[...] = chunk[...].T
    rows = wvec_ref.shape[0]
    width = chunk.shape[0]
    blocks = aux_ref.shape[0] - 8
    tile = rows // blocks
    col_logm = aux_ref[pl.ds(blocks, 1), :]
    if others:
        delta_ref, stack = refs
        for at, ref in enumerate([*chunk_refs, chunk]):
            stack[pl.ds(at * width, width), :] = ref[...]
    else:
        delta_ref = main_ref
    joined = delta_ref.shape[0] // tile
    half = joined // 2

    def part(group):
        def rows_at(at, count=1):
            return pl.ds(pl.multiple_of((group * joined + at) * tile, tile), count * tile)

        def held(at, count=1):
            return delta_ref[pl.ds(at * tile, count * tile), :]

        def score_of(at):
            return jnp.dot(wvec_ref[rows_at(at), :], chunk_turned[...], preferred_element_type=F32)

        def delta_of(at, score):
            here = rows_at(at)
            count = count_ref[here, :].astype(F32) + 256.0
            log = jnp.log(jnp.maximum(count, 1.0))
            row_logm = jnp.concatenate([logm_ref[here, :]] * (width // LANES), axis=1)
            gap = score + ((row_logm + col_logm) - log)
            confid = 0.1 + 0.25 * jnp.exp2(log * np.float32(0.5 / np.log(2.0)))
            zeroed = 0.5 * jnp.tanh(0.5 * gap) + 0.5
            deriv = jnp.where(count > 0.0, confid * gap, zeroed)
            active = aux_ref[pl.ds(group * joined + at, 1), :]
            delta_ref[pl.ds(at * tile, tile), :] = (deriv * active).astype(BF16)

        def grad_of(at, count):
            here = rows_at(at, count)
            deltas = jnp.concatenate([ref[here, :] for ref in delta_refs] + [held(at, count)], axis=1)
            main_ref[here, :] = jnp.dot(deltas, stack[...], preferred_element_type=F32)

        def term_of(at):
            turned = turned_ref[:, rows_at(at, half)]
            term = jnp.dot(turned, held(at, half), preferred_element_type=F32)
            if joined < blocks or at:
                term = term_ref[...] + term
            term_ref[...] = term

        ahead = score_of(0)
        for at in range(joined):
            score = ahead
            if at + 1 < joined:
                ahead = score_of(at + 1)
            delta_of(at, score)
            if at == half:
                term_of(0)
                if others:
                    grad_of(0, half)
        term_of(half)
        if others:
            grad_of(half, half)

    if joined < blocks:
        term_ref[...] = jnp.zeros_like(term_ref)
        pl.loop(0, blocks // joined)(part)
    else:
        part(0)
    first = 0
    for out_ref in out_refs:
        out_ref[...] = term_ref[pl.ds(first, out_ref.shape[0]), :].astype(out_ref.dtype)
        first += out_ref.shape[0]


def cells(rows_in, chunk, pieces=(), others=()):
    wvec = rows_in[0]
    rows, depth = wvec.shape
    width = chunk[0].shape[0]
    args = [*rows_in, *chunk, *[each for each, _ in others], *[delta for _, delta in others]]
    if others:
        main = jax.ShapeDtypeStruct((rows, depth), F32)
        scratch = [pltpu.VMEM((rows // 2, width), BF16), pltpu.VMEM(((len(others) + 1) * width, depth), BF16)]
    else:
        main = jax.ShapeDtypeStruct((rows, width), BF16)
        scratch = []
    if pieces:
        outs = [jax.ShapeDtypeStruct((size, width), BF16) for size in pieces]
    else:
        outs = [jax.ShapeDtypeStruct((depth, width), F32)]
    return pl.pallas_call(
        functools.partial(cells_kernel, len(others), pieces),
        in_specs=[WHOLE] * len(args),
        out_specs=[WHOLE] * (1 + len(outs)),
        out_shape=[main, *outs],
        scratch_shapes=[pltpu.VMEM((depth, width), BF16), pltpu.VMEM((depth, width), F32), *scratch],
        compiler_params=params(24),
        cost_estimate=cost(rows * width, rows * depth),
        name="cells",
    )(*args)


def finish_kernel(scale, *refs):
    own_ref, near_ref, cross_refs, out_ref, sum_ref = refs[0], refs[1], refs[2:-2], refs[-2], refs[-1]
    first = 0
    for cross_ref in cross_refs:
        here = pl.ds(first, cross_ref.shape[0])
        first += cross_ref.shape[0]
        total = own_ref[here, :] + near_ref[here, :].astype(F32) + cross_ref[...].astype(F32)
        sum_ref[here, :] = total * scale
    out_ref[...] = sum_ref[...].T


def finish(scale, own, near, *crosses):
    return pl.pallas_call(
        functools.partial(finish_kernel, scale),
        in_specs=[WHOLE] * (2 + len(crosses)),
        out_specs=WHOLE,
        out_shape=jax.ShapeDtypeStruct(own.shape[::-1], F32),
        scratch_shapes=[pltpu.VMEM(own.shape, F32)],
        compiler_params=params(8),
        cost_estimate=cost(own.size, own.size // 16),
        name="finish",
    )(own, near, *crosses)


def put_kernel(offsets, exact, scalars, perm_ref, grad_ref, out_ref, pick):
    grad = grad_ref[...]
    rows, width = grad.shape
    high = grad.astype(BF16)
    moving = high
    if exact:
        moving = jnp.concatenate([high, (grad - high.astype(F32)).astype(BF16)], axis=1)
    side = out_ref.shape[1]
    index = jnp.broadcast_to((perm_ref[...] - scalars[ROW_AT] * rows).astype(F32), (8, rows))[:1]
    vocab = lax.broadcasted_iota(jnp.int32, (side, rows), 0)
    for at, offset in enumerate(offsets):
        base = jnp.bitwise_xor(scalars[COL_AT], offset) * side
        pick[pl.ds(at * side, side), :] = onehot(index == (vocab + base).astype(F32))
    moved = jnp.dot(pick[...], moving, preferred_element_type=F32)
    if exact:
        moved = moved[:, :width] + moved[:, width:]
    out_ref[...] = moved.astype(out_ref.dtype).reshape(out_ref.shape)


def put_rows(scalars, row_perm, grad, offsets, side, exact):
    width = grad.shape[1]
    return pl.pallas_call(
        functools.partial(put_kernel, offsets, exact),
        in_specs=[SCALARS, WHOLE, WHOLE],
        out_specs=WHOLE,
        out_shape=jax.ShapeDtypeStruct((len(offsets), side, width), F32 if exact else BF16),
        scratch_shapes=[pltpu.VMEM((len(offsets) * side, grad.shape[0]), BF16)],
        compiler_params=params(24),
        cost_estimate=cost((16384 if exact and len(offsets) > 1 else 1) * grad.size, grad.size // 16),
        name="put_rows",
    )(scalars, row_perm[None, :], grad)


def swap(value, axis, bit):
    pairs = [(at, at ^ bit) for at in range(lax.axis_size(axis))]
    return lax.ppermute(value, axis, pairs)


def together(values):
    return lax.optimization_barrier(values)


def line_shards(counts, block_mask, row_perm, col_perm, row_logm, col_logm, row_emb, col_emb):
    shard_rows, shard_cols = counts.shape
    side = row_emb.shape[0]
    width = col_emb.shape[0]
    scalars = jnp.stack([lax.axis_index("row"), lax.axis_index("col")]).astype(jnp.int32)

    cross = swap(col_emb, "row", 2)
    near = swap(col_emb, "row", 1)
    count_far, aux_far, shifted, columns, values = order_first(
        scalars, col_perm, block_mask, col_logm, counts, (3,), width
    )
    ordered = functools.partial(order_next, scalars)
    row_block, shifted = together((row_emb, shifted))
    from_x = swap(row_block, "col", 2)
    from_y = swap(row_block, "col", 4)
    from_xy = swap(row_block, "col", 6)
    count_cross, count_near, aux_cross, aux_near = ordered(shifted, columns, values, (2, 1), width)
    cross, near, from_x, from_y, from_xy, count_near, shifted = together(
        (cross, near, from_x, from_y, from_xy, count_near, shifted)
    )
    far = swap(cross, "row", 1)
    from_core = swap(jnp.stack([row_emb, from_x, from_y, from_xy]), "col", 1)
    count_own, aux_own = ordered(shifted, columns, values, (0,), width)
    count_own, row_perm = together((count_own, row_perm))
    blocks = [row_emb, from_x, from_y, from_xy, from_core]
    wvec, turned, logm = take_rows(scalars, row_perm, row_logm, blocks)

    rows_in = (wvec, turned, logm)
    of_far, of_cross = (far, count_far, aux_far), (cross, count_cross, aux_cross)
    of_near, of_own = (near, count_near, aux_near), (col_emb, count_own, aux_own)
    depth = col_emb.shape[1]
    early = depth * 5 // 16
    delta_far, sent_0, sent_1 = cells(rows_in, of_far, (early, depth - early))
    far_0 = swap(sent_0, "row", 1)
    far_1 = swap(sent_1, "row", 1)
    rows_in, delta_far = together((rows_in, delta_far))
    delta_cross, term_cross = cells(rows_in, of_cross)
    rows_in, delta_cross = together((rows_in, delta_cross))
    delta_near, sent_near = cells(rows_in, of_near, (depth,))
    got_near = swap(sent_near, "row", 1)
    rows_in, delta_near, far_0 = together((rows_in, delta_near, far_0))

    sum_0 = (term_cross[:early] + far_0.astype(F32)).astype(BF16)
    rows_in, sum_0 = together((rows_in, sum_0))
    cross_0 = swap(sum_0, "row", 2)
    others = ((far, delta_far), (cross, delta_cross), (near, delta_near))
    grad, term_own = cells(rows_in, of_own, (), others)
    grad, far_1, cross_0 = together((grad, far_1, cross_0))
    sum_1 = (term_cross[early:] + far_1.astype(F32)).astype(BF16)
    cross_1 = swap(sum_1, "row", 2)
    grad, sum_1 = together((grad, sum_1))

    ordered = functools.partial(put_rows, scalars, row_perm)
    away = ordered(grad, (1, 3, 5, 7), side, False)
    core = swap(away, "col", 1)
    grad, away = together((grad, away))
    both = ordered(grad, (2, 4, 6), side, True) + core[1:].astype(F32)
    sends = [both[at].astype(BF16) for at in range(3)]
    got = [swap(sends[at], "col", bit) for at, bit in ((2, 6), (1, 4), (0, 2))]
    grad, sends = together((grad, sends))
    home = ordered(grad, (0,), side, True)
    home, term_own = together((home, term_own))
    row_sum = home[0] + core[0].astype(F32)
    for each in got:
        row_sum = row_sum + each.astype(F32)
    row_scale = np.float32(1.0 / np.sqrt(shard_cols * 8))
    col_scale = np.float32(1.0 / np.sqrt(shard_rows * 4))
    return (row_sum * row_scale, finish(col_scale, term_own, got_near, cross_0, cross_1))


def solution(mesh):
    in_specs = (
        P("row", "col"),
        P("row", "col"),
        P("row"),
        P("col"),
        P("row"),
        P("col"),
        P(("row", "col"), None),
        P(("col", "row"), None),
    )
    out_specs = (P(("row", "col"), None), P(("col", "row"), None))
    line = mesh.shape["row"] == 4 and mesh.shape["col"] == 8
    body = line_shards if line else plain_shards
    return jax.shard_map(body, mesh=mesh, in_specs=in_specs, out_specs=out_specs, check_vma=False)
```

```python
import functools

import jax
import jax.numpy as jnp
import numpy as np
from jax import lax
from jax.experimental import pallas as pl
from jax.experimental.pallas import tpu as pltpu
from jax.sharding import PartitionSpec as P

F32 = jnp.float32
BF16 = jnp.bfloat16
LANES = 128
MIB = 1 << 20


def cell_delta(score, count, active, row_part, col_part):
    real_count = count.astype(F32)
    safe = jnp.maximum(real_count, 1.0)
    pmi = jnp.log(safe) - row_part[:, None] - col_part[None, :]
    confid = 0.1 + 0.25 * jnp.sqrt(safe)
    positive = confid * (score - pmi)
    zeroed = jax.nn.sigmoid(score - pmi)
    deriv = jnp.where(count > 0, positive, zeroed)
    return (active.astype(F32) * deriv).astype(BF16)


def plain_shards(counts, block_mask, row_perm, col_perm, row_logm, col_logm, row_emb, col_emb):
    shard_rows, shard_cols = counts.shape
    all_cols = shard_cols * lax.axis_size("col")
    all_rows = shard_rows * lax.axis_size("row")
    block_side = shard_rows // block_mask.shape[0]
    row_group = lax.all_gather(row_emb, "col", axis=0, tiled=True)
    col_group = lax.all_gather(col_emb, "row", axis=0, tiled=True)
    row_local = row_perm - lax.axis_index("row") * shard_rows
    col_local = col_perm - lax.axis_index("col") * shard_cols
    wvec = jnp.take(row_group, row_local, axis=0)
    cvec = jnp.take(col_group, col_local, axis=0)
    score = lax.dot_general(wvec, cvec, (((1,), (1,)), ((), ())), preferred_element_type=F32)
    active = jnp.repeat(jnp.repeat(block_mask, block_side, axis=0), block_side, axis=1)
    delta = cell_delta(score, counts, active, row_logm, col_logm)
    gshard = jnp.dot(delta, cvec, preferred_element_type=F32) / jnp.sqrt(F32(all_cols))
    ordered = jnp.zeros(gshard.shape, F32).at[row_local].set(gshard)
    row_grad = lax.psum_scatter(ordered, "col", scatter_dimension=0, tiled=True)
    hshard = lax.dot_general(
        delta, wvec, (((0,), (0,)), ((), ())), preferred_element_type=F32
    ) / jnp.sqrt(F32(all_rows))
    col_ordered = jnp.zeros(hshard.shape, F32).at[col_local].set(hshard)
    col_grad = lax.psum_scatter(col_ordered, "row", scatter_dimension=0, tiled=True)
    return (row_grad, col_grad)


ROW_AT, COL_AT = 0, 1

WHOLE = pl.BlockSpec(memory_space=pltpu.VMEM)
SCALARS = pl.BlockSpec(memory_space=pltpu.SMEM)


def params(mib):
    return pltpu.CompilerParams(vmem_limit_bytes=mib * MIB)


def cost(flops, moved):
    return pl.CostEstimate(flops=flops, bytes_accessed=moved, transcendentals=0)


def onehot(flag):
    return jnp.where(flag, 1.0, 0.0).astype(BF16)


def pieces_of(value):
    high = value.astype(BF16)
    rest = value - high.astype(F32)
    middle = rest.astype(BF16)
    low = (rest - middle.astype(F32)).astype(BF16)
    return high, middle, low


def along_sublanes(value):
    fill = jnp.zeros((LANES - value.shape[0], LANES), F32)
    return jnp.concatenate([value, fill], axis=0).T


def copies(pairs, sems):
    made = [pltpu.make_async_copy(src, dst, sems.at[at]) for at, (src, dst) in enumerate(pairs)]
    for copy in made:
        copy.start()
    return made


def fill_pick(pick, columns, base, groups):
    vocab = (lax.broadcasted_iota(jnp.int32, (LANES, pick.shape[1]), 1) + base).astype(F32)
    for group in groups:
        here = pl.ds(group * LANES, LANES)
        index = jnp.concatenate([columns[here, :]] * (pick.shape[1] // LANES), axis=1)
        pick[here, :] = onehot(index == vocab)


def chunk_base(scalars, offset, width):
    return jnp.bitwise_xor(scalars[ROW_AT], offset) * width


def move_values(values, pick, aux_ref):
    moved = jnp.dot(values, pick[...], preferred_element_type=F32)
    rows = values.shape[0] - 24
    aux_ref[pl.ds(0, rows), :] = moved[:rows]
    aux_ref[pl.ds(rows, 8), :] = moved[rows : rows + 8] + moved[rows + 8 : rows + 16] + moved[rows + 16 :]


def order_first_kernel(offsets, scalars, perm_hbm, mask_hbm, logm_hbm, count_hbm, *refs):
    parts = len(offsets)
    outs, auxes, refs = refs[:parts], refs[parts : 2 * parts], refs[2 * parts :]
    shifted_ref, columns_ref, values_ref, perm, mask_ref, logm_ref, tiles, pick, sems, tile_sems = refs
    depth = pick.shape[1]
    width = pick.shape[2]
    rows = outs[0].shape[0]
    step = tiles.shape[1]
    steps = rows // step

    slots = tiles.shape[0]

    def tile_copy(at):
        slot = lax.rem(at, slots)
        return pltpu.make_async_copy(
            count_hbm.at[pl.ds(pl.multiple_of(at * step, step), step)], tiles.at[slot], tile_sems.at[slot]
        )

    small = copies([(perm_hbm, perm), (mask_hbm, mask_ref), (logm_hbm, logm_ref)], sems)
    tile_copy(0).start()
    for copy in small:
        copy.wait()
    columns = along_sublanes((perm[...] - scalars[COL_AT] * depth).astype(F32))
    for group in range(depth // LANES):
        columns_ref[pl.ds(group * LANES, LANES), :] = jnp.broadcast_to(
            columns[:, group : group + 1], (LANES, LANES)
        )
    blocks_r, blocks_c = mask_ref.shape
    mask = mask_ref[...].astype(F32)
    side = (blocks_r, depth // blocks_c)
    active = jnp.concatenate(
        [jnp.broadcast_to(mask[:, at : at + 1], side) for at in range(blocks_c)], axis=1
    )
    logm = jnp.broadcast_to(logm_ref[...], (8, depth))
    values = jnp.concatenate([active, *[piece.astype(F32) for piece in pieces_of(logm)]], axis=0)
    values_ref[...] = values
    values = values.astype(BF16)
    for part, offset in enumerate(offsets):
        fill_pick(pick.at[part], columns_ref, chunk_base(scalars, offset, width), range(depth // LANES))
        move_values(values, pick.at[part], auxes[part])
    tile_copy(1).start()

    @pl.loop(0, steps)
    def _(at):
        here = pl.ds(pl.multiple_of(at * step, step), step)
        tile_copy(at).wait()
        shifted = (tiles[lax.rem(at, slots)] - 256).astype(F32).astype(BF16)
        shifted_ref[here, :] = shifted

        @pl.when(at + slots < steps)
        def _():
            tile_copy(at + slots).start()

        for part in range(parts):
            moved = jnp.dot(shifted, pick[part], preferred_element_type=F32)
            outs[part][here, :] = moved.astype(BF16)


def in_hbm(value):
    return pltpu.with_memory_space_constraint(value, pltpu.HBM)


def order_first(scalars, col_perm, block_mask, col_logm, counts, offsets, width):
    rows, cols = counts.shape
    parts = len(offsets)
    blocks = block_mask.shape[0]
    outside = pl.BlockSpec(memory_space=pltpu.HBM)
    step = 512
    return pl.pallas_call(
        functools.partial(order_first_kernel, offsets),
        in_specs=[SCALARS] + [outside] * 4,
        out_specs=[WHOLE] * (2 * parts + 3),
        out_shape=[jax.ShapeDtypeStruct((rows, width), BF16)] * parts
        + [jax.ShapeDtypeStruct((blocks + 8, width), F32)] * parts
        + [
            jax.ShapeDtypeStruct((rows, cols), BF16),
            jax.ShapeDtypeStruct((cols, LANES), F32),
            jax.ShapeDtypeStruct((blocks + 24, cols), F32),
        ],
        scratch_shapes=[
            pltpu.VMEM((cols // LANES, LANES), jnp.int32),
            pltpu.VMEM(block_mask.shape, jnp.int32),
            pltpu.VMEM((1, cols), F32),
            pltpu.VMEM((2, step, cols), jnp.int32),
            pltpu.VMEM((parts, cols, width), BF16),
            pltpu.SemaphoreType.DMA((3,)),
            pltpu.SemaphoreType.DMA((2,)),
        ],
        compiler_params=params(28),
        cost_estimate=cost(2 * parts * rows * cols * width, 4 * rows * cols),
        name="order_first",
    )(scalars, *[in_hbm(each) for each in (col_perm.reshape(-1, LANES), block_mask, col_logm[None, :], counts)])


def order_next_kernel(offsets, scalars, shifted_ref, columns_ref, values_ref, *refs):
    parts = len(offsets)
    outs, auxes, pick = refs[:parts], refs[parts : 2 * parts], refs[-1]
    depth, width = pick.shape[1:]
    values = values_ref[...].astype(BF16)
    for part, offset in enumerate(offsets):
        base = chunk_base(scalars, offset, width)
        fill_pick(pick.at[part], columns_ref, base, range(depth // LANES))
        move_values(values, pick.at[part], auxes[part])
    step = 512

    @pl.loop(0, shifted_ref.shape[0] // step)
    def _(at):
        here = pl.ds(pl.multiple_of(at * step, step), step)
        for part in range(parts):
            moved = jnp.dot(shifted_ref[here, :], pick[part], preferred_element_type=F32)
            outs[part][here, :] = moved.astype(BF16)


def order_next(scalars, shifted, columns, values, offsets, width):
    rows, cols = shifted.shape
    parts = len(offsets)
    return pl.pallas_call(
        functools.partial(order_next_kernel, offsets),
        in_specs=[SCALARS] + [WHOLE] * 3,
        out_specs=[WHOLE] * (2 * parts),
        out_shape=[jax.ShapeDtypeStruct((rows, width), BF16)] * parts
        + [jax.ShapeDtypeStruct((values.shape[0] - 16, width), F32)] * parts,
        scratch_shapes=[pltpu.VMEM((parts, cols, width), BF16)],
        compiler_params=params(24),
        cost_estimate=cost((16384 if parts == 1 else 1) * rows * width, rows * width),
        name="order_next",
    )(scalars, shifted, columns, values)


def take_kernel(scalars, perm_ref, logm_ref, *refs):
    own, from_x, from_y, from_xy, from_core, out_ref, turned_ref, logm_out, group, pick = refs
    side = own.shape[0]
    mine = [own, from_x, from_y, from_xy]
    blocks = [(2 * at, mine[at]) for at in range(4)] + [(2 * at + 1, from_core.at[at]) for at in range(4)]
    for offset, block in blocks:
        first = pl.multiple_of(jnp.bitwise_xor(scalars[COL_AT], offset) * side, side)
        group[pl.ds(first, side), :] = block[...]
    rows = out_ref.shape[0]
    depth = group.shape[0]
    groups = rows // LANES
    index = (perm_ref[...] - scalars[ROW_AT] * rows).astype(F32)
    columns = along_sublanes(jnp.concatenate([index, logm_ref[...]], axis=0))
    step = pick.shape[1]
    vocab = lax.broadcasted_iota(jnp.int32, (LANES, depth), 1).astype(F32)
    for first in range(0, rows, step):
        slot = (first // step) % pick.shape[0]
        for inner in range(0, step, LANES):
            at = (first + inner) // LANES
            pick[slot, pl.ds(inner, LANES), :] = onehot(columns[:, at : at + 1] == vocab)
            logm_out[pl.ds(first + inner, LANES), :] = jnp.broadcast_to(
                columns[:, groups + at : groups + at + 1], (LANES, LANES)
            )
        taken = jnp.dot(pick[slot], group[...], preferred_element_type=F32).astype(BF16)
        out_ref[pl.ds(first, step), :] = taken
        turned_ref[:, pl.ds(first, step)] = taken.T


def take_rows(scalars, row_perm, row_logm, blocks):
    rows = row_perm.shape[0]
    side, width = blocks[0].shape
    return pl.pallas_call(
        take_kernel,
        in_specs=[SCALARS] + [WHOLE] * 7,
        out_specs=[WHOLE] * 3,
        out_shape=[
            jax.ShapeDtypeStruct((rows, width), BF16),
            jax.ShapeDtypeStruct((width, rows), BF16),
            jax.ShapeDtypeStruct((rows, LANES), F32),
        ],
        scratch_shapes=[pltpu.VMEM((8 * side, width), BF16), pltpu.VMEM((2, 512, 8 * side), BF16)],
        compiler_params=params(24),
        cost_estimate=cost(2 * rows * rows * width, 4 * rows * width),
        name="take_rows",
    )(scalars, row_perm.reshape(-1, LANES), row_logm.reshape(-1, LANES), *blocks)


def cells_kernel(others, pieces, *refs):
    wvec_ref, turned_ref, logm_ref, chunk, count_ref, aux_ref, refs = *refs[:6], refs[6:]
    chunk_refs, delta_refs, refs = refs[:others], refs[others : 2 * others], refs[2 * others :]
    outs = max(len(pieces), 1)
    main_ref, out_refs, refs = refs[0], refs[1 : 1 + outs], refs[1 + outs :]
    chunk_turned, term_ref, refs = refs[0], refs[1], refs[2:]
    chunk_turned[...] = chunk[...].T
    rows = wvec_ref.shape[0]
    width = chunk.shape[0]
    blocks = aux_ref.shape[0] - 8
    tile = rows // blocks
    col_logm = aux_ref[pl.ds(blocks, 1), :]
    if others:
        delta_ref, stack = refs
        for at, ref in enumerate([*chunk_refs, chunk]):
            stack[pl.ds(at * width, width), :] = ref[...]
    else:
        delta_ref = main_ref
    joined = delta_ref.shape[0] // tile
    half = joined // 2

    def part(group):
        def rows_at(at, count=1):
            return pl.ds(pl.multiple_of((group * joined + at) * tile, tile), count * tile)

        def held(at, count=1):
            return delta_ref[pl.ds(at * tile, count * tile), :]

        def score_of(at):
            return jnp.dot(wvec_ref[rows_at(at), :], chunk_turned[...], preferred_element_type=F32)

        def delta_of(at, score):
            here = rows_at(at)
            count = count_ref[here, :].astype(F32) + 256.0
            log = jnp.log(jnp.maximum(count, 1.0))
            row_logm = jnp.concatenate([logm_ref[here, :]] * (width // LANES), axis=1)
            gap = score + ((row_logm + col_logm) - log)
            confid = 0.1 + 0.25 * jnp.exp2(log * np.float32(0.5 / np.log(2.0)))
            zeroed = 0.5 * jnp.tanh(0.5 * gap) + 0.5
            deriv = jnp.where(count > 0.0, confid * gap, zeroed)
            active = aux_ref[pl.ds(group * joined + at, 1), :]
            delta_ref[pl.ds(at * tile, tile), :] = (deriv * active).astype(BF16)

        def grad_of(at, count):
            here = rows_at(at, count)
            deltas = jnp.concatenate([ref[here, :] for ref in delta_refs] + [held(at, count)], axis=1)
            main_ref[here, :] = jnp.dot(deltas, stack[...], preferred_element_type=F32)

        def term_of(at):
            turned = turned_ref[:, rows_at(at, half)]
            term = jnp.dot(turned, held(at, half), preferred_element_type=F32)
            if joined < blocks or at:
                term = term_ref[...] + term
            term_ref[...] = term

        ahead = score_of(0)
        for at in range(joined):
            score = ahead
            if at + 1 < joined:
                ahead = score_of(at + 1)
            delta_of(at, score)
            if at == half:
                term_of(0)
                if others:
                    grad_of(0, half)
        term_of(half)
        if others:
            grad_of(half, half)

    if joined < blocks:
        term_ref[...] = jnp.zeros_like(term_ref)
        pl.loop(0, blocks // joined)(part)
    else:
        part(0)
    first = 0
    for out_ref in out_refs:
        out_ref[...] = term_ref[pl.ds(first, out_ref.shape[0]), :].astype(out_ref.dtype)
        first += out_ref.shape[0]


def cells(rows_in, chunk, pieces=(), others=()):
    wvec = rows_in[0]
    rows, depth = wvec.shape
    width = chunk[0].shape[0]
    args = [*rows_in, *chunk, *[each for each, _ in others], *[delta for _, delta in others]]
    if others:
        main = jax.ShapeDtypeStruct((rows, depth), F32)
        scratch = [pltpu.VMEM((rows // 2, width), BF16), pltpu.VMEM(((len(others) + 1) * width, depth), BF16)]
    else:
        main = jax.ShapeDtypeStruct((rows, width), BF16)
        scratch = []
    if pieces:
        outs = [jax.ShapeDtypeStruct((size, width), BF16) for size in pieces]
    else:
        outs = [jax.ShapeDtypeStruct((depth, width), F32)]
    return pl.pallas_call(
        functools.partial(cells_kernel, len(others), pieces),
        in_specs=[WHOLE] * len(args),
        out_specs=[WHOLE] * (1 + len(outs)),
        out_shape=[main, *outs],
        scratch_shapes=[pltpu.VMEM((depth, width), BF16), pltpu.VMEM((depth, width), F32), *scratch],
        compiler_params=params(24),
        cost_estimate=cost(rows * width, rows * depth),
        name="cells",
    )(*args)


def finish_kernel(scale, *refs):
    own_ref, near_ref, cross_refs, out_ref, sum_ref = refs[0], refs[1], refs[2:-2], refs[-2], refs[-1]
    first = 0
    for cross_ref in cross_refs:
        here = pl.ds(first, cross_ref.shape[0])
        first += cross_ref.shape[0]
        total = own_ref[here, :] + near_ref[here, :].astype(F32) + cross_ref[...].astype(F32)
        sum_ref[here, :] = total * scale
    out_ref[...] = sum_ref[...].T


def finish(scale, own, near, *crosses):
    return pl.pallas_call(
        functools.partial(finish_kernel, scale),
        in_specs=[WHOLE] * (2 + len(crosses)),
        out_specs=WHOLE,
        out_shape=jax.ShapeDtypeStruct(own.shape[::-1], F32),
        scratch_shapes=[pltpu.VMEM(own.shape, F32)],
        compiler_params=params(8),
        cost_estimate=cost(own.size, own.size // 16),
        name="finish",
    )(own, near, *crosses)


def put_kernel(offsets, exact, scalars, perm_ref, grad_ref, out_ref, pick):
    grad = grad_ref[...]
    rows, width = grad.shape
    high = grad.astype(BF16)
    moving = high
    if exact:
        moving = jnp.concatenate([high, (grad - high.astype(F32)).astype(BF16)], axis=1)
    side = out_ref.shape[1]
    index = jnp.broadcast_to((perm_ref[...] - scalars[ROW_AT] * rows).astype(F32), (8, rows))[:1]
    vocab = lax.broadcasted_iota(jnp.int32, (side, rows), 0)
    for at, offset in enumerate(offsets):
        base = jnp.bitwise_xor(scalars[COL_AT], offset) * side
        pick[pl.ds(at * side, side), :] = onehot(index == (vocab + base).astype(F32))
    moved = jnp.dot(pick[...], moving, preferred_element_type=F32)
    if exact:
        moved = moved[:, :width] + moved[:, width:]
    out_ref[...] = moved.astype(out_ref.dtype).reshape(out_ref.shape)


def put_rows(scalars, row_perm, grad, offsets, side, exact):
    width = grad.shape[1]
    return pl.pallas_call(
        functools.partial(put_kernel, offsets, exact),
        in_specs=[SCALARS, WHOLE, WHOLE],
        out_specs=WHOLE,
        out_shape=jax.ShapeDtypeStruct((len(offsets), side, width), F32 if exact else BF16),
        scratch_shapes=[pltpu.VMEM((len(offsets) * side, grad.shape[0]), BF16)],
        compiler_params=params(24),
        cost_estimate=cost((16384 if exact and len(offsets) > 1 else 1) * grad.size, grad.size // 16),
        name="put_rows",
    )(scalars, row_perm[None, :], grad)


def swap(value, axis, bit):
    pairs = [(at, at ^ bit) for at in range(lax.axis_size(axis))]
    return lax.ppermute(value, axis, pairs)


def together(values):
    return lax.optimization_barrier(values)


def line_shards(counts, block_mask, row_perm, col_perm, row_logm, col_logm, row_emb, col_emb):
    shard_rows, shard_cols = counts.shape
    side = row_emb.shape[0]
    width = col_emb.shape[0]
    scalars = jnp.stack([lax.axis_index("row"), lax.axis_index("col")]).astype(jnp.int32)

    cross = swap(col_emb, "row", 2)
    near = swap(col_emb, "row", 1)
    count_far, aux_far, shifted, columns, values = order_first(
        scalars, col_perm, block_mask, col_logm, counts, (3,), width
    )
    ordered = functools.partial(order_next, scalars)
    row_block, shifted = together((row_emb, shifted))
    from_x = swap(row_block, "col", 2)
    from_y = swap(row_block, "col", 4)
    from_xy = swap(row_block, "col", 6)
    count_cross, count_near, aux_cross, aux_near = ordered(shifted, columns, values, (2, 1), width)
    cross, near, from_x, from_y, from_xy, count_near, shifted = together(
        (cross, near, from_x, from_y, from_xy, count_near, shifted)
    )
    far = swap(cross, "row", 1)
    from_core = swap(jnp.stack([row_emb, from_x, from_y, from_xy]), "col", 1)
    count_own, aux_own = ordered(shifted, columns, values, (0,), width)
    count_own, row_perm = together((count_own, row_perm))
    blocks = [row_emb, from_x, from_y, from_xy, from_core]
    wvec, turned, logm = take_rows(scalars, row_perm, row_logm, blocks)

    rows_in = (wvec, turned, logm)
    of_far, of_cross = (far, count_far, aux_far), (cross, count_cross, aux_cross)
    of_near, of_own = (near, count_near, aux_near), (col_emb, count_own, aux_own)
    depth = col_emb.shape[1]
    early = depth * 5 // 16
    delta_far, sent_0, sent_1 = cells(rows_in, of_far, (early, depth - early))
    far_0 = swap(sent_0, "row", 1)
    far_1 = swap(sent_1, "row", 1)
    rows_in, delta_far = together((rows_in, delta_far))
    delta_cross, term_cross = cells(rows_in, of_cross)
    rows_in, delta_cross = together((rows_in, delta_cross))
    delta_near, sent_near = cells(rows_in, of_near, (depth,))
    got_near = swap(sent_near, "row", 1)
    rows_in, delta_near, far_0 = together((rows_in, delta_near, far_0))

    sum_0 = (term_cross[:early] + far_0.astype(F32)).astype(BF16)
    rows_in, sum_0 = together((rows_in, sum_0))
    cross_0 = swap(sum_0, "row", 2)
    others = ((far, delta_far), (cross, delta_cross), (near, delta_near))
    grad, term_own = cells(rows_in, of_own, (), others)
    grad, far_1, cross_0 = together((grad, far_1, cross_0))
    sum_1 = (term_cross[early:] + far_1.astype(F32)).astype(BF16)
    cross_1 = swap(sum_1, "row", 2)
    grad, sum_1 = together((grad, sum_1))

    ordered = functools.partial(put_rows, scalars, row_perm)
    away = ordered(grad, (1, 3, 5, 7), side, False)
    core = swap(away, "col", 1)
    grad, away = together((grad, away))
    both = ordered(grad, (2, 4, 6), side, True) + core[1:].astype(F32)
    sends = [both[at].astype(BF16) for at in range(3)]
    got = [swap(sends[at], "col", bit) for at, bit in ((2, 6), (1, 4), (0, 2))]
    grad, sends = together((grad, sends))
    home = ordered(grad, (0,), side, True)
    home, term_own = together((home, term_own))
    row_sum = home[0] + core[0].astype(F32)
    for each in got:
        row_sum = row_sum + each.astype(F32)
    row_scale = np.float32(1.0 / np.sqrt(shard_cols * 8))
    col_scale = np.float32(1.0 / np.sqrt(shard_rows * 4))
    return (row_sum * row_scale, finish(col_scale, term_own, got_near, cross_0, cross_1))


def solution(mesh):
    in_specs = (
        P("row", "col"),
        P("row", "col"),
        P("row"),
        P("col"),
        P("row"),
        P("col"),
        P(("row", "col"), None),
        P(("col", "row"), None),
    )
    out_specs = (P(("row", "col"), None), P(("col", "row"), None))
    line = mesh.shape["row"] == 4 and mesh.shape["col"] == 8
    body = line_shards if line else plain_shards
    return jax.shard_map(body, mesh=mesh, in_specs=in_specs, out_specs=out_specs, check_vma=False)
```
